128 devices in a mesh: gx: 8 (over y, core), gy: 16 (over x, z).
Axes of the slice: x: 4, y: 4, z: 4, core: 2. Of those that a mesh axis runs over, the one named last changes fastest.
Arguments:
- level_set: float32 [256, 512, 256], P('gx', 'gy'), may hold values from -16 to 16, as said below
- velocity: bfloat16 [3, 256, 512, 256], P(None, 'gx', 'gy'), may hold values from -2 to 2
- stress_field: float32 [6, 256, 512, 256], P(None, 'gx', 'gy'), may hold values from -6 to 6
- band_tiles: int32 [8, 16, 32], P('gx', 'gy'), may hold values from 0 to 63, as said below
Outputs:
- new_level: float32 [256, 512, 256], P('gx', 'gy')
- new_stress: float32 [6, 256, 512, 256], P(None, 'gx', 'gy')
The draws below stay inside these ranges and needn't reach their ends.
Inputs may be any that keep to these rules, and one draw needn't show every extreme that they name: `level_set`: A jet-like level set clipped to 8 cells, times a cell-wise positive factor up to 2. `band_tiles`: entries are tile numbers of the device's own block as in the reference program. A device lists 1 to 32 distinct tiles; the slots after its last tile repeat its first entry.
All inputs are finite; a program needn't handle non-finite values.
Results may differ from the reference program's by a relative error of at most 0.0003.
Values sent between devices are 32-bit elements; how exact they have to be, the bound alone decides.
No kernel may reach another device: no remote copies, remote signals or barrier semaphores. Data moves between devices by JAX's collectives and lax.ppermute only.
A program may use at most 192 MiB of HBM per device.

```python
import math
import jax
import jax.numpy as jnp
from jax import lax

CX = 32
CY = 32
NZ = 256
TILE = 16
MAXT = 32
SWEEPS = 5
EXTENSIONS = 2
NX = 256
NY = 512
N_GX = 8
N_GY = 16


def jet_distance():
    x_coord = jnp.arange(NX, dtype=jnp.float32)
    y_coord = jnp.arange(NY, dtype=jnp.float32) - NY / 2.0 + 0.5
    z_coord = jnp.arange(NZ, dtype=jnp.float32) - NZ / 2.0 + 0.5
    radius = jnp.sqrt(y_coord[:, None] ** 2 + z_coord[None, :] ** 2)
    along = x_coord / NX
    swell = 0.2 * min(NY, NZ) * (1.0 + 0.5 * along) * (1.0 + 0.1 * jnp.sin(4.0 * math.pi * along))
    distance = jnp.clip(radius[None, :, :] - swell[:, None, None], -8.0, 8.0)
    return (distance, along)


def draw_level_set(key, part):
    key = jax.random.fold_in(key, 11)
    key_inner, key_outer = jax.random.split(key)
    distance, along = jet_distance()
    inner = jnp.exp(jax.random.uniform(key_inner, (NX, NY, NZ), jnp.float32, math.log(1.4), math.log(2.0)))
    outer_noise = jnp.exp(jax.random.uniform(key_outer, (NX, NY, NZ), jnp.float32, -0.1, 0.1))
    outer = (0.3 + 0.25 * along)[:, None, None] * outer_noise
    factor = jnp.where(distance > 0.0, outer, inner)
    return (distance * factor).astype(jnp.float32)


def draw_band_tiles(key, part):
    key = jax.random.fold_in(key, 23)
    key_lists, key_counts = jax.random.split(key)
    tiles_x = CX // TILE
    tiles_y = CY // TILE
    tiles_z = NZ // TILE
    count_tiles = tiles_x * tiles_y * tiles_z
    span = min(NY, NZ)
    inner_edge = max(18 * span // 100 - TILE, 0)
    outer_edge = 34 * span // 100 + TILE
    y_twice = 2 * (jnp.arange(N_GY, dtype=jnp.int32)[:, None] * CY + jnp.arange(tiles_y, dtype=jnp.int32)[None, :] * TILE) + TILE - NY
    z_twice = 2 * jnp.arange(tiles_z, dtype=jnp.int32) * TILE + TILE - NZ
    radius_twice = y_twice[:, :, None] * y_twice[:, :, None] + z_twice[None, None, :] * z_twice[None, None, :]
    near = ((radius_twice >= 2 * inner_edge * (2 * inner_edge)) & (radius_twice <= 2 * outer_edge * (2 * outer_edge))).astype(jnp.int32)
    near = jnp.broadcast_to(near[None, :, None, :, :], (N_GX, N_GY, tiles_x, tiles_y, tiles_z)).reshape(N_GX, N_GY, count_tiles)
    device_keys = jax.random.split(key_lists, N_GX * N_GY)

    def one_order(device_key):
        return jax.random.permutation(device_key, count_tiles)
    ranks = jax.vmap(one_order)(device_keys).reshape(N_GX, N_GY, count_tiles).astype(jnp.int32)
    scores = near * count_tiles + ranks
    lists = lax.top_k(scores, MAXT)[1].astype(jnp.int32)
    spread = (jnp.arange(MAXT, dtype=jnp.int32) * (count_tiles - 1) // (MAXT - 1)).astype(jnp.int32)
    lists = lists.at[0, 0].set(spread)
    near_count = jnp.sum(near, axis=2, keepdims=True).astype(jnp.int32)
    counts = jax.random.randint(key_counts, (N_GX, N_GY, 1), 1, MAXT + 1, dtype=jnp.int32)
    counts = jnp.maximum(counts, jnp.minimum(near_count, MAXT))
    counts = counts.at[0, 0, 0].set(MAXT)
    slots = jnp.arange(MAXT, dtype=jnp.int32)
    return jnp.where(slots < counts, lists, lists[:, :, :1]).astype(jnp.int32)


def shard_levels(stream_key, dims, cuts, smallest, high):
    gain = 1.0
    for position, blocks in cuts:
        steps = jax.random.uniform(jax.random.fold_in(jax.random.fold_in(stream_key, 6), position), (blocks,), jnp.float32, smallest / len(cuts), high / len(cuts))
        gain = gain * jnp.repeat(jnp.exp(steps), dims[position] // blocks).reshape((-1,) + (1,) * (len(dims) - 1 - position))
    return gain


def noise(stream_key, dims, width, most, cuts=(), held_as=jnp.bfloat16):
    entries = width * jax.random.normal(stream_key, dims, jnp.float32)
    if cuts:
        entries = entries * shard_levels(stream_key, dims, cuts, -0.22, 0.18)
    return jnp.clip(entries, -most, most).astype(held_as)


def setup_inputs(seed: int = 0) -> dict:
    key_of = jax.random.split(jax.random.key(seed), 5)
    level_set = draw_level_set(jax.random.fold_in(key_of[4], 71), 0)
    velocity = noise(key_of[1], (3, NX, NY, NZ), 0.4, 2.0, ((1, 8), (2, 16)))
    stress_field = noise(key_of[2], (6, NX, NY, NZ), 1.0, 6.0, ((1, 8), (2, 16)), jnp.float32)
    band_tiles = draw_band_tiles(jax.random.fold_in(key_of[4], 71), 0)
    return {"level_set": level_set, "velocity": velocity, "stress_field": stress_field, "band_tiles": band_tiles}


EPSILON = 1e-06
TIME_STEP = 0.4
PSEUDO_STEP = 0.3

def weno_blend(first, second, third, fourth, fifth):
    part_one = first / 3.0 - 7.0 * second / 6.0 + 11.0 * third / 6.0
    part_two = -second / 6.0 + 5.0 * third / 6.0 + fourth / 3.0
    part_three = third / 3.0 + 5.0 * fourth / 6.0 - fifth / 6.0
    smooth_one = 13.0 / 12.0 * (first - 2.0 * second + third) ** 2 + 0.25 * (first - 4.0 * second + 3.0 * third) ** 2
    smooth_two = 13.0 / 12.0 * (second - 2.0 * third + fourth) ** 2 + 0.25 * (second - fourth) ** 2
    smooth_three = 13.0 / 12.0 * (third - 2.0 * fourth + fifth) ** 2 + 0.25 * (3.0 * third - 4.0 * fourth + fifth) ** 2
    alpha_one = 0.1 / (EPSILON + smooth_one) ** 2
    alpha_two = 0.6 / (EPSILON + smooth_two) ** 2
    alpha_three = 0.3 / (EPSILON + smooth_three) ** 2
    return (alpha_one * part_one + alpha_two * part_two + alpha_three * part_three) / (alpha_one + alpha_two + alpha_three)

def upwind_term(padded, speed, axis, count):
    steps = jnp.diff(padded, axis=axis)
    parts = [lax.slice_in_dim(steps, shift, shift + count, axis=axis) for shift in range(6)]
    minus = weno_blend(parts[0], parts[1], parts[2], parts[3], parts[4])
    plus = weno_blend(parts[5], parts[4], parts[3], parts[2], parts[1])
    return speed * jnp.where(speed > 0, minus, plus)

def godunov(center, back_x, fwd_x, back_y, fwd_y, back_z, fwd_z, sign, weight):
    grow = jnp.zeros_like(center)
    shrink = jnp.zeros_like(center)
    for back, fwd in ((back_x, fwd_x), (back_y, fwd_y), (back_z, fwd_z)):
        lower = center - back
        upper = fwd - center
        grow = grow + jnp.maximum(jnp.maximum(lower, 0.0) ** 2, jnp.minimum(upper, 0.0) ** 2)
        shrink = shrink + jnp.maximum(jnp.minimum(lower, 0.0) ** 2, jnp.maximum(upper, 0.0) ** 2)
    slope = jnp.where(sign > 0, jnp.sqrt(grow), jnp.sqrt(shrink))
    return center - PSEUDO_STEP * sign * (slope - 1.0) * weight

def blend_stress(center, neighbours, tau_center, tau_neighbours, gate):
    total = jnp.zeros_like(center)
    blended = jnp.zeros_like(tau_center)
    for other, tau_other in zip(neighbours, tau_neighbours):
        factor = jax.nn.sigmoid(2.0 * (center - other))
        total = total + factor
        blended = blended + factor * tau_other
    return tau_center + gate * (blended / total - tau_center)

def band_mask(band_tiles, shape):
    size_x, size_y, size_z = shape
    rows_x, rows_y, slots = band_tiles.shape
    tiles_x = size_x // rows_x // TILE
    tiles_y = size_y // rows_y // TILE
    tiles_z = size_z // TILE
    numbers = jnp.arange(tiles_x * tiles_y * tiles_z, dtype=jnp.int32)
    flags = lax.optimization_barrier(jnp.max((band_tiles[:, :, :, None] == numbers).astype(jnp.float32), axis=2))
    flags = flags.reshape(rows_x, rows_y, tiles_x, tiles_y, tiles_z).transpose(0, 2, 1, 3, 4)
    cells = jnp.broadcast_to(flags[:, :, None, :, :, None, :, None], (rows_x, tiles_x, TILE, rows_y, tiles_y, TILE, tiles_z, TILE))
    return cells.reshape(size_x, size_y, size_z)

def reference(level_set, velocity, stress_field, band_tiles):
    size_x, size_y, size_z = level_set.shape
    band = band_mask(band_tiles, level_set.shape)
    padded = jnp.pad(level_set, 3, mode='wrap')
    speeds = velocity.astype(jnp.float32)
    drift = upwind_term(padded[:, 3:-3, 3:-3], speeds[0], 0, size_x)
    drift = drift + upwind_term(padded[3:-3, :, 3:-3], speeds[1], 1, size_y)
    drift = drift + upwind_term(padded[3:-3, 3:-3, :], speeds[2], 2, size_z)
    advected = level_set - TIME_STEP * drift
    sign = advected / jnp.sqrt(advected * advected + 1.0)
    weight = band / (1.0 + advected * advected / 36.0)
    current = advected
    for sweep_index in range(SWEEPS):
        current = godunov(current, jnp.roll(current, 1, 0), jnp.roll(current, -1, 0), jnp.roll(current, 1, 1), jnp.roll(current, -1, 1), jnp.roll(current, 1, 2), jnp.roll(current, -1, 2), sign, weight)
    after = jnp.tanh(current)
    before = jnp.tanh(advected)
    shift = jnp.sum(after - before) / jnp.sum(1.0 - after * after)
    new_level = current - shift
    gate = weight * 0.5 * (1.0 + jnp.tanh(2.0 * new_level))
    neighbours = [jnp.roll(new_level, 1, 0), jnp.roll(new_level, -1, 0), jnp.roll(new_level, 1, 1), jnp.roll(new_level, -1, 1), jnp.roll(new_level, 1, 2), jnp.roll(new_level, -1, 2)]
    stress = stress_field
    for ext_index in range(EXTENSIONS):
        tau_neighbours = [jnp.roll(stress, 1, 1), jnp.roll(stress, -1, 1), jnp.roll(stress, 1, 2), jnp.roll(stress, -1, 2), jnp.roll(stress, 1, 3), jnp.roll(stress, -1, 3)]
        stress = blend_stress(new_level, neighbours, stress, tau_neighbours, gate)
    return (new_level, stress)
```

```python
import functools

import jax
import jax.numpy as jnp
from jax import lax
from jax.experimental import pallas as pl
from jax.experimental.pallas import tpu as pltpu
from jax.sharding import PartitionSpec as P

TILE = 16
SWEEPS = 5
EPSILON = 1e-06
TIME_STEP = 0.4
PSEUDO_STEP = 0.3

CX = 32
CY = 32
LANES = 128
DEEP = 7
ROWS = 64
OWN = 16
UNIT = 16
COMPS = 6
F32 = jnp.float32
LIMIT = 60 * 1024 * 1024
ANY = pl.BlockSpec(memory_space=pl.ANY)
VMEM = pl.BlockSpec(memory_space=pltpu.VMEM)
SMEM = pl.BlockSpec(memory_space=pltpu.SMEM)


def half(h):
    return pl.ds(h * LANES, LANES)


def recip(x):
    return pl.reciprocal(x, approx=True)


def lane_shift(pair, k):
    lane = lax.broadcasted_iota(jnp.int32, pair[0].shape, pair[0].ndim - 1)
    turned = [pltpu.roll(p, (-k) % LANES, p.ndim - 1) for p in pair]
    edge = lane >= LANES - k if k > 0 else lane < -k
    return [jnp.where(edge, turned[1 - h], turned[h]) for h in range(2)]


def weno(d, positive):
    v = [jnp.where(positive, d[k], d[5 - k]) for k in range(5)]
    d1, d2, d3, d4 = (v[k + 1] - v[k] for k in range(4))
    u1, u2, u3 = d2 - d1, d3 - d2, d4 - d3
    g1 = d2 + d2 + u1
    g2 = d2 + d3
    g3 = u3 - (d3 + d3)
    scale = 13.0 / 3.0
    a1 = recip(4.0 * EPSILON + (scale * u1 * u1 + g1 * g1))
    a2 = recip(4.0 * EPSILON + (scale * u2 * u2 + g2 * g2))
    a3 = recip(4.0 * EPSILON + (scale * u3 * u3 + g3 * g3))
    a1 = a1 * a1
    a2 = 6.0 * (a2 * a2)
    a3 = 3.0 * (a3 * a3)
    top = a1 * (u1 - u2) + 0.5 * (a3 * (u2 - u3))
    mid = v[2] + (d3 + d3 + d2) * (1.0 / 6.0)
    return mid + top * (recip(a1 + a2 + a3) * (1.0 / 3.0))


def band_table(tiles_ref):
    shape = (8, LANES)
    row = lax.broadcasted_iota(jnp.int32, shape, 0)
    lane = lax.broadcasted_iota(jnp.int32, shape, 1)
    numbers = (row // 2) * 16 + (row % 2) * 8 + lane // TILE
    flags = jnp.zeros(shape, F32)
    for slot in range(tiles_ref.shape[-1]):
        flags = jnp.where(numbers == tiles_ref[0, 0, slot], 1.0, flags)
    return flags


def advect_kernel(
    tiles, level, xlo, xhi, ylo, yhi, speed,
    adv, to_xp, to_xn, to_yp, to_yn, c_pp, c_pn, c_np, c_nn,
    pad, table, sems,
):
    copies = []
    for h in range(2):
        for n, (src, at, size) in enumerate(((level, 3, CX), (xlo, 0, 3), (xhi, CX + 3, 3))):
            copies.append(
                pltpu.make_async_copy(
                    src.at[:, :, half(h)], pad.at[pl.ds(at, size), h, pl.ds(8, CY), :], sems.at[h, n]
                )
            )
    for copy in copies:
        copy.start()
    table[...] = band_table(tiles)
    for copy in copies:
        copy.wait()
    for h in range(2):
        pad[3 : CX + 3, h, 5:8, :] = ylo[:, :, half(h)]
        pad[3 : CX + 3, h, 8 + CY : 11 + CY, :] = yhi[:, :, half(h)]

    def plane(x, carry):
        for unit in range(CY // UNIT):
            at = 8 + unit * UNIT
            rows = pl.ds(unit * UNIT, UNIT)
            center = [pad[x + 3, h, pl.ds(at, UNIT), :] for h in range(2)]
            ups = [lane_shift(center, k) for k in (1, 2, 3)]
            downs = [lane_shift(center, -k) for k in (3, 2, 1)]
            for h in range(2):
                v = [speed[d, x, rows, half(h)].astype(F32) for d in range(3)]
                lx = [pad[x + 3 + k, h, pl.ds(at, UNIT), :] for k in range(-3, 4)]
                ly = [pad[x + 3, h, pl.ds(at + k, UNIT), :] for k in range(-3, 4)]
                lz = [s[h] for s in downs] + [center[h]] + [s[h] for s in ups]
                drift = None
                for vd, line in zip(v, (lx, ly, lz)):
                    steps = [line[k + 1] - line[k] for k in range(6)]
                    term = vd * weno(steps, vd > 0)
                    drift = term if drift is None else drift + term
                adv[x, rows, half(h)] = center[h] - TIME_STEP * drift
        return carry

    lax.fori_loop(0, CX, plane, 0)
    low, high = CX - DEEP, CX
    to_xp[0:DEEP] = adv[0:DEEP]
    to_xn[0:DEEP] = adv[low:high]
    row8 = lax.broadcasted_iota(jnp.int32, (8, LANES), 0)
    for h in range(2):
        for j in range(2):
            rows = pl.ds(j * TILE, TILE)
            for i, face in ((0, to_xp), (1, to_xn)):
                r = i * 4 + j * 2 + h
                face[DEEP, rows, half(h)] = jnp.broadcast_to(table[r : r + 1, :], (TILE, LANES))
        for i in range(2):
            first = table[i * 4 + h : i * 4 + h + 1, :]
            last = table[i * 4 + 2 + h : i * 4 + 3 + h, :]
            for x in range(i * TILE, i * TILE + TILE):
                to_yp[x, :, half(h)] = jnp.where(row8 == 7, first, adv[x, 0:8, half(h)])
                to_yn[x, :, half(h)] = jnp.where(row8 == 0, last, adv[x, CY - 8 : CY, half(h)])
    c_pp[...] = to_yp[0:DEEP]
    c_pn[...] = to_yn[0:DEEP]
    c_np[...] = to_yp[low:high]
    c_nn[...] = to_yn[low:high]


def advect(tiles, level, xlo, xhi, ylo, yhi, speed):
    shape = lambda *s: jax.ShapeDtypeStruct(s, F32)
    z = 2 * LANES
    return pl.pallas_call(
        advect_kernel,
        out_shape=[shape(CX, CY, z)]
        + [shape(8, CY, z)] * 2
        + [shape(CX, 8, z)] * 2
        + [shape(DEEP, 8, z)] * 4,
        in_specs=[SMEM, ANY, ANY, ANY, VMEM, VMEM, VMEM],
        out_specs=[VMEM] * 9,
        scratch_shapes=[
            pltpu.VMEM((CX + 6, 2, 48, LANES), F32),
            pltpu.VMEM((8, LANES), F32),
            pltpu.SemaphoreType.DMA((2, 3)),
        ],
        compiler_params=pltpu.CompilerParams(vmem_limit_bytes=LIMIT),
        name="advect",
    )(tiles, level, xlo, xhi, ylo, yhi, speed)


WIDE = CX + 2 * DEEP


def sweep_kernel(
    tiles, adv, xlo, xhi, ylo, yhi, c_ll, c_lh, c_hl, c_hh,
    cur_out, weight_out, part,
    first, second, factor, masks, table, sums, sems,
):
    copies = []
    for h in range(2):
        pieces = (
            (adv, DEEP, CX, OWN, CY),
            (xlo.at[pl.ds(0, DEEP)], 0, DEEP, OWN, CY),
            (xhi.at[pl.ds(0, DEEP)], DEEP + CX, DEEP, OWN, CY),
            (ylo, DEEP, CX, OWN - 8, 8),
            (yhi, DEEP, CX, OWN + CY, 8),
            (c_ll, 0, DEEP, OWN - 8, 8),
            (c_lh, 0, DEEP, OWN + CY, 8),
            (c_hl, DEEP + CX, DEEP, OWN - 8, 8),
            (c_hh, DEEP + CX, DEEP, OWN + CY, 8),
        )
        for n, (src, x, nx, y, ny) in enumerate(pieces):
            copies.append(
                pltpu.make_async_copy(
                    src.at[:, :, half(h)],
                    first.at[pl.ds(x, nx), h, pl.ds(y, ny), :],
                    sems.at[h, n],
                )
            )
        for n, src in enumerate((xlo, xhi)):
            copies.append(
                pltpu.make_async_copy(
                    src.at[pl.ds(DEEP, 1), :, half(h)], masks.at[pl.ds(n, 1), h], sems.at[h, 9 + n]
                )
            )
    for copy in copies:
        copy.start()
    table[...] = band_table(tiles)
    sums[...] = jnp.zeros(sums.shape, F32)
    for copy in copies:
        copy.wait()

    def prepare(x, bands):
        for h in range(2):
            for group in range(-1, 5):
                rows = pl.ds(OWN + 8 * group, 8)
                value = first[x, h, rows, :]
                if group == -1:
                    band = jnp.broadcast_to(value[0:1], value.shape)
                elif group == 4:
                    band = jnp.broadcast_to(value[7:8], value.shape)
                else:
                    band = bands(group, h)
                square = value * value
                weight = band * recip(1.0 + square * (1.0 / 36.0))
                sign = value * lax.rsqrt(square + 1.0)
                factor[x, h, rows, :] = PSEUDO_STEP * sign * weight
                weight_out[x, h, rows, :] = weight

    def halo_bands(n):
        return lambda group, h: masks[n, h, pl.ds(8 * group, 8), :]

    def own_bands(i):
        def bands(group, h):
            r = i * 4 + (group // 2) * 2 + h
            return jnp.broadcast_to(table[r : r + 1, :], (8, LANES))

        return bands

    def run(start, stop, bands):
        def body(x, carry):
            prepare(x, bands)
            return carry

        lax.fori_loop(start, stop, body, 0)

    run(0, DEEP, halo_bands(0))
    run(DEEP, DEEP + TILE, own_bands(0))
    run(DEEP + TILE, DEEP + CX, own_bands(1))
    run(DEEP + CX, WIDE, halo_bands(1))

    def sweep_plane(src, x):
        for unit in range(3):
            at = OWN - 8 + unit * UNIT
            rows = pl.ds(at, UNIT)
            center = [src[x, h, rows, :] for h in range(2)]
            up, down = lane_shift(center, 1), lane_shift(center, -1)
            for h in range(2):
                c = center[h]
                step = factor[x, h, rows, :]
                positive = step > 0
                pairs = (
                    (src[x - 1, h, rows, :], src[x + 1, h, rows, :]),
                    (src[x, h, pl.ds(at - 1, UNIT), :], src[x, h, pl.ds(at + 1, UNIT), :]),
                    (down[h], up[h]),
                )
                total = None
                for l, r in pairs:
                    low = jnp.minimum(jnp.minimum(l, r), c)
                    high = jnp.maximum(jnp.maximum(l, r), c)
                    diff = c - jnp.where(positive, low, high)
                    total = diff * diff if total is None else total + diff * diff
                yield unit, h, c - step * (jnp.sqrt(total) - 1.0)

    source, target = first, second
    for sweep in range(1, SWEEPS):

        def body(x, carry, source=source, target=target):
            for unit, h, value in sweep_plane(source, x):
                target[x, h, pl.ds(OWN - 8 + unit * UNIT, UNIT), :] = value
            return carry

        lax.fori_loop(sweep, WIDE - sweep, body, 0)
        source, target = target, source

    shift = SWEEPS

    def last(x, carry):
        for unit, h, value in sweep_plane(source, x):
            cur_out[x - shift, h, pl.ds(OWN - 8 + unit * UNIT, UNIT), :] = value
        return carry

    lax.fori_loop(shift, WIDE - shift, last, 0)

    def count(x, carry):
        for h in range(2):
            for unit in range(CY // UNIT):
                rows = pl.ds(OWN + unit * UNIT, UNIT)
                after = jnp.tanh(cur_out[x + 2, h, rows, :])
                before = jnp.tanh(adv[x, pl.ds(unit * UNIT, UNIT), half(h)])
                sums[0] += after - before
                sums[1] += 1.0 - after * after
        return carry

    lax.fori_loop(0, CX, count, 0)
    lane = lax.broadcasted_iota(jnp.int32, (1, LANES), 1)
    part[...] = jnp.where(lane < 64, jnp.sum(sums[0]), jnp.sum(sums[1]))


def sweeps(tiles, adv, halos):
    shape = lambda *s: jax.ShapeDtypeStruct(s, F32)
    return pl.pallas_call(
        sweep_kernel,
        out_shape=[shape(CX + 4, 2, ROWS, LANES), shape(WIDE, 2, ROWS, LANES), shape(1, LANES)],
        in_specs=[SMEM, VMEM] + [ANY] * 8,
        out_specs=[VMEM] * 3,
        scratch_shapes=[
            pltpu.VMEM((WIDE, 2, ROWS, LANES), F32),
            pltpu.VMEM((WIDE, 2, ROWS, LANES), F32),
            pltpu.VMEM((WIDE, 2, ROWS, LANES), F32),
            pltpu.VMEM((2, 2, CY, LANES), F32),
            pltpu.VMEM((8, LANES), F32),
            pltpu.VMEM((2, UNIT, LANES), F32),
            pltpu.SemaphoreType.DMA((2, 11)),
        ],
        compiler_params=pltpu.CompilerParams(vmem_limit_bytes=LIMIT),
        name="sweeps",
    )(tiles, adv, *halos)


def extend_kernel(
    parts, cur, weight, stress, xlo, xhi, ylo, yhi,
    level_out, stress_out,
    pad, ring, mix, sems,
):
    copies = []
    for h in range(2):
        for n, (src, at, size) in enumerate(((stress, 2, CX), (xlo, 0, 2), (xhi, CX + 2, 2))):
            copies.append(
                pltpu.make_async_copy(
                    src.at[:, :, :, half(h)],
                    pad.at[:, pl.ds(at, size), h, pl.ds(OWN, CY), :],
                    sems.at[h, n],
                )
            )
    for copy in copies:
        copy.start()
    sums = jnp.sum(parts[...], axis=0, keepdims=True)
    shift = sums[:, 0:1] / sums[:, 64:65]
    for copy in copies:
        copy.wait()
    for h in range(2):
        for c in range(COMPS):
            pad[c, :, h, OWN - 2 : OWN, :] = ylo[c, :, :, half(h)]
            pad[c, :, h, OWN + CY : OWN + CY + 2, :] = yhi[c, :, :, half(h)]

    def neighbours(load, at):
        center = [load(0, h, at) for h in range(2)]
        up, down = lane_shift(center, 1), lane_shift(center, -1)
        return center, [
            [
                load(-1, h, at), load(1, h, at), load(0, h, at - 1), load(0, h, at + 1),
                down[h], up[h],
            ]
            for h in range(2)
        ]

    def first_step(i, slot):
        for unit in range(3):
            at = OWN - 8 + unit * UNIT
            rows = pl.ds(at, UNIT)
            center, around = neighbours(lambda dx, h, r: cur[i + 1 + dx, h, pl.ds(r, UNIT), :], at)
            mixes = []
            for h in range(2):
                c = center[h]
                w = [
                    recip(1.0 + jnp.exp(jnp.minimum(2.0 * (n - c), 87.0)))
                    for n in around[h]
                ]
                total = w[0] + w[1] + w[2] + w[3] + w[4] + w[5]
                gate = weight[i + DEEP - 1, h, rows, :] * 0.5 * (1.0 + jnp.tanh(2.0 * (c - shift)))
                scaled = gate * recip(total)
                w = [scaled * n for n in w] + [1.0 - gate]
                mixes.append(w)
                for n in range(7):
                    mix[slot % 2, n, h, rows, :] = w[n]
            for comp in range(COMPS):
                center, around = neighbours(
                    lambda dx, h, r: pad[comp, i + 1 + dx, h, pl.ds(r, UNIT), :], at
                )
                for h in range(2):
                    value = mixes[h][6] * center[h]
                    for n in range(6):
                        value = value + mixes[h][n] * around[h][n]
                    ring[slot, comp, h, rows, :] = value

    def second_step(x, slot):
        slots = {dx: (slot + dx) % 4 for dx in (-1, 0, 1)}
        for unit in range(CY // UNIT):
            at = OWN + unit * UNIT
            rows = pl.ds(at, UNIT)
            own = pl.ds(unit * UNIT, UNIT)
            mixes = [[mix[slot % 2, n, h, rows, :] for n in range(7)] for h in range(2)]
            for comp in range(COMPS):
                center, around = neighbours(
                    lambda dx, h, r: ring[slots[dx], comp, h, pl.ds(r, UNIT), :], at
                )
                for h in range(2):
                    value = mixes[h][6] * center[h]
                    for n in range(6):
                        value = value + mixes[h][n] * around[h][n]
                    stress_out[comp, x, own, half(h)] = value
            for h in range(2):
                level_out[x, own, half(h)] = cur[x + 2, h, rows, :] - shift

    def body(group, carry):
        for k in range(4):
            i = group * 4 + k
            first_step(i, k)

            @pl.when(i >= 2)
            def _():
                second_step(i - 2, (k + 3) % 4)

        return carry

    lax.fori_loop(0, 8, body, 0)
    for i in (32, 33):
        first_step(i, i % 4)
        second_step(i - 2, (i + 3) % 4)


def extend(parts, cur, weight, stress, halos):
    shape = lambda *s: jax.ShapeDtypeStruct(s, F32)
    z = 2 * LANES
    return pl.pallas_call(
        extend_kernel,
        out_shape=[shape(CX, CY, z), shape(COMPS, CX, CY, z)],
        in_specs=[VMEM, VMEM, VMEM, ANY, ANY, ANY, VMEM, VMEM],
        out_specs=[VMEM] * 2,
        scratch_shapes=[
            pltpu.VMEM((COMPS, CX + 4, 2, ROWS, LANES), F32),
            pltpu.VMEM((4, COMPS, 2, ROWS, LANES), F32),
            pltpu.VMEM((2, 7, 2, ROWS, LANES), F32),
            pltpu.SemaphoreType.DMA((2, 3)),
        ],
        compiler_params=pltpu.CompilerParams(vmem_limit_bytes=LIMIT),
        name="extend",
    )(parts, cur, weight, stress, *halos)


def on_device(level, velocity, stress, tiles):
    nx, ny = lax.axis_size("gx"), lax.axis_size("gy")

    def send(value, dx, dy):
        if dy == 0:
            return lax.ppermute(value, "gx", [(i, (i + dx) % nx) for i in range(nx)])
        if dx == 0:
            return lax.ppermute(value, "gy", [(i, (i + dy) % ny) for i in range(ny)])
        pairs = [
            (i * ny + j, (i + dx) % nx * ny + (j + dy) % ny) for i in range(nx) for j in range(ny)
        ]
        return lax.ppermute(value, ("gx", "gy"), pairs)

    xlo = send(level[-3:], 1, 0)
    xhi = send(level[:3], -1, 0)
    ylo = send(level[:, -3:], 0, 1)
    yhi = send(level[:, :3], 0, -1)
    adv, to_xp, to_xn, to_yp, to_yn, c_pp, c_pn, c_np, c_nn = advect(
        tiles, level, xlo, xhi, ylo, yhi, velocity
    )
    halos = (
        send(to_xn, 1, 0),
        send(to_xp, -1, 0),
        send(to_yn, 0, 1),
        send(to_yp, 0, -1),
        send(c_nn, 1, 1),
        send(c_np, 1, -1),
        send(c_pn, -1, 1),
        send(c_pp, -1, -1),
    )
    cur, weight, part = sweeps(tiles, adv, halos)
    sxlo = send(stress[:, -2:], 1, 0)
    sxhi = send(stress[:, :2], -1, 0)
    edge = lambda s: jnp.concatenate((sxlo[:, :, s], stress[:, :, s], sxhi[:, :, s]), axis=1)
    sylo = send(edge(slice(-2, None)), 0, 1)
    syhi = send(edge(slice(0, 2)), 0, -1)
    parts = lax.all_gather(part, ("gx", "gy"), axis=0, tiled=True)
    return extend(parts, cur, weight, stress, (sxlo, sxhi, sylo, syhi))


def solution(mesh):
    in_specs = (
        P("gx", "gy", None),
        P(None, "gx", "gy", None),
        P(None, "gx", "gy", None),
        P("gx", "gy", None),
    )
    out_specs = (P("gx", "gy", None), P(None, "gx", "gy", None))
    return jax.shard_map(
        on_device, mesh=mesh, in_specs=in_specs, out_specs=out_specs, check_vma=False
    )
```

```python
import functools

import jax
import jax.numpy as jnp
from jax import lax
from jax.experimental import pallas as pl
from jax.experimental.pallas import tpu as pltpu
from jax.sharding import PartitionSpec as P

TILE = 16
SWEEPS = 5
EPSILON = 1e-06
TIME_STEP = 0.4
PSEUDO_STEP = 0.3

CX = 32
CY = 32
LANES = 128
DEEP = 7
ROWS = 64
OWN = 16
UNIT = 16
COMPS = 6
F32 = jnp.float32
LIMIT = 60 * 1024 * 1024
ANY = pl.BlockSpec(memory_space=pl.ANY)
VMEM = pl.BlockSpec(memory_space=pltpu.VMEM)
SMEM = pl.BlockSpec(memory_space=pltpu.SMEM)


def half(h):
    return pl.ds(h * LANES, LANES)


def recip(x):
    return pl.reciprocal(x, approx=True)


def lane_shift(pair, k):
    lane = lax.broadcasted_iota(jnp.int32, pair[0].shape, pair[0].ndim - 1)
    turned = [pltpu.roll(p, (-k) % LANES, p.ndim - 1) for p in pair]
    edge = lane >= LANES - k if k > 0 else lane < -k
    return [jnp.where(edge, turned[1 - h], turned[h]) for h in range(2)]


def weno(d, positive):
    v = [jnp.where(positive, d[k], d[5 - k]) for k in range(5)]
    d1, d2, d3, d4 = (v[k + 1] - v[k] for k in range(4))
    u1, u2, u3 = d2 - d1, d3 - d2, d4 - d3
    g1 = d2 + d2 + u1
    g2 = d2 + d3
    g3 = u3 - (d3 + d3)
    scale = 13.0 / 3.0
    a1 = recip(4.0 * EPSILON + (scale * u1 * u1 + g1 * g1))
    a2 = recip(4.0 * EPSILON + (scale * u2 * u2 + g2 * g2))
    a3 = recip(4.0 * EPSILON + (scale * u3 * u3 + g3 * g3))
    a1 = a1 * a1
    a2 = 6.0 * (a2 * a2)
    a3 = 3.0 * (a3 * a3)
    top = a1 * (u1 - u2) + 0.5 * (a3 * (u2 - u3))
    mid = v[2] + (d3 + d3 + d2) * (1.0 / 6.0)
    return mid + top * (recip(a1 + a2 + a3) * (1.0 / 3.0))


def band_table(tiles_ref):
    shape = (8, LANES)
    row = lax.broadcasted_iota(jnp.int32, shape, 0)
    lane = lax.broadcasted_iota(jnp.int32, shape, 1)
    numbers = (row // 2) * 16 + (row % 2) * 8 + lane // TILE
    flags = jnp.zeros(shape, F32)
    for slot in range(tiles_ref.shape[-1]):
        flags = jnp.where(numbers == tiles_ref[0, 0, slot], 1.0, flags)
    return flags


def advect_kernel(
    tiles, level, xlo, xhi, ylo, yhi, speed,
    adv, to_xp, to_xn, to_yp, to_yn,
    pad, table, sems,
):
    copies = []
    for h in range(2):
        for n, (src, at, size) in enumerate(((level, 3, CX), (xlo, 0, 3), (xhi, CX + 3, 3))):
            copies.append(
                pltpu.make_async_copy(
                    src.at[:, :, half(h)], pad.at[pl.ds(at, size), h, pl.ds(8, CY), :], sems.at[h, n]
                )
            )
    for copy in copies:
        copy.start()
    table[...] = band_table(tiles)
    for copy in copies:
        copy.wait()
    for h in range(2):
        pad[3 : CX + 3, h, 5:8, :] = ylo[:, :, half(h)]
        pad[3 : CX + 3, h, 8 + CY : 11 + CY, :] = yhi[:, :, half(h)]

    def plane(x, carry):
        for unit in range(CY // UNIT):
            at = 8 + unit * UNIT
            rows = pl.ds(unit * UNIT, UNIT)
            center = [pad[x + 3, h, pl.ds(at, UNIT), :] for h in range(2)]
            ups = [lane_shift(center, k) for k in (1, 2, 3)]
            downs = [lane_shift(center, -k) for k in (3, 2, 1)]
            for h in range(2):
                v = [speed[d, x, rows, half(h)].astype(F32) for d in range(3)]
                lx = [pad[x + 3 + k, h, pl.ds(at, UNIT), :] for k in range(-3, 4)]
                ly = [pad[x + 3, h, pl.ds(at + k, UNIT), :] for k in range(-3, 4)]
                lz = [s[h] for s in downs] + [center[h]] + [s[h] for s in ups]
                drift = None
                for vd, line in zip(v, (lx, ly, lz)):
                    steps = [line[k + 1] - line[k] for k in range(6)]
                    term = vd * weno(steps, vd > 0)
                    drift = term if drift is None else drift + term
                adv[x, rows, half(h)] = center[h] - TIME_STEP * drift
        return carry

    lax.fori_loop(0, CX, plane, 0, unroll=2)
    low, high = CX - DEEP, CX
    to_xp[0:DEEP] = adv[0:DEEP]
    to_xn[0:DEEP] = adv[low:high]
    row8 = lax.broadcasted_iota(jnp.int32, (8, LANES), 0)
    for h in range(2):
        for j in range(2):
            rows = pl.ds(j * TILE, TILE)
            for i, face in ((0, to_xp), (1, to_xn)):
                r = i * 4 + j * 2 + h
                face[DEEP, rows, half(h)] = jnp.broadcast_to(table[r : r + 1, :], (TILE, LANES))
        for i in range(2):
            first = table[i * 4 + h : i * 4 + h + 1, :]
            last = table[i * 4 + 2 + h : i * 4 + 3 + h, :]
            for x in range(i * TILE, i * TILE + TILE):
                to_yp[x, :, half(h)] = jnp.where(row8 == 7, first, adv[x, 0:8, half(h)])
                to_yn[x, :, half(h)] = jnp.where(row8 == 0, last, adv[x, CY - 8 : CY, half(h)])


def advect(tiles, level, xlo, xhi, ylo, yhi, speed):
    shape = lambda *s: jax.ShapeDtypeStruct(s, F32)
    z = 2 * LANES
    return pl.pallas_call(
        advect_kernel,
        out_shape=[shape(CX, CY, z)]
        + [shape(8, CY, z)] * 2
        + [shape(CX, 8, z)] * 2,
        in_specs=[SMEM, ANY, ANY, ANY, VMEM, VMEM, VMEM],
        out_specs=[VMEM] * 5,
        scratch_shapes=[
            pltpu.VMEM((CX + 6, 2, 48, LANES), F32),
            pltpu.VMEM((8, LANES), F32),
            pltpu.SemaphoreType.DMA((2, 3)),
        ],
        compiler_params=pltpu.CompilerParams(vmem_limit_bytes=LIMIT),
        name="advect",
    )(tiles, level, xlo, xhi, ylo, yhi, speed)


WIDE = CX + 2 * DEEP


def sweep_kernel(
    tiles, adv, xlo, xhi, ylo, yhi,
    cur_out, weight_out, part,
    first, second, factor, masks, table, sums, sems,
):
    copies = []
    for h in range(2):
        pieces = (
            (adv, DEEP, CX, OWN, CY),
            (xlo.at[pl.ds(0, DEEP)], 0, DEEP, OWN, CY),
            (xhi.at[pl.ds(0, DEEP)], DEEP + CX, DEEP, OWN, CY),
            (ylo, 0, WIDE, OWN - 8, 8),
            (yhi, 0, WIDE, OWN + CY, 8),
        )
        for n, (src, x, nx, y, ny) in enumerate(pieces):
            copies.append(
                pltpu.make_async_copy(
                    src.at[:, :, half(h)],
                    first.at[pl.ds(x, nx), h, pl.ds(y, ny), :],
                    sems.at[h, n],
                )
            )
        for n, src in enumerate((xlo, xhi)):
            copies.append(
                pltpu.make_async_copy(
                    src.at[pl.ds(DEEP, 1), :, half(h)], masks.at[pl.ds(n, 1), h], sems.at[h, 5 + n]
                )
            )
    for copy in copies:
        copy.start()
    table[...] = band_table(tiles)
    sums[...] = jnp.zeros(sums.shape, F32)
    for copy in copies:
        copy.wait()

    def prepare(x, bands):
        for h in range(2):
            for group in range(-1, 5):
                rows = pl.ds(OWN + 8 * group, 8)
                value = first[x, h, rows, :]
                if group == -1:
                    band = jnp.broadcast_to(value[0:1], value.shape)
                elif group == 4:
                    band = jnp.broadcast_to(value[7:8], value.shape)
                else:
                    band = bands(group, h)
                square = value * value
                weight = band * recip(1.0 + square * (1.0 / 36.0))
                sign = value * lax.rsqrt(square + 1.0)
                factor[x, h, rows, :] = PSEUDO_STEP * sign * weight
                weight_out[x, h, rows, :] = weight

    def halo_bands(n):
        return lambda group, h: masks[n, h, pl.ds(8 * group, 8), :]

    def own_bands(i):
        def bands(group, h):
            r = i * 4 + (group // 2) * 2 + h
            return jnp.broadcast_to(table[r : r + 1, :], (8, LANES))

        return bands

    def run(start, stop, bands):
        def body(x, carry):
            prepare(x, bands)
            return carry

        lax.fori_loop(start, stop, body, 0)

    run(0, DEEP, halo_bands(0))
    run(DEEP, DEEP + TILE, own_bands(0))
    run(DEEP + TILE, DEEP + CX, own_bands(1))
    run(DEEP + CX, WIDE, halo_bands(1))

    def sweep_plane(src, x):
        for unit in range(3):
            at = OWN - 8 + unit * UNIT
            rows = pl.ds(at, UNIT)
            center = [src[x, h, rows, :] for h in range(2)]
            up, down = lane_shift(center, 1), lane_shift(center, -1)
            for h in range(2):
                c = center[h]
                step = factor[x, h, rows, :]
                positive = step > 0
                pairs = (
                    (src[x - 1, h, rows, :], src[x + 1, h, rows, :]),
                    (src[x, h, pl.ds(at - 1, UNIT), :], src[x, h, pl.ds(at + 1, UNIT), :]),
                    (down[h], up[h]),
                )
                total = None
                for l, r in pairs:
                    low = jnp.minimum(jnp.minimum(l, r), c)
                    high = jnp.maximum(jnp.maximum(l, r), c)
                    diff = c - jnp.where(positive, low, high)
                    total = diff * diff if total is None else total + diff * diff
                yield unit, h, c - step * (jnp.sqrt(total) - 1.0)

    source, target = first, second
    for sweep in range(1, SWEEPS):

        def body(x, carry, source=source, target=target):
            for unit, h, value in sweep_plane(source, x):
                target[x, h, pl.ds(OWN - 8 + unit * UNIT, UNIT), :] = value
            return carry

        lax.fori_loop(sweep, WIDE - sweep, body, 0, unroll=2)
        source, target = target, source

    shift = SWEEPS

    def last(x, carry):
        for unit, h, value in sweep_plane(source, x):
            cur_out[x - shift, h, pl.ds(OWN - 8 + unit * UNIT, UNIT), :] = value
        return carry

    lax.fori_loop(shift, WIDE - shift, last, 0, unroll=2)

    def count(x, carry):
        for h in range(2):
            for unit in range(CY // UNIT):
                rows = pl.ds(OWN + unit * UNIT, UNIT)
                after = jnp.tanh(cur_out[x + 2, h, rows, :])
                before = jnp.tanh(adv[x, pl.ds(unit * UNIT, UNIT), half(h)])
                sums[0] += after - before
                sums[1] += 1.0 - after * after
        return carry

    lax.fori_loop(0, CX, count, 0, unroll=2)
    lane = lax.broadcasted_iota(jnp.int32, (1, LANES), 1)
    part[...] = jnp.where(lane < 64, jnp.sum(sums[0]), jnp.sum(sums[1]))


def sweeps(tiles, adv, halos):
    shape = lambda *s: jax.ShapeDtypeStruct(s, F32)
    return pl.pallas_call(
        sweep_kernel,
        out_shape=[shape(CX + 4, 2, ROWS, LANES), shape(WIDE, 2, ROWS, LANES), shape(1, LANES)],
        in_specs=[SMEM, VMEM] + [ANY] * 4,
        out_specs=[VMEM] * 3,
        scratch_shapes=[
            pltpu.VMEM((WIDE, 2, ROWS, LANES), F32),
            pltpu.VMEM((WIDE, 2, ROWS, LANES), F32),
            pltpu.VMEM((WIDE, 2, ROWS, LANES), F32),
            pltpu.VMEM((2, 2, CY, LANES), F32),
            pltpu.VMEM((8, LANES), F32),
            pltpu.VMEM((2, UNIT, LANES), F32),
            pltpu.SemaphoreType.DMA((2, 7)),
        ],
        compiler_params=pltpu.CompilerParams(vmem_limit_bytes=LIMIT),
        name="sweeps",
    )(tiles, adv, *halos)


def extend_kernel(
    parts, cur, weight, stress, xlo, xhi, ylo, yhi,
    level_out, stress_out,
    pad, ring, mix, sems,
):
    copies = []
    for h in range(2):
        for n, (src, at, size) in enumerate(((stress, 2, CX), (xlo, 0, 2), (xhi, CX + 2, 2))):
            copies.append(
                pltpu.make_async_copy(
                    src.at[:, :, :, half(h)],
                    pad.at[:, pl.ds(at, size), h, pl.ds(OWN, CY), :],
                    sems.at[h, n],
                )
            )
    for copy in copies:
        copy.start()
    sums = jnp.sum(parts[...], axis=0)
    shift = sums[:, 0:1] / sums[:, 64:65]
    for copy in copies:
        copy.wait()
    for h in range(2):
        for c in range(COMPS):
            pad[c, :, h, OWN - 2 : OWN, :] = ylo[c, :, :, half(h)]
            pad[c, :, h, OWN + CY : OWN + CY + 2, :] = yhi[c, :, :, half(h)]

    def neighbours(load, at):
        center = [load(0, h, at) for h in range(2)]
        up, down = lane_shift(center, 1), lane_shift(center, -1)
        return center, [
            [
                load(-1, h, at), load(1, h, at), load(0, h, at - 1), load(0, h, at + 1),
                down[h], up[h],
            ]
            for h in range(2)
        ]

    def first_step(i, slot):
        for unit in range(3):
            at = OWN - 8 + unit * UNIT
            rows = pl.ds(at, UNIT)
            center, around = neighbours(lambda dx, h, r: cur[i + 1 + dx, h, pl.ds(r, UNIT), :], at)
            mixes = []
            for h in range(2):
                c = center[h]
                w = [
                    recip(1.0 + jnp.exp(jnp.minimum(2.0 * (n - c), 87.0)))
                    for n in around[h]
                ]
                total = w[0] + w[1] + w[2] + w[3] + w[4] + w[5]
                gate = weight[i + DEEP - 1, h, rows, :] * 0.5 * (1.0 + jnp.tanh(2.0 * (c - shift)))
                scaled = gate * recip(total)
                w = [scaled * n for n in w] + [1.0 - gate]
                mixes.append(w)
                for n in range(7):
                    mix[slot % 2, n, h, rows, :] = w[n]
            for comp in range(COMPS):
                center, around = neighbours(
                    lambda dx, h, r: pad[comp, i + 1 + dx, h, pl.ds(r, UNIT), :], at
                )
                for h in range(2):
                    value = mixes[h][6] * center[h]
                    for n in range(6):
                        value = value + mixes[h][n] * around[h][n]
                    ring[slot, comp, h, rows, :] = value

    def second_step(x, slot):
        slots = {dx: (slot + dx) % 4 for dx in (-1, 0, 1)}
        for unit in range(CY // UNIT):
            at = OWN + unit * UNIT
            rows = pl.ds(at, UNIT)
            own = pl.ds(unit * UNIT, UNIT)
            mixes = [[mix[slot % 2, n, h, rows, :] for n in range(7)] for h in range(2)]
            for comp in range(COMPS):
                center, around = neighbours(
                    lambda dx, h, r: ring[slots[dx], comp, h, pl.ds(r, UNIT), :], at
                )
                for h in range(2):
                    value = mixes[h][6] * center[h]
                    for n in range(6):
                        value = value + mixes[h][n] * around[h][n]
                    stress_out[comp, x, own, half(h)] = value
            for h in range(2):
                level_out[x, own, half(h)] = cur[x + 2, h, rows, :] - shift

    def body(group, carry):
        for k in range(4):
            i = group * 4 + k
            first_step(i, k)

            @pl.when(i >= 2)
            def _():
                second_step(i - 2, (k + 3) % 4)

        return carry

    lax.fori_loop(0, 8, body, 0)
    for i in (32, 33):
        first_step(i, i % 4)
        second_step(i - 2, (i + 3) % 4)


def extend(parts, cur, weight, stress, halos):
    shape = lambda *s: jax.ShapeDtypeStruct(s, F32)
    z = 2 * LANES
    return pl.pallas_call(
        extend_kernel,
        out_shape=[shape(CX, CY, z), shape(COMPS, CX, CY, z)],
        in_specs=[VMEM, VMEM, VMEM, ANY, ANY, ANY, VMEM, VMEM],
        out_specs=[VMEM] * 2,
        scratch_shapes=[
            pltpu.VMEM((COMPS, CX + 4, 2, ROWS, LANES), F32),
            pltpu.VMEM((4, COMPS, 2, ROWS, LANES), F32),
            pltpu.VMEM((2, 7, 2, ROWS, LANES), F32),
            pltpu.SemaphoreType.DMA((2, 3)),
        ],
        compiler_params=pltpu.CompilerParams(vmem_limit_bytes=LIMIT),
        name="extend",
    )(parts, cur, weight, stress, *halos)


def on_device(level, velocity, stress, tiles):
    nx, ny = lax.axis_size("gx"), lax.axis_size("gy")

    def send(value, dx, dy):
        if dy == 0:
            return lax.ppermute(value, "gx", [(i, (i + dx) % nx) for i in range(nx)])
        if dx == 0:
            return lax.ppermute(value, "gy", [(i, (i + dy) % ny) for i in range(ny)])
        pairs = [
            (i * ny + j, (i + dx) % nx * ny + (j + dy) % ny) for i in range(nx) for j in range(ny)
        ]
        return lax.ppermute(value, ("gx", "gy"), pairs)

    xlo = send(level[-3:], 1, 0)
    xhi = send(level[:3], -1, 0)
    ylo = send(level[:, -3:], 0, 1)
    yhi = send(level[:, :3], 0, -1)
    adv, to_xp, to_xn, to_yp, to_yn = advect(tiles, level, xlo, xhi, ylo, yhi, velocity)
    stress_after, to_xp, to_xn = lax.optimization_barrier((stress, to_xp, to_xn))
    axlo, axhi = send(to_xn, 1, 0), send(to_xp, -1, 0)
    sxlo = send(stress_after[:, -2:], 1, 0)
    sxhi = send(stress_after[:, :2], -1, 0)
    row = lax.broadcasted_iota(jnp.int32, (1, 8, 1), 1)
    low = lambda face: jnp.where(row == 7, face[DEEP:, :8], face[:DEEP, :8])
    high = lambda face: jnp.where(row == 0, face[DEEP:, -8:], face[:DEEP, -8:])
    aylo = send(jnp.concatenate((high(axlo), to_yn, high(axhi)), axis=0), 0, 1)
    ayhi = send(jnp.concatenate((low(axlo), to_yp, low(axhi)), axis=0), 0, -1)
    edge = lambda s: jnp.concatenate(
        (sxlo[:, :, s], stress_after[:, :, s], sxhi[:, :, s]), axis=1
    )
    sylo = send(edge(slice(-2, None)), 0, 1)
    syhi = send(edge(slice(0, 2)), 0, -1)
    cur, weight, part = sweeps(tiles, adv, (axlo, axhi, aylo, ayhi))
    copies = jnp.broadcast_to(part[None], (nx * ny, 1, LANES))
    parts = lax.all_to_all(copies, ("gx", "gy"), 0, 0, tiled=True)
    return extend(parts, cur, weight, stress, (sxlo, sxhi, sylo, syhi))


def solution(mesh):
    in_specs = (
        P("gx", "gy", None),
        P(None, "gx", "gy", None),
        P(None, "gx", "gy", None),
        P("gx", "gy", None),
    )
    out_specs = (P("gx", "gy", None), P(None, "gx", "gy", None))
    return jax.shard_map(
        on_device, mesh=mesh, in_specs=in_specs, out_specs=out_specs, check_vma=False
    )
```

```python
import functools

import jax
import jax.numpy as jnp
from jax import lax
from jax.experimental import pallas as pl
from jax.experimental.pallas import tpu as pltpu
from jax.sharding import PartitionSpec as P

TILE = 16
SWEEPS = 5
EPSILON = 1e-06
TIME_STEP = 0.4
PSEUDO_STEP = 0.3

CX = 32
CY = 32
LANES = 128
DEEP = 7
ROWS = 64
OWN = 16
UNIT = 16
COMPS = 6
F32 = jnp.float32
LIMIT = 60 * 1024 * 1024
ANY = pl.BlockSpec(memory_space=pl.ANY)
VMEM = pl.BlockSpec(memory_space=pltpu.VMEM)
SMEM = pl.BlockSpec(memory_space=pltpu.SMEM)


def half(h):
    return pl.ds(h * LANES, LANES)


def recip(x):
    return pl.reciprocal(x, approx=True)


def lane_shift(pair, k):
    lane = lax.broadcasted_iota(jnp.int32, pair[0].shape, pair[0].ndim - 1)
    turned = [pltpu.roll(p, (-k) % LANES, p.ndim - 1) for p in pair]
    edge = lane >= LANES - k if k > 0 else lane < -k
    return [jnp.where(edge, turned[1 - h], turned[h]) for h in range(2)]


def weno(d, positive):
    v = [jnp.where(positive, d[k], d[5 - k]) for k in range(5)]
    d1, d2, d3, d4 = (v[k + 1] - v[k] for k in range(4))
    u1, u2, u3 = d2 - d1, d3 - d2, d4 - d3
    g1 = d2 + d2 + u1
    g2 = d2 + d3
    g3 = u3 - (d3 + d3)
    scale = 13.0 / 3.0
    a1 = recip(4.0 * EPSILON + (scale * u1 * u1 + g1 * g1))
    a2 = recip(4.0 * EPSILON + (scale * u2 * u2 + g2 * g2))
    a3 = recip(4.0 * EPSILON + (scale * u3 * u3 + g3 * g3))
    a1 = a1 * a1
    a2 = 6.0 * (a2 * a2)
    a3 = 3.0 * (a3 * a3)
    top = a1 * (u1 - u2) + 0.5 * (a3 * (u2 - u3))
    mid = v[2] + (d3 + d3 + d2) * (1.0 / 6.0)
    return mid + top * (recip(a1 + a2 + a3) * (1.0 / 3.0))


def band_table(tiles_ref):
    shape = (8, LANES)
    row = lax.broadcasted_iota(jnp.int32, shape, 0)
    lane = lax.broadcasted_iota(jnp.int32, shape, 1)
    numbers = (row // 2) * 16 + (row % 2) * 8 + lane // TILE
    flags = jnp.zeros(shape, F32)
    for slot in range(tiles_ref.shape[-1]):
        flags = jnp.where(numbers == tiles_ref[0, 0, slot], 1.0, flags)
    return flags


def derivative(line, speed):
    return speed * weno([line[k + 1] - line[k] for k in range(6)], speed > 0)


def along_x(pad, x, h, at, size):
    return [pad[x + k, h, pl.ds(at, size), :] for k in range(-3, 4)]


def along_y(pad, x, h, at, size):
    return [pad[x, h, pl.ds(at + k, size), :] for k in range(-3, 4)]


def inner_kernel(level, speed, drift, pad, sems):
    copies = [
        pltpu.make_async_copy(level.at[:, :, half(h)], pad.at[:, h], sems.at[h]) for h in range(2)
    ]
    for copy in copies:
        copy.start()
    for copy in copies:
        copy.wait()

    def plane(x, with_x):
        for unit in range(CY // UNIT):
            rows = pl.ds(unit * UNIT, UNIT)
            v = [[speed[d, x, rows, half(h)].astype(F32) for h in range(2)] for d in range(3)]
            for part in range(UNIT // 8):
                at = unit * UNIT + 8 * part
                cut = slice(8 * part, 8 * part + 8)
                center = [pad[x, h, pl.ds(at, 8), :] for h in range(2)]
                ups = [lane_shift(center, k) for k in (1, 2, 3)]
                downs = [lane_shift(center, -k) for k in (3, 2, 1)]
                for h in range(2):
                    line = [s[h] for s in downs] + [center[h]] + [s[h] for s in ups]
                    total = derivative(line, v[2][h][cut])
                    if with_x:
                        total = total + derivative(along_x(pad, x, h, at, 8), v[0][h][cut])
                    if 8 <= at < CY - 8:
                        total = total + derivative(along_y(pad, x, h, at, 8), v[1][h][cut])
                    drift[x, pl.ds(at, 8), half(h)] = total

    def inner(x, carry):
        plane(x, True)
        return carry

    def outer(x, carry):
        plane(x, False)
        plane(x + CX - 3, False)
        return carry

    lax.fori_loop(0, 3, outer, 0)
    lax.fori_loop(3, CX - 3, inner, 0, unroll=2)


def inner_drift(level, speed):
    return pl.pallas_call(
        inner_kernel,
        out_shape=jax.ShapeDtypeStruct(level.shape, F32),
        in_specs=[ANY, VMEM],
        out_specs=VMEM,
        scratch_shapes=[
            pltpu.VMEM((CX, 2, CY, LANES), F32),
            pltpu.SemaphoreType.DMA((2,)),
        ],
        compiler_params=pltpu.CompilerParams(vmem_limit_bytes=LIMIT),
        cost_estimate=pl.CostEstimate(
            flops=180 * level.size, bytes_accessed=14 * level.size, transcendentals=9 * level.size
        ),
        name="inner_drift",
    )(level, speed)


def advect_kernel(
    tiles, level, xlo, xhi, ylo, yhi, speed, drift,
    adv, to_xp, to_xn, to_yp, to_yn,
    pad, table, sems,
):
    copies = []
    for h in range(2):
        for n, (src, at, size) in enumerate(((level, 3, CX), (xlo, 0, 3), (xhi, CX + 3, 3))):
            copies.append(
                pltpu.make_async_copy(
                    src.at[:, :, half(h)], pad.at[pl.ds(at, size), h, pl.ds(8, CY), :], sems.at[h, n]
                )
            )
    for copy in copies:
        copy.start()
    table[...] = band_table(tiles)
    for h in range(2):
        pad[3 : CX + 3, h, 5:8, :] = ylo[:, :, half(h)]
        pad[3 : CX + 3, h, 8 + CY : 11 + CY, :] = yhi[:, :, half(h)]
    for copy in copies:
        copy.wait()

    def plane(x, with_x):
        for unit in range(CY // UNIT):
            rows = pl.ds(unit * UNIT, UNIT)
            for h in range(2):
                vx = speed[0, x, rows, half(h)].astype(F32) if with_x else None
                vy = speed[1, x, rows, half(h)].astype(F32)
                for part in range(UNIT // 8):
                    at = unit * UNIT + 8 * part
                    cut = slice(8 * part, 8 * part + 8)
                    total = drift[x, pl.ds(at, 8), half(h)]
                    if with_x:
                        total = total + derivative(along_x(pad, x + 3, h, at + 8, 8), vx[cut])
                    if at in (0, CY - 8):
                        total = total + derivative(along_y(pad, x + 3, h, at + 8, 8), vy[cut])
                    adv[x, pl.ds(at, 8), half(h)] = (
                        pad[x + 3, h, pl.ds(at + 8, 8), :] - TIME_STEP * total
                    )

    def inner(x, carry):
        plane(x, False)
        return carry

    def outer(x, carry):
        plane(x, True)
        plane(x + CX - 3, True)
        return carry

    lax.fori_loop(0, 3, outer, 0)
    lax.fori_loop(3, CX - 3, inner, 0, unroll=2)
    low, high = CX - DEEP, CX
    to_xp[0:DEEP] = adv[0:DEEP]
    to_xn[0:DEEP] = adv[low:high]
    row8 = lax.broadcasted_iota(jnp.int32, (8, LANES), 0)
    for h in range(2):
        for j in range(2):
            rows = pl.ds(j * TILE, TILE)
            for i, face in ((0, to_xp), (1, to_xn)):
                r = i * 4 + j * 2 + h
                face[DEEP, rows, half(h)] = jnp.broadcast_to(table[r : r + 1, :], (TILE, LANES))
        for i in range(2):
            first = table[i * 4 + h : i * 4 + h + 1, :]
            last = table[i * 4 + 2 + h : i * 4 + 3 + h, :]
            for x in range(i * TILE, i * TILE + TILE):
                to_yp[x, :, half(h)] = jnp.where(row8 == 7, first, adv[x, 0:8, half(h)])
                to_yn[x, :, half(h)] = jnp.where(row8 == 0, last, adv[x, CY - 8 : CY, half(h)])


def advect(tiles, level, xlo, xhi, ylo, yhi, speed, drift):
    shape = lambda *s: jax.ShapeDtypeStruct(s, F32)
    z = 2 * LANES
    return pl.pallas_call(
        advect_kernel,
        out_shape=[shape(CX, CY, z)]
        + [shape(8, CY, z)] * 2
        + [shape(CX, 8, z)] * 2,
        in_specs=[SMEM, ANY, ANY, ANY, VMEM, VMEM, VMEM, VMEM],
        out_specs=[VMEM] * 5,
        scratch_shapes=[
            pltpu.VMEM((CX + 6, 2, 48, LANES), F32),
            pltpu.VMEM((8, LANES), F32),
            pltpu.SemaphoreType.DMA((2, 3)),
        ],
        compiler_params=pltpu.CompilerParams(vmem_limit_bytes=LIMIT),
        name="advect",
    )(tiles, level, xlo, xhi, ylo, yhi, speed, drift)


WIDE = CX + 2 * DEEP


def sweep_kernel(
    tiles, adv, xlo, xhi, ylo, yhi,
    cur_out, weight_out, part,
    first, second, factor, masks, table, sums, sems,
):
    copies = []
    for h in range(2):
        pieces = (
            (adv, DEEP, CX, OWN, CY),
            (xlo.at[pl.ds(0, DEEP)], 0, DEEP, OWN, CY),
            (xhi.at[pl.ds(0, DEEP)], DEEP + CX, DEEP, OWN, CY),
            (ylo, 0, WIDE, OWN - 8, 8),
            (yhi, 0, WIDE, OWN + CY, 8),
        )
        for n, (src, x, nx, y, ny) in enumerate(pieces):
            copies.append(
                pltpu.make_async_copy(
                    src.at[:, :, half(h)],
                    first.at[pl.ds(x, nx), h, pl.ds(y, ny), :],
                    sems.at[h, n],
                )
            )
        for n, src in enumerate((xlo, xhi)):
            copies.append(
                pltpu.make_async_copy(
                    src.at[pl.ds(DEEP, 1), :, half(h)], masks.at[pl.ds(n, 1), h], sems.at[h, 5 + n]
                )
            )
    for copy in copies:
        copy.start()
    table[...] = band_table(tiles)
    sums[...] = jnp.zeros(sums.shape, F32)
    for copy in copies:
        copy.wait()

    def prepare(x, bands, keep):
        for h in range(2):
            saved = {}
            for group in range(-1, 5):
                rows = pl.ds(OWN + 8 * group, 8)
                value = first[x, h, rows, :]
                if group == -1:
                    band = jnp.broadcast_to(value[0:1], value.shape)
                elif group == 4:
                    band = jnp.broadcast_to(value[7:8], value.shape)
                else:
                    band = bands(group, h)
                square = value * value
                weight = band * recip(1.0 + square * (1.0 / 36.0))
                sign = value * lax.rsqrt(square + 1.0)
                factor[x, h, rows, :] = PSEUDO_STEP * sign * weight
                saved[group] = weight
            if keep:
                saved[4] = jnp.where(row8 < 4, saved[4], saved[-1])
                for group in range(5):
                    weight_out[x - DEEP + 1, h, pl.ds(OWN + 8 * group, 8), :] = saved[group]

    def halo_bands(n):
        return lambda group, h: masks[n, h, pl.ds(8 * group, 8), :]

    def own_bands(i):
        def bands(group, h):
            r = i * 4 + (group // 2) * 2 + h
            return jnp.broadcast_to(table[r : r + 1, :], (8, LANES))

        return bands

    row8 = lax.broadcasted_iota(jnp.int32, (8, LANES), 0)

    def run(start, stop, bands, keep):
        def body(x, carry):
            prepare(x, bands, keep)
            return carry

        lax.fori_loop(start, stop, body, 0, unroll=2)

    run(1, DEEP - 1, halo_bands(0), False)
    prepare(DEEP - 1, halo_bands(0), True)
    run(DEEP, DEEP + TILE, own_bands(0), True)
    run(DEEP + TILE, DEEP + CX, own_bands(1), True)
    prepare(DEEP + CX, halo_bands(1), True)
    run(DEEP + CX + 1, WIDE - 1, halo_bands(1), False)

    def sweep_plane(src, x):
        for unit in range(3):
            at = OWN - 8 + unit * UNIT
            rows = pl.ds(at, UNIT)
            center = [src[x, h, rows, :] for h in range(2)]
            up, down = lane_shift(center, 1), lane_shift(center, -1)
            for h in range(2):
                c = center[h]
                step = factor[x, h, rows, :]
                positive = step > 0
                pairs = (
                    (src[x - 1, h, rows, :], src[x + 1, h, rows, :]),
                    (src[x, h, pl.ds(at - 1, UNIT), :], src[x, h, pl.ds(at + 1, UNIT), :]),
                    (down[h], up[h]),
                )
                total = None
                for l, r in pairs:
                    low = jnp.minimum(jnp.minimum(l, r), c)
                    high = jnp.maximum(jnp.maximum(l, r), c)
                    diff = c - jnp.where(positive, low, high)
                    total = diff * diff if total is None else total + diff * diff
                yield unit, h, c - step * (jnp.sqrt(total) - 1.0)

    source, target = first, second
    for sweep in range(1, SWEEPS):

        def body(x, carry, source=source, target=target):
            for unit, h, value in sweep_plane(source, x):
                target[x, h, pl.ds(OWN - 8 + unit * UNIT, UNIT), :] = value
            return carry

        lax.fori_loop(sweep, WIDE - sweep, body, 0, unroll=2)
        source, target = target, source

    shift = SWEEPS

    def last(x, carry):
        values = [{}, {}]
        for unit, h, value in sweep_plane(source, x):
            values[h][2 * unit], values[h][2 * unit + 1] = value[:8], value[8:]
        for h in range(2):
            v = values[h]
            v[5] = jnp.where(row8 < 4, v[5], v[0])
            v[0], v[6] = v[5], v[1]
            for n in range(7):
                cur_out[x - shift, h, pl.ds(OWN - 8 + 8 * n, 8), :] = v[n]
        return carry

    lax.fori_loop(shift, WIDE - shift, last, 0, unroll=2)

    def count(x, carry):
        for h in range(2):
            for unit in range(CY // UNIT):
                rows = pl.ds(OWN + unit * UNIT, UNIT)
                after = jnp.tanh(cur_out[x + 2, h, rows, :])
                before = jnp.tanh(adv[x, pl.ds(unit * UNIT, UNIT), half(h)])
                sums[0] += after - before
                sums[1] += 1.0 - after * after
        return carry

    lax.fori_loop(0, CX, count, 0, unroll=2)
    lane = lax.broadcasted_iota(jnp.int32, (1, LANES), 1)
    part[...] = jnp.where(lane < 64, jnp.sum(sums[0]), jnp.sum(sums[1]))


def sweeps(tiles, adv, halos):
    shape = lambda *s: jax.ShapeDtypeStruct(s, F32)
    return pl.pallas_call(
        sweep_kernel,
        out_shape=[shape(CX + 4, 2, ROWS, LANES), shape(CX + 2, 2, ROWS, LANES), shape(1, LANES)],
        in_specs=[SMEM, VMEM] + [ANY] * 4,
        out_specs=[VMEM] * 3,
        scratch_shapes=[
            pltpu.VMEM((WIDE, 2, ROWS, LANES), F32),
            pltpu.VMEM((WIDE, 2, ROWS, LANES), F32),
            pltpu.VMEM((WIDE, 2, ROWS, LANES), F32),
            pltpu.VMEM((2, 2, CY, LANES), F32),
            pltpu.VMEM((8, LANES), F32),
            pltpu.VMEM((2, UNIT, LANES), F32),
            pltpu.SemaphoreType.DMA((2, 7)),
        ],
        compiler_params=pltpu.CompilerParams(vmem_limit_bytes=LIMIT),
        name="sweeps",
    )(tiles, adv, *halos)


CHUNKS = ((0, 10), (10, 18), (18, 26), (26, 32))


def extend_kernel(
    parts, cur, weight, stress, xlo, xhi, ylo, yhi,
    level_out, stress_out,
    pad, ring, mix, stage, sems, out_sems,
):
    def chunk(n):
        start, stop = CHUNKS[n]
        pieces = [(stress.at[:, pl.ds(start, stop - start)], start + 2, stop - start)]
        if n == 0:
            pieces.append((xlo, 0, 2))
        if n == len(CHUNKS) - 1:
            pieces.append((xhi, CX + 2, 2))
        copies = []
        for h in range(2):
            for m, (src, at, size) in enumerate(pieces):
                for k, (y, ny, row) in enumerate(((0, CY, OWN), (0, 8, OWN + CY + 8))):
                    copies.append(
                        pltpu.make_async_copy(
                            src.at[:, :, pl.ds(y, ny), half(h)],
                            pad.at[:, pl.ds(at, size), h, pl.ds(row, ny), :],
                            sems.at[n, h, m, k],
                        )
                    )
        return copies

    chunks = [chunk(n) for n in range(len(CHUNKS))]
    for copies in chunks:
        for copy in copies:
            copy.start()
    sums = jnp.sum(parts[...], axis=0)
    shift = sums[:, 0:1] / sums[:, 64:65]
    for h in range(2):
        for c in range(COMPS):
            low, high = ylo[c, :, :, half(h)], yhi[c, :, :, half(h)]
            pad[c, :, h, OWN - 2 : OWN, :] = low
            pad[c, :, h, OWN + CY + 6 : OWN + CY + 8, :] = low
            pad[c, :, h, OWN + CY : OWN + CY + 2, :] = high

    def neighbours(load, at):
        center = [load(0, h, at) for h in range(2)]
        up, down = lane_shift(center, 1), lane_shift(center, -1)
        return center, [
            [
                load(-1, h, at), load(1, h, at), load(0, h, at - 1), load(0, h, at + 1),
                down[h], up[h],
            ]
            for h in range(2)
        ]

    def blend(mixes, center, around):
        value = mixes[6] * center
        for n in range(6):
            value = value + mixes[n] * around[n]
        return value

    def first_step(i, slot, groups=5):
        for group in range(groups):
            at = OWN + 8 * group
            rows = pl.ds(at, 8)
            center, around = neighbours(lambda dx, h, r: cur[i + 1 + dx, h, pl.ds(r, 8), :], at)
            mixes = []
            for h in range(2):
                c = center[h]
                w = [
                    recip(1.0 + jnp.exp(jnp.minimum(2.0 * (n - c), 87.0)))
                    for n in around[h]
                ]
                total = w[0] + w[1] + w[2] + w[3] + w[4] + w[5]
                gate = weight[i, h, rows, :] * 0.5 * (1.0 + jnp.tanh(2.0 * (c - shift)))
                scaled = gate * recip(total)
                w = [scaled * n for n in w] + [1.0 - gate]
                mixes.append(w)
                if group < 4:
                    for n in range(7):
                        mix[slot % 2, n, h, rows, :] = w[n]
            for comp in range(COMPS):
                center, around = neighbours(
                    lambda dx, h, r: pad[comp, i + 1 + dx, h, pl.ds(r, 8), :], at
                )
                for h in range(2):
                    value = blend(mixes[h], center[h], around[h])
                    ring[slot, comp, h, rows, :] = value
                    if group == 4:
                        ring[slot, comp, h, pl.ds(OWN - 8, 8), :] = value

    def second_step(x, slot):
        slots = {dx: (slot + dx) % 4 for dx in (-1, 0, 1)}
        for group in range(CY // 8):
            at = OWN + 8 * group
            rows = pl.ds(at, 8)
            own = pl.ds(8 * group, 8)
            mixes = [[mix[slot % 2, n, h, rows, :] for n in range(7)] for h in range(2)]
            for comp in range(COMPS):
                center, around = neighbours(
                    lambda dx, h, r: ring[slots[dx], comp, h, pl.ds(r, 8), :], at
                )
                for h in range(2):
                    stage[comp, x, own, half(h)] = blend(mixes[h], center[h], around[h])
            for h in range(2):
                level_out[x, own, half(h)] = cur[x + 2, h, rows, :] - shift

    outs = []
    for n in range(len(CHUNKS)):
        for copy in chunks[n]:
            copy.wait()
        if n == 0:
            first_step(0, 0, groups=4)
            first_step(1, 1)

        def body(group, carry):
            for k in range(4):
                i = group * 4 + k + 2
                first_step(i, (k + 2) % 4)
                second_step(i - 2, (k + 1) % 4)
            return carry

        lax.fori_loop(2 * n, 2 * n + 2, body, 0)
        planes = pl.ds(8 * n, 8)
        outs.append(
            pltpu.make_async_copy(stage.at[:, planes], stress_out.at[:, planes], out_sems.at[n])
        )
        outs[-1].start()
    for copy in outs:
        copy.wait()


def extend(parts, cur, weight, stress, halos):
    shape = lambda *s: jax.ShapeDtypeStruct(s, F32)
    z = 2 * LANES
    return pl.pallas_call(
        extend_kernel,
        out_shape=[shape(CX, CY, z), shape(COMPS, CX, CY, z)],
        in_specs=[VMEM, VMEM, VMEM, ANY, ANY, ANY, VMEM, VMEM],
        out_specs=[VMEM, ANY],
        scratch_shapes=[
            pltpu.VMEM((COMPS, CX + 4, 2, ROWS, LANES), F32),
            pltpu.VMEM((4, COMPS, 2, ROWS, LANES), F32),
            pltpu.VMEM((2, 7, 2, ROWS, LANES), F32),
            pltpu.VMEM((COMPS, CX, CY, z), F32),
            pltpu.SemaphoreType.DMA((4, 2, 2, 2)),
            pltpu.SemaphoreType.DMA((4,)),
        ],
        compiler_params=pltpu.CompilerParams(vmem_limit_bytes=LIMIT),
        name="extend",
    )(parts, cur, weight, stress, *halos)


def on_device(level, velocity, stress, tiles):
    nx, ny = lax.axis_size("gx"), lax.axis_size("gy")

    def send(value, dx, dy):
        if dy == 0:
            return lax.ppermute(value, "gx", [(i, (i + dx) % nx) for i in range(nx)])
        if dx == 0:
            return lax.ppermute(value, "gy", [(i, (i + dy) % ny) for i in range(ny)])
        pairs = [
            (i * ny + j, (i + dx) % nx * ny + (j + dy) % ny) for i in range(nx) for j in range(ny)
        ]
        return lax.ppermute(value, ("gx", "gy"), pairs)

    xlo = send(level[-3:], 1, 0)
    xhi = send(level[:3], -1, 0)
    ylo = send(level[:, -3:], 0, 1)
    yhi = send(level[:, :3], 0, -1)
    drift = inner_drift(level, velocity)
    adv, to_xp, to_xn, to_yp, to_yn = advect(tiles, level, xlo, xhi, ylo, yhi, velocity, drift)
    axlo, axhi = send(to_xn, 1, 0), send(to_xp, -1, 0)
    row = lax.broadcasted_iota(jnp.int32, (1, 8, 1), 1)
    low = lambda face: jnp.where(row == 7, face[DEEP:, :8], face[:DEEP, :8])
    high = lambda face: jnp.where(row == 0, face[DEEP:, -8:], face[:DEEP, -8:])
    aylo = send(jnp.concatenate((high(axlo), to_yn, high(axhi)), axis=0), 0, 1)
    ayhi = send(jnp.concatenate((low(axlo), to_yp, low(axhi)), axis=0), 0, -1)
    faces = (stress[:, -2:], stress[:, :2])
    faces, _, _ = lax.optimization_barrier((faces, axlo, axhi))
    sxlo, sxhi = send(faces[0], 1, 0), send(faces[1], -1, 0)
    edge = lambda s: jnp.concatenate((sxlo[:, :, s], stress[:, :, s], sxhi[:, :, s]), axis=1)
    edges = (edge(slice(-2, None)), edge(slice(0, 2)))
    edges, aylo, ayhi = lax.optimization_barrier((edges, aylo, ayhi))
    sylo, syhi = send(edges[0], 0, 1), send(edges[1], 0, -1)
    cur, weight, part = sweeps(tiles, adv, (axlo, axhi, aylo, ayhi))
    for axis, count in (("gx", nx), ("gy", ny)):
        copies = jnp.broadcast_to(part[None], (count, 1, LANES))
        parts = lax.all_to_all(copies, axis, 0, 0, tiled=True)
        part = jnp.sum(parts, axis=0)
    return extend(parts, cur, weight, stress, (sxlo, sxhi, sylo, syhi))


def solution(mesh):
    in_specs = (
        P("gx", "gy", None),
        P(None, "gx", "gy", None),
        P(None, "gx", "gy", None),
        P("gx", "gy", None),
    )
    out_specs = (P("gx", "gy", None), P(None, "gx", "gy", None))
    return jax.shard_map(
        on_device, mesh=mesh, in_specs=in_specs, out_specs=out_specs, check_vma=False
    )
```

```python
import functools

import jax
import jax.numpy as jnp
from jax import lax
from jax.experimental import pallas as pl
from jax.experimental.pallas import tpu as pltpu
from jax.sharding import PartitionSpec as P

TILE = 16
SWEEPS = 5
EPSILON = 1e-06
TIME_STEP = 0.4
PSEUDO_STEP = 0.3

CX = 32
CY = 32
LANES = 128
DEEP = 7
ROWS = 64
OWN = 16
UNIT = 16
COMPS = 6
F32 = jnp.float32
LIMIT = 60 * 1024 * 1024
ANY = pl.BlockSpec(memory_space=pl.ANY)
VMEM = pl.BlockSpec(memory_space=pltpu.VMEM)
SMEM = pl.BlockSpec(memory_space=pltpu.SMEM)


def half(h):
    return pl.ds(h * LANES, LANES)


def recip(x):
    return pl.reciprocal(x, approx=True)


def lane_shift(pair, k):
    lane = lax.broadcasted_iota(jnp.int32, pair[0].shape, pair[0].ndim - 1)
    turned = [pltpu.roll(p, (-k) % LANES, p.ndim - 1) for p in pair]
    edge = lane >= LANES - k if k > 0 else lane < -k
    return [jnp.where(edge, turned[1 - h], turned[h]) for h in range(2)]


def weno(d, positive):
    v = [jnp.where(positive, d[k], d[5 - k]) for k in range(5)]
    d1, d2, d3, d4 = (v[k + 1] - v[k] for k in range(4))
    u1, u2, u3 = d2 - d1, d3 - d2, d4 - d3
    g1 = d2 + d2 + u1
    g2 = d2 + d3
    g3 = u3 - (d3 + d3)
    scale = 13.0 / 3.0
    a1 = recip(4.0 * EPSILON + (scale * u1 * u1 + g1 * g1))
    a2 = recip(4.0 * EPSILON + (scale * u2 * u2 + g2 * g2))
    a3 = recip(4.0 * EPSILON + (scale * u3 * u3 + g3 * g3))
    a1 = a1 * a1
    a2 = 6.0 * (a2 * a2)
    a3 = 3.0 * (a3 * a3)
    top = a1 * (u1 - u2) + 0.5 * (a3 * (u2 - u3))
    mid = v[2] + (d3 + d3 + d2) * (1.0 / 6.0)
    return mid + top * (recip(a1 + a2 + a3) * (1.0 / 3.0))


def band_table(tiles_ref):
    shape = (8, LANES)
    row = lax.broadcasted_iota(jnp.int32, shape, 0)
    lane = lax.broadcasted_iota(jnp.int32, shape, 1)
    numbers = (row // 2) * 16 + (row % 2) * 8 + lane // TILE
    flags = jnp.zeros(shape, F32)
    for slot in range(tiles_ref.shape[-1]):
        flags = jnp.where(numbers == tiles_ref[0, 0, slot], 1.0, flags)
    return flags


def derivative(line, speed):
    return speed * weno([line[k + 1] - line[k] for k in range(6)], speed > 0)


def along_x(pad, x, h, at, size):
    return [pad[x + k, h, pl.ds(at, size), :] for k in range(-3, 4)]


def along_y(pad, x, h, at, size):
    return [pad[x, h, pl.ds(at + k, size), :] for k in range(-3, 4)]


def inner_kernel(level, speed, drift, pad, sems):
    copies = [
        pltpu.make_async_copy(level.at[:, :, half(h)], pad.at[:, h], sems.at[h]) for h in range(2)
    ]
    for copy in copies:
        copy.start()
    for copy in copies:
        copy.wait()

    def plane(x, with_x):
        for unit in range(CY // UNIT):
            rows = pl.ds(unit * UNIT, UNIT)
            v = [[speed[d, x, rows, half(h)].astype(F32) for h in range(2)] for d in range(3)]
            for part in range(UNIT // 8):
                at = unit * UNIT + 8 * part
                cut = slice(8 * part, 8 * part + 8)
                center = [pad[x, h, pl.ds(at, 8), :] for h in range(2)]
                ups = [lane_shift(center, k) for k in (1, 2, 3)]
                downs = [lane_shift(center, -k) for k in (3, 2, 1)]
                for h in range(2):
                    line = [s[h] for s in downs] + [center[h]] + [s[h] for s in ups]
                    total = derivative(line, v[2][h][cut])
                    if with_x:
                        total = total + derivative(along_x(pad, x, h, at, 8), v[0][h][cut])
                    if 8 <= at < CY - 8:
                        total = total + derivative(along_y(pad, x, h, at, 8), v[1][h][cut])
                    drift[x, pl.ds(at, 8), half(h)] = total

    def inner(x, carry):
        plane(x, True)
        return carry

    def outer(x, carry):
        plane(x, False)
        plane(x + CX - 3, False)
        return carry

    lax.fori_loop(0, 3, outer, 0)
    lax.fori_loop(3, CX - 3, inner, 0, unroll=2)


def inner_drift(level, speed):
    return pl.pallas_call(
        inner_kernel,
        out_shape=jax.ShapeDtypeStruct(level.shape, F32),
        in_specs=[ANY, VMEM],
        out_specs=VMEM,
        scratch_shapes=[
            pltpu.VMEM((CX, 2, CY, LANES), F32),
            pltpu.SemaphoreType.DMA((2,)),
        ],
        compiler_params=pltpu.CompilerParams(vmem_limit_bytes=LIMIT),
        cost_estimate=pl.CostEstimate(
            flops=180 * level.size, bytes_accessed=14 * level.size, transcendentals=9 * level.size
        ),
        name="inner_drift",
    )(level, speed)


def advect_kernel(
    tiles, level, xlo, xhi, ylo, yhi, speed, drift,
    adv, to_xp, to_xn, to_yp, to_yn,
    pad, table, sems,
):
    copies = []
    for h in range(2):
        for n, (src, at, size) in enumerate(((level, 3, CX), (xlo, 0, 3), (xhi, CX + 3, 3))):
            copies.append(
                pltpu.make_async_copy(
                    src.at[:, :, half(h)], pad.at[pl.ds(at, size), h, pl.ds(8, CY), :], sems.at[h, n]
                )
            )
    for copy in copies:
        copy.start()
    table[...] = band_table(tiles)
    for h in range(2):
        pad[3 : CX + 3, h, 5:8, :] = ylo[:, :, half(h)]
        pad[3 : CX + 3, h, 8 + CY : 11 + CY, :] = yhi[:, :, half(h)]
    for copy in copies:
        copy.wait()

    def plane(x, with_x):
        for unit in range(CY // UNIT):
            rows = pl.ds(unit * UNIT, UNIT)
            for h in range(2):
                vx = speed[0, x, rows, half(h)].astype(F32) if with_x else None
                vy = speed[1, x, rows, half(h)].astype(F32)
                for part in range(UNIT // 8):
                    at = unit * UNIT + 8 * part
                    cut = slice(8 * part, 8 * part + 8)
                    total = drift[x, pl.ds(at, 8), half(h)]
                    if with_x:
                        total = total + derivative(along_x(pad, x + 3, h, at + 8, 8), vx[cut])
                    if at in (0, CY - 8):
                        total = total + derivative(along_y(pad, x + 3, h, at + 8, 8), vy[cut])
                    adv[x, pl.ds(at, 8), half(h)] = (
                        pad[x + 3, h, pl.ds(at + 8, 8), :] - TIME_STEP * total
                    )

    def inner(x, carry):
        plane(x, False)
        return carry

    def outer(x, carry):
        plane(x, True)
        plane(x + CX - 3, True)
        return carry

    lax.fori_loop(0, 3, outer, 0)
    lax.fori_loop(3, CX - 3, inner, 0, unroll=2)
    low, high = CX - DEEP, CX
    to_xp[0:DEEP] = adv[0:DEEP]
    to_xn[0:DEEP] = adv[low:high]
    row8 = lax.broadcasted_iota(jnp.int32, (8, LANES), 0)
    for h in range(2):
        for j in range(2):
            rows = pl.ds(j * TILE, TILE)
            for i, face in ((0, to_xp), (1, to_xn)):
                r = i * 4 + j * 2 + h
                face[DEEP, rows, half(h)] = jnp.broadcast_to(table[r : r + 1, :], (TILE, LANES))
        for i in range(2):
            first = table[i * 4 + h : i * 4 + h + 1, :]
            last = table[i * 4 + 2 + h : i * 4 + 3 + h, :]
            for x in range(i * TILE, i * TILE + TILE):
                to_yp[x, :, half(h)] = jnp.where(row8 == 7, first, adv[x, 0:8, half(h)])
                to_yn[x, :, half(h)] = jnp.where(row8 == 0, last, adv[x, CY - 8 : CY, half(h)])


def advect(tiles, level, xlo, xhi, ylo, yhi, speed, drift):
    shape = lambda *s: jax.ShapeDtypeStruct(s, F32)
    z = 2 * LANES
    return pl.pallas_call(
        advect_kernel,
        out_shape=[shape(CX, CY, z)]
        + [shape(8, CY, z)] * 2
        + [shape(CX, 8, z)] * 2,
        in_specs=[SMEM, ANY, ANY, ANY, VMEM, VMEM, VMEM, VMEM],
        out_specs=[VMEM] * 5,
        scratch_shapes=[
            pltpu.VMEM((CX + 6, 2, 48, LANES), F32),
            pltpu.VMEM((8, LANES), F32),
            pltpu.SemaphoreType.DMA((2, 3)),
        ],
        compiler_params=pltpu.CompilerParams(vmem_limit_bytes=LIMIT),
        name="advect",
    )(tiles, level, xlo, xhi, ylo, yhi, speed, drift)


WIDE = CX + 2 * DEEP


def sweep_kernel(
    tiles, adv, xlo, xhi, ylo, yhi, clo, chi,
    cur_out, weight_out, part,
    first, second, factor, masks, table, sums, sems,
):
    copies = []
    for h in range(2):
        pieces = (
            (adv, DEEP, CX, OWN, CY),
            (xlo.at[pl.ds(0, DEEP)], 0, DEEP, OWN, CY),
            (xhi.at[pl.ds(0, DEEP)], DEEP + CX, DEEP, OWN, CY),
            (ylo, DEEP, CX, OWN - 8, 8),
            (yhi, DEEP, CX, OWN + CY, 8),
            (clo.at[pl.ds(0, DEEP)], 0, DEEP, OWN - 8, 8),
            (clo.at[pl.ds(DEEP, DEEP)], DEEP + CX, DEEP, OWN - 8, 8),
            (chi.at[pl.ds(0, DEEP)], 0, DEEP, OWN + CY, 8),
            (chi.at[pl.ds(DEEP, DEEP)], DEEP + CX, DEEP, OWN + CY, 8),
        )
        for n, (src, x, nx, y, ny) in enumerate(pieces):
            copies.append(
                pltpu.make_async_copy(
                    src.at[:, :, half(h)],
                    first.at[pl.ds(x, nx), h, pl.ds(y, ny), :],
                    sems.at[h, n],
                )
            )
        for n, src in enumerate((xlo, xhi)):
            copies.append(
                pltpu.make_async_copy(
                    src.at[pl.ds(DEEP, 1), :, half(h)], masks.at[pl.ds(n, 1), h], sems.at[h, 9 + n]
                )
            )
    for copy in copies:
        copy.start()
    table[...] = band_table(tiles)
    sums[...] = jnp.zeros(sums.shape, F32)
    for copy in copies:
        copy.wait()

    def prepare(x, bands, keep):
        for h in range(2):
            for group in range(-1, 5):
                rows = pl.ds(OWN + 8 * group, 8)
                value = first[x, h, rows, :]
                if group == -1:
                    band = jnp.broadcast_to(value[0:1], value.shape)
                elif group == 4:
                    band = jnp.broadcast_to(value[7:8], value.shape)
                else:
                    band = bands(group, h)
                square = value * value
                weight = band * recip(1.0 + square * (1.0 / 36.0))
                sign = value * lax.rsqrt(square + 1.0)
                factor[x, h, rows, :] = PSEUDO_STEP * sign * weight
                if keep:
                    weight_out[x - DEEP + 1, h, rows, :] = weight

    def halo_bands(n):
        return lambda group, h: masks[n, h, pl.ds(8 * group, 8), :]

    def own_bands(i):
        def bands(group, h):
            r = i * 4 + (group // 2) * 2 + h
            return jnp.broadcast_to(table[r : r + 1, :], (8, LANES))

        return bands

    def run(start, stop, bands, keep):
        def body(x, carry):
            prepare(x, bands, keep)
            return carry

        lax.fori_loop(start, stop, body, 0, unroll=2)

    run(1, DEEP - 1, halo_bands(0), False)
    prepare(DEEP - 1, halo_bands(0), True)
    run(DEEP, DEEP + TILE, own_bands(0), True)
    run(DEEP + TILE, DEEP + CX, own_bands(1), True)
    prepare(DEEP + CX, halo_bands(1), True)
    run(DEEP + CX + 1, WIDE - 1, halo_bands(1), False)

    def sweep_plane(src, x, dst, y, groups):
        start = OWN + CY // 2 - 4 * groups
        rows = [pl.ds(start + k, 8, stride=groups) for k in range(-1, groups + 1)]
        lines = [[src[x, h, r, :] for r in rows] for h in range(2)]
        for k in range(1, groups + 1):
            center = [lines[h][k] for h in range(2)]
            up, down = lane_shift(center, 1), lane_shift(center, -1)
            for h in range(2):
                c = center[h]
                step = factor[x, h, rows[k], :]
                positive = step > 0
                pairs = (
                    (src[x - 1, h, rows[k], :], src[x + 1, h, rows[k], :]),
                    (lines[h][k - 1], lines[h][k + 1]),
                    (down[h], up[h]),
                )
                total = None
                for l, r in pairs:
                    low = jnp.minimum(jnp.minimum(l, r), c)
                    high = jnp.maximum(jnp.maximum(l, r), c)
                    diff = c - jnp.where(positive, low, high)
                    total = diff * diff if total is None else total + diff * diff
                dst[y, h, rows[k], :] = c - step * (jnp.sqrt(total) - 1.0)

    source, target = first, second
    for sweep in range(1, SWEEPS + 1):
        offset, dst = (0, target) if sweep < SWEEPS else (SWEEPS, cur_out)
        groups = 6 if DEEP - sweep > 4 else 5

        def body(x, carry, source=source, dst=dst, offset=offset, groups=groups):
            sweep_plane(source, x, dst, x - offset, groups)
            return carry

        lax.fori_loop(sweep, WIDE - sweep, body, 0, unroll=2)
        source, target = target, source

    def count(x, carry):
        for h in range(2):
            for unit in range(CY // UNIT):
                rows = pl.ds(OWN + unit * UNIT, UNIT)
                after = jnp.tanh(cur_out[x + 2, h, rows, :])
                before = jnp.tanh(adv[x, pl.ds(unit * UNIT, UNIT), half(h)])
                sums[0] += after - before
                sums[1] += 1.0 - after * after
        return carry

    lax.fori_loop(0, CX, count, 0, unroll=2)
    lane = lax.broadcasted_iota(jnp.int32, (1, LANES), 1)
    part[...] = jnp.where(lane < 64, jnp.sum(sums[0]), jnp.sum(sums[1]))


def sweeps(tiles, adv, halos):
    shape = lambda *s: jax.ShapeDtypeStruct(s, F32)
    return pl.pallas_call(
        sweep_kernel,
        out_shape=[shape(CX + 4, 2, ROWS, LANES), shape(CX + 2, 2, ROWS, LANES), shape(1, LANES)],
        in_specs=[SMEM, VMEM] + [ANY] * 6,
        out_specs=[VMEM] * 3,
        scratch_shapes=[
            pltpu.VMEM((WIDE, 2, ROWS, LANES), F32),
            pltpu.VMEM((WIDE, 2, ROWS, LANES), F32),
            pltpu.VMEM((WIDE, 2, ROWS, LANES), F32),
            pltpu.VMEM((2, 2, CY, LANES), F32),
            pltpu.VMEM((8, LANES), F32),
            pltpu.VMEM((2, UNIT, LANES), F32),
            pltpu.SemaphoreType.DMA((2, 11)),
        ],
        compiler_params=pltpu.CompilerParams(vmem_limit_bytes=LIMIT),
        name="sweeps",
    )(tiles, adv, *halos)


CHUNKS = ((0, 10), (10, 18), (18, 26), (26, 32))


def extend_kernel(
    parts, cur, weight, stress, xlo, xhi, ylo, yhi, clo, chi,
    level_out, stress_out,
    pad, ring, mix, stage, sems, out_sems,
):
    def chunk(n):
        start, stop = CHUNKS[n]
        pieces = [(stress.at[:, pl.ds(start, stop - start)], start + 2, stop - start)]
        if n == 0:
            pieces.append((xlo, 0, 2))
        if n == len(CHUNKS) - 1:
            pieces.append((xhi, CX + 2, 2))
        return [
            pltpu.make_async_copy(
                src.at[:, :, :, half(h)],
                pad.at[:, pl.ds(at, size), h, pl.ds(OWN, CY), :],
                sems.at[n, h, m],
            )
            for h in range(2)
            for m, (src, at, size) in enumerate(pieces)
        ]

    chunks = [chunk(n) for n in range(len(CHUNKS))]
    for copies in chunks:
        for copy in copies:
            copy.start()
    sums = parts[...]
    shift = sums[:, 0:1] / sums[:, 64:65]
    for h in range(2):
        for c in range(COMPS):
            pad[c, 2 : CX + 2, h, OWN - 2 : OWN, :] = ylo[c, :, :, half(h)]
            pad[c, 2 : CX + 2, h, OWN + CY : OWN + CY + 2, :] = yhi[c, :, :, half(h)]
            for corner, row in ((clo, OWN - 1), (chi, OWN + CY)):
                for x, n in ((1, c), (CX + 2, COMPS + c)):
                    at = 2 * DEEP + n // 8
                    pad[c, x, h, row : row + 1, :] = corner[at, n % 8 : n % 8 + 1, half(h)]

    def blend(mixes, center, around):
        value = mixes[6] * center
        for n in range(6):
            value = value + mixes[n] * around[n]
        return value

    def neighbours(load, groups):
        start = OWN + CY // 2 - 4 * groups
        rows = [pl.ds(start + k, 8, stride=groups) for k in range(-1, groups + 1)]
        lines = [[load(0, h, r) for r in rows] for h in range(2)]
        for k in range(1, groups + 1):
            center = [lines[h][k] for h in range(2)]
            up, down = lane_shift(center, 1), lane_shift(center, -1)
            yield rows[k], center, [
                [
                    load(-1, h, rows[k]), load(1, h, rows[k]), lines[h][k - 1], lines[h][k + 1],
                    down[h], up[h],
                ]
                for h in range(2)
            ]

    def first_step(i, slot, groups=5):
        levels = neighbours(lambda dx, h, r: cur[i + 1 + dx, h, r, :], groups)
        comps = [
            neighbours(lambda dx, h, r, c=c: pad[c, i + 1 + dx, h, r, :], groups)
            for c in range(COMPS)
        ]
        for rows, center, around in levels:
            mixes = []
            for h in range(2):
                c = center[h]
                w = [
                    recip(1.0 + jnp.exp(jnp.minimum(2.0 * (n - c), 87.0)))
                    for n in around[h]
                ]
                total = w[0] + w[1] + w[2] + w[3] + w[4] + w[5]
                gate = weight[i, h, rows, :] * 0.5 * (1.0 + jnp.tanh(2.0 * (c - shift)))
                scaled = gate * recip(total)
                w = [scaled * n for n in w] + [1.0 - gate]
                mixes.append(w)
                for n in range(7):
                    mix[slot % 2, n, h, rows, :] = w[n]
            for comp in range(COMPS):
                _, center, around = next(comps[comp])
                for h in range(2):
                    ring[slot, comp, h, rows, :] = blend(mixes[h], center[h], around[h])

    def second_step(x, slot):
        slots = {dx: (slot + dx) % 4 for dx in (-1, 0, 1)}
        groups = CY // 8
        comps = [
            neighbours(lambda dx, h, r, c=c: ring[slots[dx], c, h, r, :], groups)
            for c in range(COMPS)
        ]
        for k in range(groups):
            rows = pl.ds(OWN + k, 8, stride=groups)
            mixes = [[mix[slot % 2, n, h, rows, :] for n in range(7)] for h in range(2)]
            for comp in range(COMPS):
                _, center, around = next(comps[comp])
                for h in range(2):
                    stage[comp, x, h, pl.ds(k, 8, stride=groups), :] = blend(
                        mixes[h], center[h], around[h]
                    )
        for h in range(2):
            level_out[x, :, half(h)] = cur[x + 2, h, OWN : OWN + CY, :] - shift

    outs = []
    for n in range(len(CHUNKS)):
        for copy in chunks[n]:
            copy.wait()
        if n == 0:
            first_step(0, 0, groups=4)
            first_step(1, 1)

        def body(group, carry):
            for k in range(4):
                i = group * 4 + k + 2
                first_step(i, (k + 2) % 4)
                second_step(i - 2, (k + 1) % 4)
            return carry

        lax.fori_loop(2 * n, 2 * n + 2, body, 0)
        planes = pl.ds(8 * n, 8)
        for h in range(2):
            copy = pltpu.make_async_copy(
                stage.at[:, planes, h], stress_out.at[:, planes, :, half(h)], out_sems.at[n, h]
            )
            copy.start()
            outs.append(copy)
    for copy in outs:
        copy.wait()


def extend(parts, cur, weight, stress, halos):
    shape = lambda *s: jax.ShapeDtypeStruct(s, F32)
    z = 2 * LANES
    return pl.pallas_call(
        extend_kernel,
        out_shape=[shape(CX, CY, z), shape(COMPS, CX, CY, z)],
        in_specs=[VMEM, VMEM, VMEM, ANY, ANY, ANY, VMEM, VMEM, VMEM, VMEM],
        out_specs=[VMEM, ANY],
        scratch_shapes=[
            pltpu.VMEM((COMPS, CX + 4, 2, ROWS, LANES), F32),
            pltpu.VMEM((4, COMPS, 2, ROWS, LANES), F32),
            pltpu.VMEM((2, 7, 2, ROWS, LANES), F32),
            pltpu.VMEM((COMPS, CX, 2, CY, LANES), F32),
            pltpu.SemaphoreType.DMA((4, 2, 2)),
            pltpu.SemaphoreType.DMA((4, 2)),
        ],
        compiler_params=pltpu.CompilerParams(vmem_limit_bytes=LIMIT),
        name="extend",
    )(parts, cur, weight, stress, *halos)


def on_device(level, velocity, stress, tiles):
    nx, ny = lax.axis_size("gx"), lax.axis_size("gy")

    def send(value, dx, dy):
        if dy == 0:
            return lax.ppermute(value, "gx", [(i, (i + dx) % nx) for i in range(nx)])
        if dx == 0:
            return lax.ppermute(value, "gy", [(i, (i + dy) % ny) for i in range(ny)])
        pairs = [
            (i * ny + j, (i + dx) % nx * ny + (j + dy) % ny) for i in range(nx) for j in range(ny)
        ]
        return lax.ppermute(value, ("gx", "gy"), pairs)

    def total(value):
        rounds = (
            ("gx", [[i ^ 1 for i in range(nx)]]),
            ("gx", [[(i + 2 * k) % nx for i in range(nx)] for k in range(1, nx // 2)]),
            ("gy", [[i // 4 * 4 + (i + k) % 4 for i in range(ny)] for k in range(1, 4)]),
            ("gy", [[(i + 4 * k) % ny for i in range(ny)] for k in range(1, ny // 4)]),
        )
        for axis, moves in rounds:
            moved = [lax.ppermute(value, axis, list(enumerate(move))) for move in moves]
            for other in moved:
                value = value + other
        return value

    xlo = send(level[-3:], 1, 0)
    xhi = send(level[:3], -1, 0)
    ylo = send(level[:, -3:], 0, 1)
    yhi = send(level[:, :3], 0, -1)
    sxlo, sxhi = send(stress[:, -2:], 1, 0), send(stress[:, :2], -1, 0)
    sylo, syhi = send(stress[:, :, -2:], 0, 1), send(stress[:, :, :2], 0, -1)
    drift = inner_drift(level, velocity)
    adv, to_xp, to_xn, to_yp, to_yn = advect(tiles, level, xlo, xhi, ylo, yhi, velocity, drift)
    axlo, axhi = send(to_xn, 1, 0), send(to_xp, -1, 0)
    aylo, ayhi = send(to_yn, 0, 1), send(to_yp, 0, -1)
    row = lax.broadcasted_iota(jnp.int32, (1, 8, 1), 1)
    none = jnp.zeros((4, 2 * LANES), F32)

    def corners(rows, mark, y):
        faces = [jnp.where(row == mark, f[DEEP:, rows], f[:DEEP, rows]) for f in (axlo, axhi)]
        tail = jnp.concatenate((sxlo[:, 1, y], sxhi[:, 0, y], none), axis=0)
        return jnp.concatenate(faces + [tail.reshape(2, 8, 2 * LANES)], axis=0)

    clo = send(corners(slice(-8, None), 0, CY - 1), 0, 1)
    chi = send(corners(slice(0, 8), 7, 0), 0, -1)
    cur, weight, part = sweeps(tiles, adv, (axlo, axhi, aylo, ayhi, clo, chi))
    return extend(
        total(part), cur, weight, stress, (sxlo, sxhi, sylo, syhi, clo, chi)
    )


def solution(mesh):
    in_specs = (
        P("gx", "gy", None),
        P(None, "gx", "gy", None),
        P(None, "gx", "gy", None),
        P("gx", "gy", None),
    )
    out_specs = (P("gx", "gy", None), P(None, "gx", "gy", None))
    return jax.shard_map(
        on_device, mesh=mesh, in_specs=in_specs, out_specs=out_specs, check_vma=False
    )
```

```python
import functools

import jax
import jax.numpy as jnp
from jax import lax
from jax.experimental import pallas as pl
from jax.experimental.pallas import tpu as pltpu
from jax.sharding import PartitionSpec as P

TILE = 16
SWEEPS = 5
EPSILON = 1e-06
TIME_STEP = 0.4
PSEUDO_STEP = 0.3

CX = 32
CY = 32
LANES = 128
DEEP = 7
ROWS = 64
OWN = 16
UNIT = 16
COMPS = 6
F32 = jnp.float32
DOUBLED = 2.0 * 1.4426950408889634
LIMIT = 60 * 1024 * 1024
ANY = pl.BlockSpec(memory_space=pl.ANY)
VMEM = pl.BlockSpec(memory_space=pltpu.VMEM)
SMEM = pl.BlockSpec(memory_space=pltpu.SMEM)


def half(h):
    return pl.ds(h * LANES, LANES)


def recip(x):
    return pl.reciprocal(x, approx=True)


def lane_shift(pair, k):
    lane = lax.broadcasted_iota(jnp.int32, pair[0].shape, pair[0].ndim - 1)
    turned = [pltpu.roll(p, (-k) % LANES, p.ndim - 1) for p in pair]
    edge = lane >= LANES - k if k > 0 else lane < -k
    return [jnp.where(edge, turned[1 - h], turned[h]) for h in range(2)]


def weno(d, positive):
    v = [jnp.where(positive, d[k], d[5 - k]) for k in range(5)]
    d1, d2, d3, d4 = (v[k + 1] - v[k] for k in range(4))
    u1, u2, u3 = d2 - d1, d3 - d2, d4 - d3
    g1 = d2 + d2 + u1
    g2 = d2 + d3
    g3 = u3 - (d3 + d3)
    scale = 13.0 / 3.0
    a1 = recip(4.0 * EPSILON + (scale * u1 * u1 + g1 * g1))
    a2 = recip(4.0 * EPSILON + (scale * u2 * u2 + g2 * g2))
    a3 = recip(4.0 * EPSILON + (scale * u3 * u3 + g3 * g3))
    a1 = a1 * a1
    a2 = 6.0 * (a2 * a2)
    a3 = 3.0 * (a3 * a3)
    top = a1 * (u1 - u2) + 0.5 * (a3 * (u2 - u3))
    mid = v[2] + (d3 + d3 + d2) * (1.0 / 6.0)
    return mid + top * (recip(a1 + a2 + a3) * (1.0 / 3.0))


def band_table(tiles_ref):
    shape = (8, LANES)
    row = lax.broadcasted_iota(jnp.int32, shape, 0)
    lane = lax.broadcasted_iota(jnp.int32, shape, 1)
    numbers = (row // 2) * 16 + (row % 2) * 8 + lane // TILE
    flags = jnp.zeros(shape, F32)
    for slot in range(tiles_ref.shape[-1]):
        flags = jnp.where(numbers == tiles_ref[0, 0, slot], 1.0, flags)
    return flags


def derivative(line, speed):
    return speed * weno([line[k + 1] - line[k] for k in range(6)], speed > 0)


def along_x(pad, x, h, at, size):
    return [pad[x + k, h, pl.ds(at, size), :] for k in range(-3, 4)]


def along_y(pad, x, h, at, size):
    return [pad[x, h, pl.ds(at + k, size), :] for k in range(-3, 4)]


def cut_kernel(level, stress, to_xp, to_xn, to_yp, to_yn, faces, x_sems, y_sems):
    copies = []
    for n, (out, at) in enumerate(((to_xp, 0), (to_xn, CX))):
        deep = lambda size: pl.ds(at and at - size, size)
        copies.append(pltpu.make_async_copy(level.at[deep(3)], out.at[pl.ds(0, 3)], x_sems.at[n, 0]))
        for c in range(COMPS):
            copies.append(
                pltpu.make_async_copy(
                    stress.at[c, deep(2)], out.at[pl.ds(3 + 2 * c, 2)], x_sems.at[n, 1 + c]
                )
            )
    for copy in copies:
        copy.start()
    sides = []
    for n, y in enumerate((0, CY - 8)):
        side = []
        for h in range(2):
            for m in range(1 + COMPS):
                src = stress.at[m - 1] if m else level
                side.append(
                    pltpu.make_async_copy(
                        src.at[:, pl.ds(y, 8), half(h)], faces.at[m, n, h], y_sems.at[m, n, h]
                    )
                )
        for copy in side:
            copy.start()
        sides.append(side)
    flat = faces.reshape(1 + COMPS, 2, 2, CX * 8, LANES)
    for n, out in enumerate((to_yp, to_yn)):
        for copy in sides[n]:
            copy.wait()
        for h in range(2):
            for m in range(1 + COMPS):
                depth = 2 if m else 3
                first = 1 + 2 * m if m else 0
                for k in range(depth):
                    row = k if n == 0 else 8 - depth + k
                    for x in range(0, CX, 8):
                        out[first + k, x : x + 8, half(h)] = flat[
                            m, n, h, pl.ds(8 * x + row, 8, stride=8), :
                        ]
    for copy in copies:
        copy.wait()


def cut(level, stress):
    message = jax.ShapeDtypeStruct((3 + 2 * COMPS, CX, 2 * LANES), F32)
    return pl.pallas_call(
        cut_kernel,
        out_shape=[message] * 4,
        in_specs=[ANY] * 2,
        out_specs=[ANY] * 2 + [VMEM] * 2,
        scratch_shapes=[
            pltpu.VMEM((1 + COMPS, 2, 2, CX, 8, LANES), F32),
            pltpu.SemaphoreType.DMA((2, 1 + COMPS)),
            pltpu.SemaphoreType.DMA((1 + COMPS, 2, 2)),
        ],
        compiler_params=pltpu.CompilerParams(vmem_limit_bytes=LIMIT),
        name="cut",
    )(level, stress)


def inner_kernel(level, speed, drift, pad, sems):
    copies = [
        pltpu.make_async_copy(level.at[:, :, half(h)], pad.at[:, h], sems.at[h]) for h in range(2)
    ]
    for copy in copies:
        copy.start()
    for copy in copies:
        copy.wait()

    def plane(x, with_x):
        for unit in range(CY // UNIT):
            rows = pl.ds(unit * UNIT, UNIT)
            v = [[speed[d, x, rows, half(h)].astype(F32) for h in range(2)] for d in range(3)]
            for part in range(UNIT // 8):
                at = unit * UNIT + 8 * part
                cut = slice(8 * part, 8 * part + 8)
                center = [pad[x, h, pl.ds(at, 8), :] for h in range(2)]
                ups = [lane_shift(center, k) for k in (1, 2, 3)]
                downs = [lane_shift(center, -k) for k in (3, 2, 1)]
                for h in range(2):
                    line = [s[h] for s in downs] + [center[h]] + [s[h] for s in ups]
                    total = derivative(line, v[2][h][cut])
                    if with_x:
                        total = total + derivative(along_x(pad, x, h, at, 8), v[0][h][cut])
                    if 8 <= at < CY - 8:
                        total = total + derivative(along_y(pad, x, h, at, 8), v[1][h][cut])
                    drift[x, pl.ds(at, 8), half(h)] = total

    def inner(x, carry):
        plane(x, True)
        return carry

    def outer(x, carry):
        plane(x, False)
        plane(x + CX - 3, False)
        return carry

    lax.fori_loop(0, 3, outer, 0)
    lax.fori_loop(3, CX - 3, inner, 0, unroll=2)


def inner_drift(level, speed):
    return pl.pallas_call(
        inner_kernel,
        out_shape=jax.ShapeDtypeStruct(level.shape, F32),
        in_specs=[ANY, VMEM],
        out_specs=VMEM,
        scratch_shapes=[
            pltpu.VMEM((CX, 2, CY, LANES), F32),
            pltpu.SemaphoreType.DMA((2,)),
        ],
        compiler_params=pltpu.CompilerParams(vmem_limit_bytes=LIMIT),
        cost_estimate=pl.CostEstimate(
            flops=180 * level.size, bytes_accessed=14 * level.size, transcendentals=9 * level.size
        ),
        name="inner_drift",
    )(level, speed)


def advect_kernel(
    tiles, level, xlo, xhi, ylo, yhi, speed, drift,
    adv, to_xp, to_xn, to_yp, to_yn,
    pad, table, faces, sems, y_sems,
):
    copies = []
    for h in range(2):
        for n, (src, at, size) in enumerate(((level, 3, CX), (xlo, 0, 3), (xhi, CX + 3, 3))):
            copies.append(
                pltpu.make_async_copy(
                    src.at[pl.ds(0, size), :, half(h)],
                    pad.at[pl.ds(at, size), h, pl.ds(8, CY), :],
                    sems.at[h, n],
                )
            )
    for n, src in enumerate((ylo, yhi)):
        copies.append(pltpu.make_async_copy(src.at[pl.ds(0, 3)], faces.at[n], y_sems.at[n]))
    for copy in copies:
        copy.start()
    table[...] = band_table(tiles)
    for copy in copies:
        copy.wait()
    flat = pad.reshape((CX + 6) * 2 * 48, LANES)
    for n, row in enumerate((5, 8 + CY)):
        for h in range(2):
            for k in range(3):
                for x in range(0, CX, 8):
                    rows = pl.ds(((x + 3) * 2 + h) * 48 + row + k, 8, stride=96)
                    flat[rows, :] = faces[n, k, x : x + 8, half(h)]

    def plane(x, with_x):
        for unit in range(CY // UNIT):
            rows = pl.ds(unit * UNIT, UNIT)
            for h in range(2):
                vx = speed[0, x, rows, half(h)].astype(F32) if with_x else None
                vy = speed[1, x, rows, half(h)].astype(F32)
                for part in range(UNIT // 8):
                    at = unit * UNIT + 8 * part
                    cut = slice(8 * part, 8 * part + 8)
                    total = drift[x, pl.ds(at, 8), half(h)]
                    if with_x:
                        total = total + derivative(along_x(pad, x + 3, h, at + 8, 8), vx[cut])
                    if at in (0, CY - 8):
                        total = total + derivative(along_y(pad, x + 3, h, at + 8, 8), vy[cut])
                    adv[x, pl.ds(at, 8), half(h)] = (
                        pad[x + 3, h, pl.ds(at + 8, 8), :] - TIME_STEP * total
                    )

    def inner(x, carry):
        plane(x, False)
        return carry

    def outer(x, carry):
        plane(x, True)
        plane(x + CX - 3, True)
        return carry

    lax.fori_loop(0, 3, outer, 0)
    lax.fori_loop(3, CX - 3, inner, 0, unroll=2)
    low, high = CX - DEEP, CX
    to_xp[0:DEEP] = adv[0:DEEP]
    to_xn[0:DEEP] = adv[low:high]
    row8 = lax.broadcasted_iota(jnp.int32, (8, LANES), 0)
    for h in range(2):
        for j in range(2):
            rows = pl.ds(j * TILE, TILE)
            for i, face in ((0, to_xp), (1, to_xn)):
                r = i * 4 + j * 2 + h
                face[DEEP, rows, half(h)] = jnp.broadcast_to(table[r : r + 1, :], (TILE, LANES))
        for i in range(2):
            first = table[i * 4 + h : i * 4 + h + 1, :]
            last = table[i * 4 + 2 + h : i * 4 + 3 + h, :]
            for x in range(i * TILE, i * TILE + TILE):
                to_yp[x, :, half(h)] = jnp.where(row8 == 7, first, adv[x, 0:8, half(h)])
                to_yn[x, :, half(h)] = jnp.where(row8 == 0, last, adv[x, CY - 8 : CY, half(h)])


def advect(tiles, level, xlo, xhi, ylo, yhi, speed, drift):
    shape = lambda *s: jax.ShapeDtypeStruct(s, F32)
    z = 2 * LANES
    return pl.pallas_call(
        advect_kernel,
        out_shape=[shape(CX, CY, z)]
        + [shape(8, CY, z)] * 2
        + [shape(CX, 8, z)] * 2,
        in_specs=[SMEM, ANY, ANY, ANY, ANY, ANY, VMEM, VMEM],
        out_specs=[VMEM] * 5,
        scratch_shapes=[
            pltpu.VMEM((CX + 6, 2, 48, LANES), F32),
            pltpu.VMEM((8, LANES), F32),
            pltpu.VMEM((2, 3, CX, z), F32),
            pltpu.SemaphoreType.DMA((2, 3)),
            pltpu.SemaphoreType.DMA((2,)),
        ],
        compiler_params=pltpu.CompilerParams(vmem_limit_bytes=LIMIT),
        name="advect",
    )(tiles, level, xlo, xhi, ylo, yhi, speed, drift)


WIDE = CX + 2 * DEEP


def sweep_kernel(
    tiles, adv, xlo, xhi, ylo, yhi, clo, chi,
    cur_out, weight_out, part,
    first, second, factor, masks, table, sums, sems,
):
    copies = []
    for h in range(2):
        pieces = (
            (adv, DEEP, CX, OWN, CY),
            (xlo.at[pl.ds(0, DEEP)], 0, DEEP, OWN, CY),
            (xhi.at[pl.ds(0, DEEP)], DEEP + CX, DEEP, OWN, CY),
            (ylo, DEEP, CX, OWN - 8, 8),
            (yhi, DEEP, CX, OWN + CY, 8),
            (clo.at[pl.ds(0, DEEP)], 0, DEEP, OWN - 8, 8),
            (clo.at[pl.ds(DEEP, DEEP)], DEEP + CX, DEEP, OWN - 8, 8),
            (chi.at[pl.ds(0, DEEP)], 0, DEEP, OWN + CY, 8),
            (chi.at[pl.ds(DEEP, DEEP)], DEEP + CX, DEEP, OWN + CY, 8),
        )
        for n, (src, x, nx, y, ny) in enumerate(pieces):
            copies.append(
                pltpu.make_async_copy(
                    src.at[:, :, half(h)],
                    first.at[pl.ds(x, nx), h, pl.ds(y, ny), :],
                    sems.at[h, n],
                )
            )
        for n, src in enumerate((xlo, xhi)):
            copies.append(
                pltpu.make_async_copy(
                    src.at[pl.ds(DEEP, 1), :, half(h)], masks.at[pl.ds(n, 1), h], sems.at[h, 9 + n]
                )
            )
    for copy in copies:
        copy.start()
    table[...] = band_table(tiles)
    sums[...] = jnp.zeros(sums.shape, F32)
    for copy in copies:
        copy.wait()

    def prepare(x, bands, keep):
        for h in range(2):
            for group in range(-1, 5):
                rows = pl.ds(OWN + 8 * group, 8)
                value = first[x, h, rows, :]
                if group == -1:
                    band = jnp.broadcast_to(value[0:1], value.shape)
                elif group == 4:
                    band = jnp.broadcast_to(value[7:8], value.shape)
                else:
                    band = bands(group, h)
                square = value * value
                weight = band * recip(1.0 + square * (1.0 / 36.0))
                sign = value * lax.rsqrt(square + 1.0)
                factor[x, h, rows, :] = PSEUDO_STEP * sign * weight
                if keep:
                    weight_out[x - DEEP + 1, h, rows, :] = weight

    def halo_bands(n):
        return lambda group, h: masks[n, h, pl.ds(8 * group, 8), :]

    def own_bands(i):
        def bands(group, h):
            r = i * 4 + (group // 2) * 2 + h
            return jnp.broadcast_to(table[r : r + 1, :], (8, LANES))

        return bands

    def run(start, stop, bands, keep):
        def body(x, carry):
            prepare(x, bands, keep)
            return carry

        lax.fori_loop(start, stop, body, 0, unroll=2)

    run(1, DEEP - 1, halo_bands(0), False)
    prepare(DEEP - 1, halo_bands(0), True)
    run(DEEP, DEEP + TILE, own_bands(0), True)
    run(DEEP + TILE, DEEP + CX, own_bands(1), True)
    prepare(DEEP + CX, halo_bands(1), True)
    run(DEEP + CX + 1, WIDE - 1, halo_bands(1), False)

    def sweep_plane(src, x, dst, y, groups):
        start = OWN + CY // 2 - 4 * groups
        rows = [pl.ds(start + k, 8, stride=groups) for k in range(-1, groups + 1)]
        lines = [[src[x, h, r, :] for r in rows] for h in range(2)]
        for k in range(1, groups + 1):
            center = [lines[h][k] for h in range(2)]
            up, down = lane_shift(center, 1), lane_shift(center, -1)
            for h in range(2):
                c = center[h]
                step = factor[x, h, rows[k], :]
                positive = step > 0
                pairs = (
                    (src[x - 1, h, rows[k], :], src[x + 1, h, rows[k], :]),
                    (lines[h][k - 1], lines[h][k + 1]),
                    (down[h], up[h]),
                )
                total = None
                for l, r in pairs:
                    low = jnp.minimum(jnp.minimum(l, r), c)
                    high = jnp.maximum(jnp.maximum(l, r), c)
                    diff = c - jnp.where(positive, low, high)
                    total = diff * diff if total is None else total + diff * diff
                slope = total * lax.rsqrt(jnp.maximum(total, 1e-36))
                dst[y, h, rows[k], :] = c - step * (slope - 1.0)

    source, target = first, second
    for sweep in range(1, SWEEPS + 1):
        offset, dst = (0, target) if sweep < SWEEPS else (SWEEPS, cur_out)
        groups = 6 if DEEP - sweep > 4 else 5

        def body(x, carry, source=source, dst=dst, offset=offset, groups=groups):
            sweep_plane(source, x, dst, x - offset, groups)
            return carry

        lax.fori_loop(sweep, WIDE - sweep, body, 0, unroll=2)
        source, target = target, source

    def count(x, carry):
        for h in range(2):
            for unit in range(CY // UNIT):
                rows = pl.ds(OWN + unit * UNIT, UNIT)
                after = jnp.tanh(cur_out[x + 2, h, rows, :])
                before = jnp.tanh(adv[x, pl.ds(unit * UNIT, UNIT), half(h)])
                sums[0] += after - before
                sums[1] += 1.0 - after * after
        return carry

    lax.fori_loop(0, CX, count, 0, unroll=2)
    lane = lax.broadcasted_iota(jnp.int32, (1, LANES), 1)
    part[...] = jnp.where(lane < 64, jnp.sum(sums[0]), jnp.sum(sums[1]))


def sweeps(tiles, adv, halos):
    shape = lambda *s: jax.ShapeDtypeStruct(s, F32)
    return pl.pallas_call(
        sweep_kernel,
        out_shape=[shape(CX + 4, 2, ROWS, LANES), shape(CX + 2, 2, ROWS, LANES), shape(1, LANES)],
        in_specs=[SMEM, VMEM] + [ANY] * 6,
        out_specs=[VMEM] * 3,
        scratch_shapes=[
            pltpu.VMEM((WIDE, 2, ROWS, LANES), F32),
            pltpu.VMEM((WIDE, 2, ROWS, LANES), F32),
            pltpu.VMEM((WIDE, 2, ROWS, LANES), F32),
            pltpu.VMEM((2, 2, CY, LANES), F32),
            pltpu.VMEM((8, LANES), F32),
            pltpu.VMEM((2, UNIT, LANES), F32),
            pltpu.SemaphoreType.DMA((2, 11)),
        ],
        compiler_params=pltpu.CompilerParams(vmem_limit_bytes=LIMIT),
        name="sweeps",
    )(tiles, adv, *halos)


CHUNKS = ((0, 10), (10, 18), (18, 26), (26, 32))


def extend_kernel(
    parts, cur, weight, stress, xlo, xhi, ylo, yhi, clo, chi,
    level_out, stress_out,
    pad, ring, mix, stage, sems, x_sems, out_sems,
):
    def chunk(n):
        start, stop = CHUNKS[n]
        own = stress.at[:, pl.ds(start, stop - start)]
        copies = [
            pltpu.make_async_copy(
                own.at[:, :, :, half(h)],
                pad.at[:, pl.ds(start + 2, stop - start), h, pl.ds(OWN, CY), :],
                sems.at[n, h],
            )
            for h in range(2)
        ]
        for side, src in ((0, xlo), (3, xhi)):
            if n == side:
                at = 0 if n == 0 else CX + 2
                for h in range(2):
                    for c in range(COMPS):
                        copies.append(
                            pltpu.make_async_copy(
                                src.at[pl.ds(3 + 2 * c, 2), :, half(h)],
                                pad.at[c, pl.ds(at, 2), h, pl.ds(OWN, CY), :],
                                x_sems.at[side % 2, h, c],
                            )
                        )
        return copies

    chunks = [chunk(n) for n in range(len(CHUNKS))]
    for copies in chunks:
        for copy in copies:
            copy.start()
    sums = parts[...]
    shift = sums[:, 0:1] / sums[:, 64:65]
    flat = pad.reshape(COMPS, (CX + 4) * 2 * ROWS, LANES)
    for h in range(2):
        for c in range(COMPS):
            for face, row in ((ylo, OWN - 2), (yhi, OWN + CY)):
                for k in range(2):
                    for x in range(0, CX, 8):
                        at = ((x + 2) * 2 + h) * ROWS + row + k
                        flat[c, pl.ds(at, 8, stride=2 * ROWS), :] = face[
                            3 + 2 * c + k, x : x + 8, half(h)
                        ]
            for corner, row in ((clo, OWN - 1), (chi, OWN + CY)):
                for x, n in ((1, c), (CX + 2, COMPS + c)):
                    at = 2 * DEEP + n // 8
                    pad[c, x, h, row : row + 1, :] = corner[at, n % 8 : n % 8 + 1, half(h)]

    def blend(mixes, center, around):
        value = mixes[6] * center
        for n in range(6):
            value = value + mixes[n] * around[n]
        return value

    def neighbours(load, groups):
        start = OWN + CY // 2 - 4 * groups
        rows = [pl.ds(start + k, 8, stride=groups) for k in range(-1, groups + 1)]
        lines = [[load(0, h, r) for r in rows] for h in range(2)]
        for k in range(1, groups + 1):
            center = [lines[h][k] for h in range(2)]
            up, down = lane_shift(center, 1), lane_shift(center, -1)
            yield rows[k], center, [
                [
                    load(-1, h, rows[k]), load(1, h, rows[k]), lines[h][k - 1], lines[h][k + 1],
                    down[h], up[h],
                ]
                for h in range(2)
            ]

    def first_step(i, slot, groups=5):
        levels = neighbours(lambda dx, h, r: cur[i + 1 + dx, h, r, :] * DOUBLED, groups)
        comps = [
            neighbours(lambda dx, h, r, c=c: pad[c, i + 1 + dx, h, r, :], groups)
            for c in range(COMPS)
        ]
        for rows, center, around in levels:
            mixes = []
            for h in range(2):
                c = center[h]
                w = [recip(1.0 + jnp.exp2(jnp.minimum(n - c, 125.5))) for n in around[h]]
                total = w[0] + w[1] + w[2] + w[3] + w[4] + w[5]
                gate = weight[i, h, rows, :] * 0.5 * (1.0 + jnp.tanh(c * (2.0 / DOUBLED) - 2.0 * shift))
                scaled = gate * recip(total)
                w = [scaled * n for n in w] + [1.0 - gate]
                mixes.append(w)
                for n in range(7):
                    mix[slot % 2, n, h, rows, :] = w[n]
            for comp in range(COMPS):
                _, center, around = next(comps[comp])
                for h in range(2):
                    ring[slot, comp, h, rows, :] = blend(mixes[h], center[h], around[h])

    def second_step(x, slot):
        slots = {dx: (slot + dx) % 4 for dx in (-1, 0, 1)}
        groups = CY // 8
        comps = [
            neighbours(lambda dx, h, r, c=c: ring[slots[dx], c, h, r, :], groups)
            for c in range(COMPS)
        ]
        for k in range(groups):
            rows = pl.ds(OWN + k, 8, stride=groups)
            mixes = [[mix[slot % 2, n, h, rows, :] for n in range(7)] for h in range(2)]
            for comp in range(COMPS):
                _, center, around = next(comps[comp])
                for h in range(2):
                    stage[comp, x, h, pl.ds(k, 8, stride=groups), :] = blend(
                        mixes[h], center[h], around[h]
                    )
        for h in range(2):
            level_out[x, :, half(h)] = cur[x + 2, h, OWN : OWN + CY, :] - shift

    outs = []
    for n in range(len(CHUNKS)):
        for copy in chunks[n]:
            copy.wait()
        if n == 0:
            first_step(0, 0, groups=4)
            first_step(1, 1)

        def body(group, carry):
            for k in range(4):
                i = group * 4 + k + 2
                first_step(i, (k + 2) % 4)
                second_step(i - 2, (k + 1) % 4)
            return carry

        lax.fori_loop(2 * n, 2 * n + 2, body, 0)
        planes = pl.ds(8 * n, 8)
        for h in range(2):
            copy = pltpu.make_async_copy(
                stage.at[:, planes, h], stress_out.at[:, planes, :, half(h)], out_sems.at[n, h]
            )
            copy.start()
            outs.append(copy)
    for copy in outs:
        copy.wait()


def extend(parts, cur, weight, stress, halos):
    shape = lambda *s: jax.ShapeDtypeStruct(s, F32)
    z = 2 * LANES
    return pl.pallas_call(
        extend_kernel,
        out_shape=[shape(CX, CY, z), shape(COMPS, CX, CY, z)],
        in_specs=[VMEM, VMEM, VMEM, ANY, ANY, ANY, VMEM, VMEM, VMEM, VMEM],
        out_specs=[VMEM, ANY],
        scratch_shapes=[
            pltpu.VMEM((COMPS, CX + 4, 2, ROWS, LANES), F32),
            pltpu.VMEM((4, COMPS, 2, ROWS, LANES), F32),
            pltpu.VMEM((2, 7, 2, ROWS, LANES), F32),
            pltpu.VMEM((COMPS, CX, 2, CY, LANES), F32),
            pltpu.SemaphoreType.DMA((4, 2)),
            pltpu.SemaphoreType.DMA((2, 2, COMPS)),
            pltpu.SemaphoreType.DMA((4, 2)),
        ],
        compiler_params=pltpu.CompilerParams(vmem_limit_bytes=LIMIT),
        name="extend",
    )(parts, cur, weight, stress, *halos)


def on_device(level, velocity, stress, tiles):
    nx, ny = lax.axis_size("gx"), lax.axis_size("gy")

    def send(value, dx, dy):
        if dy == 0:
            return lax.ppermute(value, "gx", [(i, (i + dx) % nx) for i in range(nx)])
        if dx == 0:
            return lax.ppermute(value, "gy", [(i, (i + dy) % ny) for i in range(ny)])
        pairs = [
            (i * ny + j, (i + dx) % nx * ny + (j + dy) % ny) for i in range(nx) for j in range(ny)
        ]
        return lax.ppermute(value, ("gx", "gy"), pairs)

    def total(value):
        rounds = (
            ("gx", [[i ^ 1 for i in range(nx)]]),
            ("gx", [[(i + 2 * k) % nx for i in range(nx)] for k in range(1, nx // 2)]),
            ("gy", [[i // 4 * 4 + (i + k) % 4 for i in range(ny)] for k in range(1, 4)]),
            ("gy", [[(i + 4 * k) % ny for i in range(ny)] for k in range(1, ny // 4)]),
        )
        for axis, moves in rounds:
            moved = [lax.ppermute(value, axis, list(enumerate(move))) for move in moves]
            for other in moved:
                value = value + other
        return value

    to_xp, to_xn, to_yp, to_yn = cut(level, stress)
    xlo, xhi = send(to_xn, 1, 0), send(to_xp, -1, 0)
    ylo, yhi = send(to_yn, 0, 1), send(to_yp, 0, -1)
    drift = inner_drift(level, velocity)
    adv, to_xp, to_xn, to_yp, to_yn = advect(tiles, level, xlo, xhi, ylo, yhi, velocity, drift)
    axlo, axhi = send(to_xn, 1, 0), send(to_xp, -1, 0)
    aylo, ayhi = send(to_yn, 0, 1), send(to_yp, 0, -1)
    row = lax.broadcasted_iota(jnp.int32, (1, 8, 1), 1)
    none = jnp.zeros((4, 2 * LANES), F32)

    def corners(rows, mark, y):
        faces = [jnp.where(row == mark, f[DEEP:, rows], f[:DEEP, rows]) for f in (axlo, axhi)]
        tail = jnp.concatenate((xlo[4::2, y], xhi[3:-1:2, y], none), axis=0)
        return jnp.concatenate(faces + [tail.reshape(2, 8, 2 * LANES)], axis=0)

    clo = send(corners(slice(-8, None), 0, CY - 1), 0, 1)
    chi = send(corners(slice(0, 8), 7, 0), 0, -1)
    cur, weight, part = sweeps(tiles, adv, (axlo, axhi, aylo, ayhi, clo, chi))
    return extend(
        total(part), cur, weight, stress, (xlo, xhi, ylo, yhi, clo, chi)
    )


def solution(mesh):
    in_specs = (
        P("gx", "gy", None),
        P(None, "gx", "gy", None),
        P(None, "gx", "gy", None),
        P("gx", "gy", None),
    )
    out_specs = (P("gx", "gy", None), P(None, "gx", "gy", None))
    return jax.shard_map(
        on_device, mesh=mesh, in_specs=in_specs, out_specs=out_specs, check_vma=False
    )
```

```python
import functools

import jax
import jax.numpy as jnp
from jax import lax
from jax.experimental import pallas as pl
from jax.experimental.pallas import tpu as pltpu
from jax.sharding import PartitionSpec as P

TILE = 16
SWEEPS = 5
EPSILON = 1e-06
TIME_STEP = 0.4
PSEUDO_STEP = 0.3

CX = 32
CY = 32
LANES = 128
DEEP = 7
ROWS = 64
OWN = 16
UNIT = 16
COMPS = 6
F32 = jnp.float32
DOUBLED = 2.0 * 1.4426950408889634
MIB = 1024 * 1024
ANY = pl.BlockSpec(memory_space=pl.ANY)
VMEM = pl.BlockSpec(memory_space=pltpu.VMEM)
SMEM = pl.BlockSpec(memory_space=pltpu.SMEM)


def half(h):
    return pl.ds(h * LANES, LANES)


def recip(x):
    return pl.reciprocal(x, approx=True)


def lane_shift(pair, k):
    lane = lax.broadcasted_iota(jnp.int32, pair[0].shape, pair[0].ndim - 1)
    turned = [pltpu.roll(p, (-k) % LANES, p.ndim - 1) for p in pair]
    edge = lane >= LANES - k if k > 0 else lane < -k
    return [jnp.where(edge, turned[1 - h], turned[h]) for h in range(2)]


def weno(d, positive):
    v = [jnp.where(positive, d[k], d[5 - k]) for k in range(5)]
    d1, d2, d3, d4 = (v[k + 1] - v[k] for k in range(4))
    u1, u2, u3 = d2 - d1, d3 - d2, d4 - d3
    g1 = d2 + d2 + u1
    g2 = d2 + d3
    g3 = u3 - (d3 + d3)
    scale = 13.0 / 3.0
    a1 = recip(4.0 * EPSILON + (scale * u1 * u1 + g1 * g1))
    a2 = recip(4.0 * EPSILON + (scale * u2 * u2 + g2 * g2))
    a3 = recip(4.0 * EPSILON + (scale * u3 * u3 + g3 * g3))
    a1 = a1 * a1
    a2 = 6.0 * (a2 * a2)
    a3 = 3.0 * (a3 * a3)
    top = a1 * (u1 - u2) + 0.5 * (a3 * (u2 - u3))
    mid = v[2] + (d3 + d3 + d2) * (1.0 / 6.0)
    return mid + top * (recip(a1 + a2 + a3) * (1.0 / 3.0))


def band_table(tiles_ref):
    shape = (8, LANES)
    row = lax.broadcasted_iota(jnp.int32, shape, 0)
    lane = lax.broadcasted_iota(jnp.int32, shape, 1)
    numbers = (row // 2) * 16 + (row % 2) * 8 + lane // TILE
    flags = jnp.zeros(shape, F32)
    for slot in range(tiles_ref.shape[-1]):
        flags = jnp.where(numbers == tiles_ref[0, 0, slot], 1.0, flags)
    return flags


def derivative(line, speed):
    return speed * weno([line[k + 1] - line[k] for k in range(6)], speed > 0)


def along_x(pad, x, h, at, size):
    return [pad[x + k, h, pl.ds(at, size), :] for k in range(-3, 4)]


def along_y(pad, x, h, at, size):
    return [pad[x, h, pl.ds(at + k, size), :] for k in range(-3, 4)]


def cut_kernel(level, stress, to_xp, to_xn, to_yp, to_yn, faces, x_sems, y_sems):
    copies = []
    for n, (out, at) in enumerate(((to_xp, 0), (to_xn, CX))):
        deep = lambda size: pl.ds(at and at - size, size)
        copies.append(pltpu.make_async_copy(level.at[deep(3)], out.at[pl.ds(0, 3)], x_sems.at[n, 0]))
        for c in range(COMPS):
            copies.append(
                pltpu.make_async_copy(
                    stress.at[c, deep(2)], out.at[pl.ds(3 + 2 * c, 2)], x_sems.at[n, 1 + c]
                )
            )
    for copy in copies:
        copy.start()
    sides = []
    for n, y in enumerate((0, CY - 8)):
        side = []
        for h in range(2):
            for m in range(1 + COMPS):
                src = stress.at[m - 1] if m else level
                side.append(
                    pltpu.make_async_copy(
                        src.at[:, pl.ds(y, 8), half(h)], faces.at[m, n, h], y_sems.at[m, n, h]
                    )
                )
        for copy in side:
            copy.start()
        sides.append(side)
    flat = faces.reshape(1 + COMPS, 2, 2, CX * 8, LANES)
    for n, out in enumerate((to_yp, to_yn)):
        for copy in sides[n]:
            copy.wait()
        for h in range(2):
            for m in range(1 + COMPS):
                depth = 2 if m else 3
                first = 1 + 2 * m if m else 0
                for k in range(depth):
                    row = k if n == 0 else 8 - depth + k
                    for x in range(0, CX, 8):
                        out[first + k, x : x + 8, half(h)] = flat[
                            m, n, h, pl.ds(8 * x + row, 8, stride=8), :
                        ]
    for copy in copies:
        copy.wait()


def cut(level, stress):
    message = jax.ShapeDtypeStruct((3 + 2 * COMPS, CX, 2 * LANES), F32)
    return pl.pallas_call(
        cut_kernel,
        out_shape=[message] * 4,
        in_specs=[ANY] * 2,
        out_specs=[VMEM] * 4,
        scratch_shapes=[
            pltpu.VMEM((1 + COMPS, 2, 2, CX, 8, LANES), F32),
            pltpu.SemaphoreType.DMA((2, 1 + COMPS)),
            pltpu.SemaphoreType.DMA((1 + COMPS, 2, 2)),
        ],
        compiler_params=pltpu.CompilerParams(vmem_limit_bytes=10 * MIB),
        name="cut",
    )(level, stress)


def inner_kernel(level, speed, drift, pad, sems):
    copies = [
        pltpu.make_async_copy(level.at[:, :, half(h)], pad.at[:, h], sems.at[h]) for h in range(2)
    ]
    for copy in copies:
        copy.start()
    for copy in copies:
        copy.wait()

    def plane(x, with_x):
        for unit in range(CY // UNIT):
            rows = pl.ds(unit * UNIT, UNIT)
            v = [[speed[d, x, rows, half(h)].astype(F32) for h in range(2)] for d in range(3)]
            for part in range(UNIT // 8):
                at = unit * UNIT + 8 * part
                cut = slice(8 * part, 8 * part + 8)
                center = [pad[x, h, pl.ds(at, 8), :] for h in range(2)]
                ups = [lane_shift(center, k) for k in (1, 2, 3)]
                downs = [lane_shift(center, -k) for k in (3, 2, 1)]
                for h in range(2):
                    line = [s[h] for s in downs] + [center[h]] + [s[h] for s in ups]
                    total = derivative(line, v[2][h][cut])
                    if with_x:
                        total = total + derivative(along_x(pad, x, h, at, 8), v[0][h][cut])
                    if 8 <= at < CY - 8:
                        total = total + derivative(along_y(pad, x, h, at, 8), v[1][h][cut])
                    drift[x, pl.ds(at, 8), half(h)] = total

    def inner(x, carry):
        plane(x, True)
        return carry

    def outer(x, carry):
        plane(x, False)
        plane(x + CX - 3, False)
        return carry

    lax.fori_loop(0, 3, outer, 0)
    lax.fori_loop(3, CX - 3, inner, 0, unroll=2)


def inner_drift(level, speed):
    return pl.pallas_call(
        inner_kernel,
        out_shape=jax.ShapeDtypeStruct(level.shape, F32),
        in_specs=[ANY, VMEM],
        out_specs=VMEM,
        scratch_shapes=[
            pltpu.VMEM((CX, 2, CY, LANES), F32),
            pltpu.SemaphoreType.DMA((2,)),
        ],
        compiler_params=pltpu.CompilerParams(vmem_limit_bytes=10 * MIB),
        cost_estimate=pl.CostEstimate(
            flops=180 * level.size, bytes_accessed=14 * level.size, transcendentals=9 * level.size
        ),
        name="inner_drift",
    )(level, speed)


def advect_kernel(
    tiles, level, xlo, xhi, ylo, yhi, speed, drift,
    adv, to_xp, to_xn, to_yp, to_yn, tail_p, tail_n,
    pad, table, faces, ends, sems, y_sems, end_sems,
):
    copies = []
    for h in range(2):
        for n, (src, at, size) in enumerate(((level, 3, CX), (xlo, 0, 3), (xhi, CX + 3, 3))):
            copies.append(
                pltpu.make_async_copy(
                    src.at[pl.ds(0, size), :, half(h)],
                    pad.at[pl.ds(at, size), h, pl.ds(8, CY), :],
                    sems.at[h, n],
                )
            )
    for n, src in enumerate((ylo, yhi)):
        copies.append(pltpu.make_async_copy(src.at[pl.ds(0, 3)], faces.at[n], y_sems.at[n]))
    for n, src in enumerate((xlo, xhi)):
        for m, y in enumerate((0, CY - 8)):
            copies.append(
                pltpu.make_async_copy(
                    src.at[pl.ds(3, 2 * COMPS), pl.ds(y, 8)], ends.at[n, m], end_sems.at[n, m]
                )
            )
    for copy in copies:
        copy.start()
    table[...] = band_table(tiles)
    for copy in copies:
        copy.wait()
    for m, (tail, row) in enumerate(((tail_p, 0), (tail_n, 7))):
        tail[...] = jnp.zeros(tail.shape, F32)
        for n in range(2):
            for c in range(COMPS):
                to = n * COMPS + c
                tail[to // 8, to % 8 : to % 8 + 1, :] = ends[n, m, 2 * c + 1 - n, row : row + 1, :]
    flat = pad.reshape((CX + 6) * 2 * 48, LANES)
    for n, row in enumerate((5, 8 + CY)):
        for h in range(2):
            for k in range(3):
                for x in range(0, CX, 8):
                    rows = pl.ds(((x + 3) * 2 + h) * 48 + row + k, 8, stride=96)
                    flat[rows, :] = faces[n, k, x : x + 8, half(h)]

    def plane(x, with_x):
        for unit in range(CY // UNIT):
            rows = pl.ds(unit * UNIT, UNIT)
            for h in range(2):
                vx = speed[0, x, rows, half(h)].astype(F32) if with_x else None
                vy = speed[1, x, rows, half(h)].astype(F32)
                for part in range(UNIT // 8):
                    at = unit * UNIT + 8 * part
                    cut = slice(8 * part, 8 * part + 8)
                    total = drift[x, pl.ds(at, 8), half(h)]
                    if with_x:
                        total = total + derivative(along_x(pad, x + 3, h, at + 8, 8), vx[cut])
                    if at in (0, CY - 8):
                        total = total + derivative(along_y(pad, x + 3, h, at + 8, 8), vy[cut])
                    adv[x, pl.ds(at, 8), half(h)] = (
                        pad[x + 3, h, pl.ds(at + 8, 8), :] - TIME_STEP * total
                    )

    def inner(x, carry):
        plane(x, False)
        return carry

    def outer(x, carry):
        plane(x, True)
        plane(x + CX - 3, True)
        return carry

    lax.fori_loop(0, 3, outer, 0)
    lax.fori_loop(3, CX - 3, inner, 0, unroll=2)
    low, high = CX - DEEP, CX
    to_xp[0:DEEP] = adv[0:DEEP]
    to_xn[0:DEEP] = adv[low:high]
    row8 = lax.broadcasted_iota(jnp.int32, (8, LANES), 0)
    for h in range(2):
        for j in range(2):
            rows = pl.ds(j * TILE, TILE)
            for i, face in ((0, to_xp), (1, to_xn)):
                r = i * 4 + j * 2 + h
                face[DEEP, rows, half(h)] = jnp.broadcast_to(table[r : r + 1, :], (TILE, LANES))
        for i in range(2):
            first = table[i * 4 + h : i * 4 + h + 1, :]
            last = table[i * 4 + 2 + h : i * 4 + 3 + h, :]
            for x in range(i * TILE, i * TILE + TILE):
                to_yp[x, :, half(h)] = jnp.where(row8 == 7, first, adv[x, 0:8, half(h)])
                to_yn[x, :, half(h)] = jnp.where(row8 == 0, last, adv[x, CY - 8 : CY, half(h)])


def advect(tiles, level, xlo, xhi, ylo, yhi, speed, drift):
    shape = lambda *s: jax.ShapeDtypeStruct(s, F32)
    z = 2 * LANES
    return pl.pallas_call(
        advect_kernel,
        out_shape=[shape(CX, CY, z)]
        + [shape(8, CY, z)] * 2
        + [shape(CX, 8, z)] * 2
        + [shape(2, 8, z)] * 2,
        in_specs=[SMEM, ANY, ANY, ANY, ANY, ANY, VMEM, VMEM],
        out_specs=[VMEM] * 7,
        scratch_shapes=[
            pltpu.VMEM((CX + 6, 2, 48, LANES), F32),
            pltpu.VMEM((8, LANES), F32),
            pltpu.VMEM((2, 3, CX, z), F32),
            pltpu.VMEM((2, 2, 2 * COMPS, 8, z), F32),
            pltpu.SemaphoreType.DMA((2, 3)),
            pltpu.SemaphoreType.DMA((2,)),
            pltpu.SemaphoreType.DMA((2, 2)),
        ],
        compiler_params=pltpu.CompilerParams(vmem_limit_bytes=12 * MIB),
        name="advect",
    )(tiles, level, xlo, xhi, ylo, yhi, speed, drift)


WIDE = CX + 2 * DEEP


def sweep_kernel(
    tiles, adv, xlo, xhi, ylo, yhi, clo, chi,
    cur_out, weight_out, part,
    first, second, factor, masks, table, sums, sems,
):
    copies = []
    for h in range(2):
        pieces = (
            (adv, DEEP, CX, OWN, CY),
            (xlo.at[pl.ds(0, DEEP)], 0, DEEP, OWN, CY),
            (xhi.at[pl.ds(0, DEEP)], DEEP + CX, DEEP, OWN, CY),
            (ylo, DEEP, CX, OWN - 8, 8),
            (yhi, DEEP, CX, OWN + CY, 8),
            (clo.at[pl.ds(0, DEEP)], 0, DEEP, OWN - 8, 8),
            (clo.at[pl.ds(DEEP, DEEP)], DEEP + CX, DEEP, OWN - 8, 8),
            (chi.at[pl.ds(0, DEEP)], 0, DEEP, OWN + CY, 8),
            (chi.at[pl.ds(DEEP, DEEP)], DEEP + CX, DEEP, OWN + CY, 8),
        )
        for n, (src, x, nx, y, ny) in enumerate(pieces):
            copies.append(
                pltpu.make_async_copy(
                    src.at[:, :, half(h)],
                    first.at[pl.ds(x, nx), h, pl.ds(y, ny), :],
                    sems.at[h, n],
                )
            )
        for n, src in enumerate((xlo, xhi)):
            copies.append(
                pltpu.make_async_copy(
                    src.at[pl.ds(DEEP, 1), :, half(h)], masks.at[pl.ds(n, 1), h], sems.at[h, 9 + n]
                )
            )
    for copy in copies:
        copy.start()
    table[...] = band_table(tiles)
    sums[...] = jnp.zeros(sums.shape, F32)
    for copy in copies:
        copy.wait()

    def prepare(x, bands, keep):
        for h in range(2):
            for group in range(-1, 5):
                rows = pl.ds(OWN + 8 * group, 8)
                value = first[x, h, rows, :]
                if group == -1:
                    band = jnp.broadcast_to(value[0:1], value.shape)
                elif group == 4:
                    band = jnp.broadcast_to(value[7:8], value.shape)
                else:
                    band = bands(group, h)
                square = value * value
                weight = band * recip(1.0 + square * (1.0 / 36.0))
                sign = value * lax.rsqrt(square + 1.0)
                factor[x, h, rows, :] = PSEUDO_STEP * sign * weight
                if keep:
                    weight_out[x - DEEP + 1, h, rows, :] = weight

    def halo_bands(n):
        return lambda group, h: masks[n, h, pl.ds(8 * group, 8), :]

    def own_bands(i):
        def bands(group, h):
            r = i * 4 + (group // 2) * 2 + h
            return jnp.broadcast_to(table[r : r + 1, :], (8, LANES))

        return bands

    def run(start, stop, bands, keep):
        def body(x, carry):
            prepare(x, bands, keep)
            return carry

        lax.fori_loop(start, stop, body, 0, unroll=2)

    run(1, DEEP - 1, halo_bands(0), False)
    prepare(DEEP - 1, halo_bands(0), True)
    run(DEEP, DEEP + TILE, own_bands(0), True)
    run(DEEP + TILE, DEEP + CX, own_bands(1), True)
    prepare(DEEP + CX, halo_bands(1), True)
    run(DEEP + CX + 1, WIDE - 1, halo_bands(1), False)

    def sweep_plane(src, x, dst, y, groups):
        start = OWN + CY // 2 - 4 * groups
        rows = [pl.ds(start + k, 8, stride=groups) for k in range(-1, groups + 1)]
        lines = [[src[x, h, r, :] for r in rows] for h in range(2)]
        for k in range(1, groups + 1):
            center = [lines[h][k] for h in range(2)]
            up, down = lane_shift(center, 1), lane_shift(center, -1)
            for h in range(2):
                c = center[h]
                step = factor[x, h, rows[k], :]
                positive = step > 0
                pairs = (
                    (src[x - 1, h, rows[k], :], src[x + 1, h, rows[k], :]),
                    (lines[h][k - 1], lines[h][k + 1]),
                    (down[h], up[h]),
                )
                total = None
                for l, r in pairs:
                    low = jnp.minimum(jnp.minimum(l, r), c)
                    high = jnp.maximum(jnp.maximum(l, r), c)
                    diff = c - jnp.where(positive, low, high)
                    total = diff * diff if total is None else total + diff * diff
                slope = total * lax.rsqrt(jnp.maximum(total, 1e-36))
                dst[y, h, rows[k], :] = c - step * (slope - 1.0)

    source, target = first, second
    for sweep in range(1, SWEEPS + 1):
        offset, dst = (0, target) if sweep < SWEEPS else (SWEEPS, cur_out)
        groups = 6 if DEEP - sweep > 4 else 5

        def body(x, carry, source=source, dst=dst, offset=offset, groups=groups):
            sweep_plane(source, x, dst, x - offset, groups)
            return carry

        lax.fori_loop(sweep, WIDE - sweep, body, 0, unroll=2)
        source, target = target, source

    def count(x, carry):
        for h in range(2):
            for unit in range(CY // UNIT):
                rows = pl.ds(OWN + unit * UNIT, UNIT)
                after = jnp.tanh(cur_out[x + 2, h, rows, :])
                before = jnp.tanh(adv[x, pl.ds(unit * UNIT, UNIT), half(h)])
                sums[0] += after - before
                sums[1] += 1.0 - after * after
        return carry

    lax.fori_loop(0, CX, count, 0, unroll=2)
    lane = lax.broadcasted_iota(jnp.int32, (1, LANES), 1)
    sums_row = jnp.where(lane < 64, jnp.sum(sums[0]), jnp.sum(sums[1]))
    part[...] = jnp.broadcast_to(sums_row, part.shape)


def sweeps(tiles, adv, halos, count):
    shape = lambda *s: jax.ShapeDtypeStruct(s, F32)
    return pl.pallas_call(
        sweep_kernel,
        out_shape=[shape(CX + 4, 2, ROWS, LANES), shape(CX + 2, 2, ROWS, LANES), shape(count, 1, LANES)],
        in_specs=[SMEM, VMEM] + [ANY] * 6,
        out_specs=[VMEM] * 3,
        scratch_shapes=[
            pltpu.VMEM((WIDE, 2, ROWS, LANES), F32),
            pltpu.VMEM((WIDE, 2, ROWS, LANES), F32),
            pltpu.VMEM((WIDE, 2, ROWS, LANES), F32),
            pltpu.VMEM((2, 2, CY, LANES), F32),
            pltpu.VMEM((8, LANES), F32),
            pltpu.VMEM((2, UNIT, LANES), F32),
            pltpu.SemaphoreType.DMA((2, 11)),
        ],
        compiler_params=pltpu.CompilerParams(vmem_limit_bytes=22 * MIB),
        name="sweeps",
    )(tiles, adv, *halos)


CHUNKS = ((0, 10), (10, 18), (18, 26), (26, 32))


def extend_kernel(
    parts, cur, weight, stress, xlo, xhi, ylo, yhi, clo, chi,
    level_out, stress_out,
    pad, ring, mix, stage, sems, x_sems, out_sems,
):
    def chunk(n):
        start, stop = CHUNKS[n]
        own = stress.at[:, pl.ds(start, stop - start)]
        copies = [
            pltpu.make_async_copy(
                own.at[:, :, :, half(h)],
                pad.at[:, pl.ds(start + 2, stop - start), h, pl.ds(OWN, CY), :],
                sems.at[n, h],
            )
            for h in range(2)
        ]
        for side, src in ((0, xlo), (3, xhi)):
            if n == side:
                at = 0 if n == 0 else CX + 2
                for h in range(2):
                    for c in range(COMPS):
                        copies.append(
                            pltpu.make_async_copy(
                                src.at[pl.ds(3 + 2 * c, 2), :, half(h)],
                                pad.at[c, pl.ds(at, 2), h, pl.ds(OWN, CY), :],
                                x_sems.at[side % 2, h, c],
                            )
                        )
        return copies

    chunks = [chunk(n) for n in range(len(CHUNKS))]
    for copies in chunks:
        for copy in copies:
            copy.start()
    sums = jnp.sum(parts[...], axis=0)
    shift = sums[:, 0:1] / sums[:, 64:65]
    flat = pad.reshape(COMPS, (CX + 4) * 2 * ROWS, LANES)
    for h in range(2):
        for c in range(COMPS):
            for face, row in ((ylo, OWN - 2), (yhi, OWN + CY)):
                for k in range(2):
                    for x in range(0, CX, 8):
                        at = ((x + 2) * 2 + h) * ROWS + row + k
                        flat[c, pl.ds(at, 8, stride=2 * ROWS), :] = face[
                            3 + 2 * c + k, x : x + 8, half(h)
                        ]
            for corner, row in ((clo, OWN - 1), (chi, OWN + CY)):
                for x, n in ((1, c), (CX + 2, COMPS + c)):
                    at = 2 * DEEP + n // 8
                    pad[c, x, h, row : row + 1, :] = corner[at, n % 8 : n % 8 + 1, half(h)]

    def blend(mixes, center, around):
        value = mixes[6] * center
        for n in range(6):
            value = value + mixes[n] * around[n]
        return value

    def row_groups(groups):
        start = OWN + CY // 2 - 4 * groups
        return [pl.ds(start + k, 8, stride=groups) for k in range(-1, groups + 1)]

    def face(here, there):
        grown = jnp.exp2(jnp.minimum(there - here, 125.5))
        factor = recip(1.0 + grown)
        return factor, grown * factor

    def neighbours(load, groups):
        rows = row_groups(groups)
        lines = [[load(0, h, r) for r in rows] for h in range(2)]
        for k in range(1, groups + 1):
            center = [lines[h][k] for h in range(2)]
            up, down = lane_shift(center, 1), lane_shift(center, -1)
            yield rows[k], center, [
                [
                    load(-1, h, rows[k]), load(1, h, rows[k]), lines[h][k - 1], lines[h][k + 1],
                    down[h], up[h],
                ]
                for h in range(2)
            ]

    def first_step(i, slot, groups=5):
        load = lambda dx, h, r: cur[i + 1 + dx, h, r, :] * DOUBLED
        comps = [
            neighbours(lambda dx, h, r, c=c: pad[c, i + 1 + dx, h, r, :], groups)
            for c in range(COMPS)
        ]
        rows_of = row_groups(groups)
        lines = [[load(0, h, r) for r in rows_of] for h in range(2)]
        below = [face(lines[h][1], lines[h][0])[0] for h in range(2)]
        for k in range(1, groups + 1):
            rows = rows_of[k]
            center = [lines[h][k] for h in range(2)]
            along_z = [face(c, n) for c, n in zip(center, lane_shift(center, 1))]
            back_z = lane_shift([back for _, back in along_z], -1)
            mixes = []
            for h in range(2):
                c = center[h]
                ahead, back = face(c, lines[h][k + 1])
                w = [
                    face(c, load(-1, h, rows))[0], face(c, load(1, h, rows))[0],
                    below[h], ahead, back_z[h], along_z[h][0],
                ]
                below[h] = back
                total = w[0] + w[1] + w[2] + w[3] + w[4] + w[5]
                gate = weight[i, h, rows, :] * 0.5 * (
                    1.0 + jnp.tanh(c * (2.0 / DOUBLED) - 2.0 * shift)
                )
                scaled = gate * recip(total)
                w = [scaled * n for n in w] + [1.0 - gate]
                mixes.append(w)
                for n in range(7):
                    mix[slot % 2, n, h, rows, :] = w[n]
            for comp in range(COMPS):
                _, center, around = next(comps[comp])
                for h in range(2):
                    ring[slot, comp, h, rows, :] = blend(mixes[h], center[h], around[h])

    def second_step(x, slot):
        slots = {dx: (slot + dx) % 4 for dx in (-1, 0, 1)}
        groups = CY // 8
        comps = [
            neighbours(lambda dx, h, r, c=c: ring[slots[dx], c, h, r, :], groups)
            for c in range(COMPS)
        ]
        for k in range(groups):
            rows = pl.ds(OWN + k, 8, stride=groups)
            mixes = [[mix[slot % 2, n, h, rows, :] for n in range(7)] for h in range(2)]
            for comp in range(COMPS):
                _, center, around = next(comps[comp])
                for h in range(2):
                    stage[comp, x, h, pl.ds(k, 8, stride=groups), :] = blend(
                        mixes[h], center[h], around[h]
                    )
        for h in range(2):
            level_out[x, :, half(h)] = cur[x + 2, h, OWN : OWN + CY, :] - shift

    outs = []
    for n in range(len(CHUNKS)):
        for copy in chunks[n]:
            copy.wait()
        if n == 0:
            first_step(0, 0, groups=4)
            first_step(1, 1)

        def body(group, carry):
            for k in range(4):
                i = group * 4 + k + 2
                first_step(i, (k + 2) % 4)
                second_step(i - 2, (k + 1) % 4)
            return carry

        lax.fori_loop(2 * n, 2 * n + 2, body, 0)
        planes = pl.ds(8 * n, 8)
        for h in range(2):
            copy = pltpu.make_async_copy(
                stage.at[:, planes, h], stress_out.at[:, planes, :, half(h)], out_sems.at[n, h]
            )
            copy.start()
            outs.append(copy)
    for copy in outs:
        copy.wait()


def extend(parts, cur, weight, stress, halos):
    shape = lambda *s: jax.ShapeDtypeStruct(s, F32)
    z = 2 * LANES
    return pl.pallas_call(
        extend_kernel,
        out_shape=[shape(CX, CY, z), shape(COMPS, CX, CY, z)],
        in_specs=[VMEM, VMEM, VMEM, ANY, ANY, ANY, VMEM, VMEM, VMEM, VMEM],
        out_specs=[VMEM, ANY],
        scratch_shapes=[
            pltpu.VMEM((COMPS, CX + 4, 2, ROWS, LANES), F32),
            pltpu.VMEM((4, COMPS, 2, ROWS, LANES), F32),
            pltpu.VMEM((2, 7, 2, ROWS, LANES), F32),
            pltpu.VMEM((COMPS, CX, 2, CY, LANES), F32),
            pltpu.SemaphoreType.DMA((4, 2)),
            pltpu.SemaphoreType.DMA((2, 2, COMPS)),
            pltpu.SemaphoreType.DMA((4, 2)),
        ],
        compiler_params=pltpu.CompilerParams(vmem_limit_bytes=36 * MIB),
        name="extend",
    )(parts, cur, weight, stress, *halos)


def on_device(level, velocity, stress, tiles):
    nx, ny = lax.axis_size("gx"), lax.axis_size("gy")

    def send(value, dx, dy):
        if dy == 0:
            return lax.ppermute(value, "gx", [(i, (i + dx) % nx) for i in range(nx)])
        if dx == 0:
            return lax.ppermute(value, "gy", [(i, (i + dy) % ny) for i in range(ny)])
        pairs = [
            (i * ny + j, (i + dx) % nx * ny + (j + dy) % ny) for i in range(nx) for j in range(ny)
        ]
        return lax.ppermute(value, ("gx", "gy"), pairs)

    to_xp, to_xn, to_yp, to_yn = cut(level, stress)
    xlo, xhi = send(to_xn, 1, 0), send(to_xp, -1, 0)
    ylo, yhi = send(to_yn, 0, 1), send(to_yp, 0, -1)
    drift = inner_drift(level, velocity)
    adv, to_xp, to_xn, to_yp, to_yn, tail_p, tail_n = advect(
        tiles, level, xlo, xhi, ylo, yhi, velocity, drift
    )
    axlo, axhi = send(to_xn, 1, 0), send(to_xp, -1, 0)
    aylo, ayhi = send(to_yn, 0, 1), send(to_yp, 0, -1)
    row = lax.broadcasted_iota(jnp.int32, (1, 8, 1), 1)

    def corners(rows, mark, tail):
        faces = [jnp.where(row == mark, f[DEEP:, rows], f[:DEEP, rows]) for f in (axlo, axhi)]
        return jnp.concatenate(faces + [tail], axis=0)

    clo = send(corners(slice(-8, None), 0, tail_n), 0, 1)
    chi = send(corners(slice(0, 8), 7, tail_p), 0, -1)
    cur, weight, part = sweeps(tiles, adv, (axlo, axhi, aylo, ayhi, clo, chi), nx * ny)
    parts = lax.all_to_all(part, ("gx", "gy"), 0, 0, tiled=True)
    return extend(parts, cur, weight, stress, (xlo, xhi, ylo, yhi, clo, chi))


def solution(mesh):
    in_specs = (
        P("gx", "gy", None),
        P(None, "gx", "gy", None),
        P(None, "gx", "gy", None),
        P("gx", "gy", None),
    )
    out_specs = (P("gx", "gy", None), P(None, "gx", "gy", None))
    return jax.shard_map(
        on_device, mesh=mesh, in_specs=in_specs, out_specs=out_specs, check_vma=False
    )
```

```python
import functools

import jax
import jax.numpy as jnp
from jax import lax
from jax.experimental import pallas as pl
from jax.experimental.pallas import tpu as pltpu
from jax.sharding import PartitionSpec as P

TILE = 16
SWEEPS = 5
EPSILON = 1e-06
TIME_STEP = 0.4
PSEUDO_STEP = 0.3

CX = 32
CY = 32
LANES = 128
DEEP = 7
ROWS = 64
OWN = 16
UNIT = 16
COMPS = 6
F32 = jnp.float32
DOUBLED = 2.0 * 1.4426950408889634
MIB = 1024 * 1024
ANY = pl.BlockSpec(memory_space=pl.ANY)
VMEM = pl.BlockSpec(memory_space=pltpu.VMEM)
SMEM = pl.BlockSpec(memory_space=pltpu.SMEM)


def half(h):
    return pl.ds(h * LANES, LANES)


def recip(x):
    return pl.reciprocal(x, approx=True)


def lane_shift(pair, k):
    lane = lax.broadcasted_iota(jnp.int32, pair[0].shape, pair[0].ndim - 1)
    turned = [pltpu.roll(p, (-k) % LANES, p.ndim - 1) for p in pair]
    edge = lane >= LANES - k if k > 0 else lane < -k
    return [jnp.where(edge, turned[1 - h], turned[h]) for h in range(2)]


def weno(d, positive):
    v = [jnp.where(positive, d[k], d[5 - k]) for k in range(5)]
    d1, d2, d3, d4 = (v[k + 1] - v[k] for k in range(4))
    u1, u2, u3 = d2 - d1, d3 - d2, d4 - d3
    g1 = d2 + d2 + u1
    g2 = d2 + d3
    g3 = u3 - (d3 + d3)
    scale = 13.0 / 3.0
    a1 = recip(4.0 * EPSILON + (scale * u1 * u1 + g1 * g1))
    a2 = recip(4.0 * EPSILON + (scale * u2 * u2 + g2 * g2))
    a3 = recip(4.0 * EPSILON + (scale * u3 * u3 + g3 * g3))
    a1 = a1 * a1
    a2 = 6.0 * (a2 * a2)
    a3 = 3.0 * (a3 * a3)
    top = a1 * (u1 - u2) + 0.5 * (a3 * (u2 - u3))
    mid = v[2] + (d3 + d3 + d2) * (1.0 / 6.0)
    return mid + top * (recip(a1 + a2 + a3) * (1.0 / 3.0))


def band_table(tiles_ref):
    shape = (8, LANES)
    row = lax.broadcasted_iota(jnp.int32, shape, 0)
    lane = lax.broadcasted_iota(jnp.int32, shape, 1)
    numbers = (row // 2) * 16 + (row % 2) * 8 + lane // TILE
    flags = jnp.zeros(shape, F32)
    for slot in range(tiles_ref.shape[-1]):
        flags = jnp.where(numbers == tiles_ref[0, 0, slot], 1.0, flags)
    return flags


def derivative(line, speed):
    return speed * weno([line[k + 1] - line[k] for k in range(6)], speed > 0)


def along_x(pad, x, h, at, size):
    return [pad[x + k, h, pl.ds(at, size), :] for k in range(-3, 4)]


def along_y(pad, x, h, at, size):
    return [pad[x, h, pl.ds(at + k, size), :] for k in range(-3, 4)]


def cut_kernel(
    level, stress, to_xp, to_xn, to_yp, to_yn, to_syp, to_syn, faces, x_sems, y_sems
):
    copies = []
    for n, (out, at) in enumerate(((to_xp, 0), (to_xn, CX))):
        deep = lambda size: pl.ds(at and at - size, size)
        copies.append(pltpu.make_async_copy(level.at[deep(3)], out.at[pl.ds(0, 3)], x_sems.at[n, 0]))
        for c in range(COMPS):
            copies.append(
                pltpu.make_async_copy(
                    stress.at[c, deep(2)], out.at[pl.ds(3 + 2 * c, 2)], x_sems.at[n, 1 + c]
                )
            )
    for copy in copies:
        copy.start()
    sides = []
    for n, y in enumerate((0, CY - 8)):
        side = []
        for h in range(2):
            for m in range(1 + COMPS):
                src = stress.at[m - 1] if m else level
                side.append(
                    pltpu.make_async_copy(
                        src.at[:, pl.ds(y, 8), half(h)], faces.at[m, n, h], y_sems.at[m, n, h]
                    )
                )
        for copy in side:
            copy.start()
        sides.append(side)
    flat = faces.reshape(1 + COMPS, 2, 2, CX * 8, LANES)
    for n, outs in enumerate(((to_yp, to_syp), (to_yn, to_syn))):
        for copy in sides[n]:
            copy.wait()
        for h in range(2):
            for m in range(1 + COMPS):
                depth = 2 if m else 3
                out = outs[min(m, 1)]
                first = 2 * m - 2 if m else 0
                for k in range(depth):
                    row = k if n == 0 else 8 - depth + k
                    for x in range(0, CX, 8):
                        out[first + k, x : x + 8, half(h)] = flat[
                            m, n, h, pl.ds(8 * x + row, 8, stride=8), :
                        ]
    for copy in copies:
        copy.wait()


def cut(level, stress):
    message = lambda planes: jax.ShapeDtypeStruct((planes, CX, 2 * LANES), F32)
    return pl.pallas_call(
        cut_kernel,
        out_shape=[message(3 + 2 * COMPS)] * 2 + [message(3)] * 2 + [message(2 * COMPS)] * 2,
        in_specs=[ANY] * 2,
        out_specs=[VMEM] * 6,
        scratch_shapes=[
            pltpu.VMEM((1 + COMPS, 2, 2, CX, 8, LANES), F32),
            pltpu.SemaphoreType.DMA((2, 1 + COMPS)),
            pltpu.SemaphoreType.DMA((1 + COMPS, 2, 2)),
        ],
        compiler_params=pltpu.CompilerParams(vmem_limit_bytes=57 * MIB),
        name="cut",
    )(level, stress)


def inner_kernel(level, speed, drift, pad, sems):
    copies = [
        pltpu.make_async_copy(level.at[:, :, half(h)], pad.at[:, h], sems.at[h]) for h in range(2)
    ]
    for copy in copies:
        copy.start()
    for copy in copies:
        copy.wait()

    def plane(x, with_x):
        for unit in range(CY // UNIT):
            rows = pl.ds(unit * UNIT, UNIT)
            v = [[speed[d, x, rows, half(h)].astype(F32) for h in range(2)] for d in range(3)]
            for part in range(UNIT // 8):
                at = unit * UNIT + 8 * part
                cut = slice(8 * part, 8 * part + 8)
                center = [pad[x, h, pl.ds(at, 8), :] for h in range(2)]
                ups = [lane_shift(center, k) for k in (1, 2, 3)]
                downs = [lane_shift(center, -k) for k in (3, 2, 1)]
                for h in range(2):
                    line = [s[h] for s in downs] + [center[h]] + [s[h] for s in ups]
                    total = derivative(line, v[2][h][cut])
                    if with_x:
                        total = total + derivative(along_x(pad, x, h, at, 8), v[0][h][cut])
                    if 8 <= at < CY - 8:
                        total = total + derivative(along_y(pad, x, h, at, 8), v[1][h][cut])
                    drift[x, pl.ds(at, 8), half(h)] = total

    def inner(x, carry):
        plane(x, True)
        return carry

    def outer(x, carry):
        plane(x, False)
        plane(x + CX - 3, False)
        return carry

    lax.fori_loop(0, 3, outer, 0)
    lax.fori_loop(3, CX - 3, inner, 0, unroll=2)


def inner_drift(level, speed):
    return pl.pallas_call(
        inner_kernel,
        out_shape=jax.ShapeDtypeStruct(level.shape, F32),
        in_specs=[ANY, VMEM],
        out_specs=VMEM,
        scratch_shapes=[
            pltpu.VMEM((CX, 2, CY, LANES), F32),
            pltpu.SemaphoreType.DMA((2,)),
        ],
        compiler_params=pltpu.CompilerParams(vmem_limit_bytes=10 * MIB),
        cost_estimate=pl.CostEstimate(
            flops=180 * level.size, bytes_accessed=14 * level.size, transcendentals=9 * level.size
        ),
        name="inner_drift",
    )(level, speed)


def advect_kernel(
    tiles, level, xlo, xhi, ylo, yhi, speed, drift,
    adv, to_xp, to_xn, to_yp, to_yn, tail_p, tail_n,
    pad, table, faces, ends, sems, y_sems, end_sems,
):
    copies = []
    for h in range(2):
        for n, (src, at, size) in enumerate(((level, 3, CX), (xlo, 0, 3), (xhi, CX + 3, 3))):
            copies.append(
                pltpu.make_async_copy(
                    src.at[pl.ds(0, size), :, half(h)],
                    pad.at[pl.ds(at, size), h, pl.ds(8, CY), :],
                    sems.at[h, n],
                )
            )
    for n, src in enumerate((ylo, yhi)):
        copies.append(pltpu.make_async_copy(src, faces.at[n], y_sems.at[n]))
    for n, src in enumerate((xlo, xhi)):
        for m, y in enumerate((0, CY - 8)):
            copies.append(
                pltpu.make_async_copy(
                    src.at[pl.ds(3, 2 * COMPS), pl.ds(y, 8)], ends.at[n, m], end_sems.at[n, m]
                )
            )
    for copy in copies:
        copy.start()
    table[...] = band_table(tiles)
    for copy in copies:
        copy.wait()
    for m, (tail, row) in enumerate(((tail_p, 0), (tail_n, 7))):
        tail[...] = jnp.zeros(tail.shape, F32)
        for n in range(2):
            for c in range(COMPS):
                to = n * COMPS + c
                tail[to // 8, to % 8 : to % 8 + 1, :] = ends[n, m, 2 * c + 1 - n, row : row + 1, :]
    flat = pad.reshape((CX + 6) * 2 * 48, LANES)
    for n, row in enumerate((5, 8 + CY)):
        for h in range(2):
            for k in range(3):
                for x in range(0, CX, 8):
                    rows = pl.ds(((x + 3) * 2 + h) * 48 + row + k, 8, stride=96)
                    flat[rows, :] = faces[n, k, x : x + 8, half(h)]

    def plane(x, with_x):
        for unit in range(CY // UNIT):
            rows = pl.ds(unit * UNIT, UNIT)
            for h in range(2):
                vx = speed[0, x, rows, half(h)].astype(F32) if with_x else None
                vy = speed[1, x, rows, half(h)].astype(F32)
                for part in range(UNIT // 8):
                    at = unit * UNIT + 8 * part
                    cut = slice(8 * part, 8 * part + 8)
                    total = drift[x, pl.ds(at, 8), half(h)]
                    if with_x:
                        total = total + derivative(along_x(pad, x + 3, h, at + 8, 8), vx[cut])
                    if at in (0, CY - 8):
                        total = total + derivative(along_y(pad, x + 3, h, at + 8, 8), vy[cut])
                    adv[x, pl.ds(at, 8), half(h)] = (
                        pad[x + 3, h, pl.ds(at + 8, 8), :] - TIME_STEP * total
                    )

    def inner(x, carry):
        plane(x, False)
        return carry

    def outer(x, carry):
        plane(x, True)
        plane(x + CX - 3, True)
        return carry

    lax.fori_loop(0, 3, outer, 0)
    lax.fori_loop(3, CX - 3, inner, 0, unroll=2)
    low, high = CX - DEEP, CX
    to_xp[0:DEEP] = adv[0:DEEP]
    to_xn[0:DEEP] = adv[low:high]
    row8 = lax.broadcasted_iota(jnp.int32, (8, LANES), 0)
    for h in range(2):
        for j in range(2):
            rows = pl.ds(j * TILE, TILE)
            for i, face in ((0, to_xp), (1, to_xn)):
                r = i * 4 + j * 2 + h
                face[DEEP, rows, half(h)] = jnp.broadcast_to(table[r : r + 1, :], (TILE, LANES))
        for i in range(2):
            first = table[i * 4 + h : i * 4 + h + 1, :]
            last = table[i * 4 + 2 + h : i * 4 + 3 + h, :]
            for x in range(i * TILE, i * TILE + TILE):
                to_yp[x, :, half(h)] = jnp.where(row8 == 7, first, adv[x, 0:8, half(h)])
                to_yn[x, :, half(h)] = jnp.where(row8 == 0, last, adv[x, CY - 8 : CY, half(h)])


def advect(tiles, level, xlo, xhi, ylo, yhi, speed, drift):
    shape = lambda *s: jax.ShapeDtypeStruct(s, F32)
    z = 2 * LANES
    return pl.pallas_call(
        advect_kernel,
        out_shape=[shape(CX, CY, z)]
        + [shape(8, CY, z)] * 2
        + [shape(CX, 8, z)] * 2
        + [shape(2, 8, z)] * 2,
        in_specs=[SMEM, ANY, ANY, ANY, ANY, ANY, VMEM, VMEM],
        out_specs=[VMEM] * 7,
        scratch_shapes=[
            pltpu.VMEM((CX + 6, 2, 48, LANES), F32),
            pltpu.VMEM((8, LANES), F32),
            pltpu.VMEM((2, 3, CX, z), F32),
            pltpu.VMEM((2, 2, 2 * COMPS, 8, z), F32),
            pltpu.SemaphoreType.DMA((2, 3)),
            pltpu.SemaphoreType.DMA((2,)),
            pltpu.SemaphoreType.DMA((2, 2)),
        ],
        compiler_params=pltpu.CompilerParams(vmem_limit_bytes=12 * MIB),
        name="advect",
    )(tiles, level, xlo, xhi, ylo, yhi, speed, drift)


WIDE = CX + 2 * DEEP


def sweep_kernel(
    tiles, adv, xlo, xhi, ylo, yhi, clo, chi,
    cur_out, weight_out, part,
    first, second, factor, masks, table, sums, sems,
):
    copies = []
    for h in range(2):
        pieces = (
            (adv, DEEP, CX, OWN, CY),
            (xlo.at[pl.ds(0, DEEP)], 0, DEEP, OWN, CY),
            (xhi.at[pl.ds(0, DEEP)], DEEP + CX, DEEP, OWN, CY),
            (ylo, DEEP, CX, OWN - 8, 8),
            (yhi, DEEP, CX, OWN + CY, 8),
            (clo.at[pl.ds(0, DEEP)], 0, DEEP, OWN - 8, 8),
            (clo.at[pl.ds(DEEP, DEEP)], DEEP + CX, DEEP, OWN - 8, 8),
            (chi.at[pl.ds(0, DEEP)], 0, DEEP, OWN + CY, 8),
            (chi.at[pl.ds(DEEP, DEEP)], DEEP + CX, DEEP, OWN + CY, 8),
        )
        for n, (src, x, nx, y, ny) in enumerate(pieces):
            copies.append(
                pltpu.make_async_copy(
                    src.at[:, :, half(h)],
                    first.at[pl.ds(x, nx), h, pl.ds(y, ny), :],
                    sems.at[h, n],
                )
            )
        for n, src in enumerate((xlo, xhi)):
            copies.append(
                pltpu.make_async_copy(
                    src.at[pl.ds(DEEP, 1), :, half(h)], masks.at[pl.ds(n, 1), h], sems.at[h, 9 + n]
                )
            )
    for copy in copies:
        copy.start()
    table[...] = band_table(tiles)
    sums[...] = jnp.zeros(sums.shape, F32)
    for copy in copies:
        copy.wait()

    def prepare(x, bands, keep):
        for h in range(2):
            for group in range(-1, 5):
                rows = pl.ds(OWN + 8 * group, 8)
                value = first[x, h, rows, :]
                if group == -1:
                    band = jnp.broadcast_to(value[0:1], value.shape)
                elif group == 4:
                    band = jnp.broadcast_to(value[7:8], value.shape)
                else:
                    band = bands(group, h)
                square = value * value
                weight = band * recip(1.0 + square * (1.0 / 36.0))
                sign = value * lax.rsqrt(square + 1.0)
                factor[x, h, rows, :] = PSEUDO_STEP * sign * weight
                if keep:
                    weight_out[x - DEEP + 1, h, rows, :] = weight

    def halo_bands(n):
        return lambda group, h: masks[n, h, pl.ds(8 * group, 8), :]

    def own_bands(i):
        def bands(group, h):
            r = i * 4 + (group // 2) * 2 + h
            return jnp.broadcast_to(table[r : r + 1, :], (8, LANES))

        return bands

    def run(start, stop, bands, keep):
        def body(x, carry):
            prepare(x, bands, keep)
            return carry

        lax.fori_loop(start, stop, body, 0, unroll=2)

    run(1, DEEP - 1, halo_bands(0), False)
    prepare(DEEP - 1, halo_bands(0), True)
    run(DEEP, DEEP + TILE, own_bands(0), True)
    run(DEEP + TILE, DEEP + CX, own_bands(1), True)
    prepare(DEEP + CX, halo_bands(1), True)
    run(DEEP + CX + 1, WIDE - 1, halo_bands(1), False)

    def sweep_plane(src, x, dst, y, groups):
        start = OWN + CY // 2 - 4 * groups
        rows = [pl.ds(start + k, 8, stride=groups) for k in range(-1, groups + 1)]
        lines = [[src[x, h, r, :] for r in rows] for h in range(2)]
        for k in range(1, groups + 1):
            center = [lines[h][k] for h in range(2)]
            up, down = lane_shift(center, 1), lane_shift(center, -1)
            for h in range(2):
                c = center[h]
                step = factor[x, h, rows[k], :]
                positive = step > 0
                pairs = (
                    (src[x - 1, h, rows[k], :], src[x + 1, h, rows[k], :]),
                    (lines[h][k - 1], lines[h][k + 1]),
                    (down[h], up[h]),
                )
                total = None
                for l, r in pairs:
                    low = jnp.minimum(jnp.minimum(l, r), c)
                    high = jnp.maximum(jnp.maximum(l, r), c)
                    diff = c - jnp.where(positive, low, high)
                    total = diff * diff if total is None else total + diff * diff
                slope = total * lax.rsqrt(jnp.maximum(total, 1e-36))
                dst[y, h, rows[k], :] = c - step * (slope - 1.0)

    source, target = first, second
    for sweep in range(1, SWEEPS + 1):
        offset, dst = (0, target) if sweep < SWEEPS else (SWEEPS, cur_out)
        groups = 6 if DEEP - sweep > 4 else 5

        def body(x, carry, source=source, dst=dst, offset=offset, groups=groups):
            sweep_plane(source, x, dst, x - offset, groups)
            return carry

        lax.fori_loop(sweep, WIDE - sweep, body, 0, unroll=2)
        source, target = target, source

    def count(x, carry):
        for h in range(2):
            for unit in range(CY // UNIT):
                rows = pl.ds(OWN + unit * UNIT, UNIT)
                after = jnp.tanh(cur_out[x + 2, h, rows, :])
                before = jnp.tanh(adv[x, pl.ds(unit * UNIT, UNIT), half(h)])
                sums[0] += after - before
                sums[1] += 1.0 - after * after
        return carry

    lax.fori_loop(0, CX, count, 0, unroll=2)
    lane = lax.broadcasted_iota(jnp.int32, (1, LANES), 1)
    sums_row = jnp.where(lane < 64, jnp.sum(sums[0]), jnp.sum(sums[1]))
    part[...] = jnp.broadcast_to(sums_row, part.shape)


def sweeps(tiles, adv, halos, count):
    shape = lambda *s: jax.ShapeDtypeStruct(s, F32)
    return pl.pallas_call(
        sweep_kernel,
        out_shape=[shape(CX + 4, 2, ROWS, LANES), shape(CX + 2, 2, ROWS, LANES), shape(count, 1, LANES)],
        in_specs=[SMEM, VMEM] + [ANY] * 6,
        out_specs=[VMEM] * 3,
        scratch_shapes=[
            pltpu.VMEM((WIDE, 2, ROWS, LANES), F32),
            pltpu.VMEM((WIDE, 2, ROWS, LANES), F32),
            pltpu.VMEM((WIDE, 2, ROWS, LANES), F32),
            pltpu.VMEM((2, 2, CY, LANES), F32),
            pltpu.VMEM((8, LANES), F32),
            pltpu.VMEM((2, UNIT, LANES), F32),
            pltpu.SemaphoreType.DMA((2, 11)),
        ],
        compiler_params=pltpu.CompilerParams(vmem_limit_bytes=22 * MIB),
        name="sweeps",
    )(tiles, adv, *halos)


CHUNKS = ((0, 10), (10, 18), (18, 26), (26, 32))


def extend_kernel(
    parts, cur, weight, stress, xlo, xhi, ylo, yhi, clo, chi,
    level_out, stress_out,
    pad, ring, mix, stage, sems, x_sems, out_sems,
):
    def chunk(n):
        start, stop = CHUNKS[n]
        own = stress.at[:, pl.ds(start, stop - start)]
        copies = [
            pltpu.make_async_copy(
                own.at[:, :, :, half(h)],
                pad.at[:, pl.ds(start + 2, stop - start), h, pl.ds(OWN, CY), :],
                sems.at[n, h],
            )
            for h in range(2)
        ]
        for side, src in ((0, xlo), (3, xhi)):
            if n == side:
                at = 0 if n == 0 else CX + 2
                for h in range(2):
                    for c in range(COMPS):
                        copies.append(
                            pltpu.make_async_copy(
                                src.at[pl.ds(3 + 2 * c, 2), :, half(h)],
                                pad.at[c, pl.ds(at, 2), h, pl.ds(OWN, CY), :],
                                x_sems.at[side % 2, h, c],
                            )
                        )
        return copies

    chunks = [chunk(n) for n in range(len(CHUNKS))]
    for copies in chunks:
        for copy in copies:
            copy.start()
    sums = jnp.sum(parts[...], axis=0)
    shift = sums[:, 0:1] / sums[:, 64:65]
    flat = pad.reshape(COMPS, (CX + 4) * 2 * ROWS, LANES)
    for h in range(2):
        for c in range(COMPS):
            for face, row in ((ylo, OWN - 2), (yhi, OWN + CY)):
                for k in range(2):
                    for x in range(0, CX, 8):
                        at = ((x + 2) * 2 + h) * ROWS + row + k
                        flat[c, pl.ds(at, 8, stride=2 * ROWS), :] = face[
                            2 * c + k, x : x + 8, half(h)
                        ]
            for corner, row in ((clo, OWN - 1), (chi, OWN + CY)):
                for x, n in ((1, c), (CX + 2, COMPS + c)):
                    at = 2 * DEEP + n // 8
                    pad[c, x, h, row : row + 1, :] = corner[at, n % 8 : n % 8 + 1, half(h)]

    def blend(mixes, center, around):
        value = mixes[6] * center
        for n in range(6):
            value = value + mixes[n] * around[n]
        return value

    def row_groups(groups):
        start = OWN + CY // 2 - 4 * groups
        return [pl.ds(start + k, 8, stride=groups) for k in range(-1, groups + 1)]

    def face(here, there):
        grown = jnp.exp2(jnp.minimum(there - here, 125.5))
        factor = recip(1.0 + grown)
        return factor, grown * factor

    def neighbours(load, groups):
        rows = row_groups(groups)
        lines = [[load(0, h, r) for r in rows] for h in range(2)]
        for k in range(1, groups + 1):
            center = [lines[h][k] for h in range(2)]
            up, down = lane_shift(center, 1), lane_shift(center, -1)
            yield rows[k], center, [
                [
                    load(-1, h, rows[k]), load(1, h, rows[k]), lines[h][k - 1], lines[h][k + 1],
                    down[h], up[h],
                ]
                for h in range(2)
            ]

    def first_step(i, slot, groups=5):
        load = lambda dx, h, r: cur[i + 1 + dx, h, r, :] * DOUBLED
        comps = [
            neighbours(lambda dx, h, r, c=c: pad[c, i + 1 + dx, h, r, :], groups)
            for c in range(COMPS)
        ]
        rows_of = row_groups(groups)
        lines = [[load(0, h, r) for r in rows_of] for h in range(2)]
        below = [face(lines[h][1], lines[h][0])[0] for h in range(2)]
        for k in range(1, groups + 1):
            rows = rows_of[k]
            center = [lines[h][k] for h in range(2)]
            along_z = [face(c, n) for c, n in zip(center, lane_shift(center, 1))]
            back_z = lane_shift([back for _, back in along_z], -1)
            mixes = []
            for h in range(2):
                c = center[h]
                ahead, back = face(c, lines[h][k + 1])
                w = [
                    face(c, load(-1, h, rows))[0], face(c, load(1, h, rows))[0],
                    below[h], ahead, back_z[h], along_z[h][0],
                ]
                below[h] = back
                total = w[0] + w[1] + w[2] + w[3] + w[4] + w[5]
                gate = weight[i, h, rows, :] * 0.5 * (
                    1.0 + jnp.tanh(c * (2.0 / DOUBLED) - 2.0 * shift)
                )
                scaled = gate * recip(total)
                w = [scaled * n for n in w] + [1.0 - gate]
                mixes.append(w)
                for n in range(7):
                    mix[slot % 2, n, h, rows, :] = w[n]
            for comp in range(COMPS):
                _, center, around = next(comps[comp])
                for h in range(2):
                    ring[slot, comp, h, rows, :] = blend(mixes[h], center[h], around[h])

    def second_step(x, slot):
        slots = {dx: (slot + dx) % 4 for dx in (-1, 0, 1)}
        groups = CY // 8
        comps = [
            neighbours(lambda dx, h, r, c=c: ring[slots[dx], c, h, r, :], groups)
            for c in range(COMPS)
        ]
        for k in range(groups):
            rows = pl.ds(OWN + k, 8, stride=groups)
            mixes = [[mix[slot % 2, n, h, rows, :] for n in range(7)] for h in range(2)]
            for comp in range(COMPS):
                _, center, around = next(comps[comp])
                for h in range(2):
                    stage[comp, x, h, pl.ds(k, 8, stride=groups), :] = blend(
                        mixes[h], center[h], around[h]
                    )
        for h in range(2):
            level_out[x, :, half(h)] = cur[x + 2, h, OWN : OWN + CY, :] - shift

    outs = []
    for n in range(len(CHUNKS)):
        for copy in chunks[n]:
            copy.wait()
        if n == 0:
            first_step(0, 0, groups=4)
            first_step(1, 1)

        def body(group, carry):
            for k in range(4):
                i = group * 4 + k + 2
                first_step(i, (k + 2) % 4)
                second_step(i - 2, (k + 1) % 4)
            return carry

        lax.fori_loop(2 * n, 2 * n + 2, body, 0)
        planes = pl.ds(8 * n, 8)
        for h in range(2):
            copy = pltpu.make_async_copy(
                stage.at[:, planes, h], stress_out.at[:, planes, :, half(h)], out_sems.at[n, h]
            )
            copy.start()
            outs.append(copy)
    for copy in outs:
        copy.wait()


def extend(parts, cur, weight, stress, halos):
    shape = lambda *s: jax.ShapeDtypeStruct(s, F32)
    z = 2 * LANES
    return pl.pallas_call(
        extend_kernel,
        out_shape=[shape(CX, CY, z), shape(COMPS, CX, CY, z)],
        in_specs=[VMEM, VMEM, VMEM, ANY, ANY, ANY, VMEM, VMEM, VMEM, VMEM],
        out_specs=[VMEM, ANY],
        scratch_shapes=[
            pltpu.VMEM((COMPS, CX + 4, 2, ROWS, LANES), F32),
            pltpu.VMEM((4, COMPS, 2, ROWS, LANES), F32),
            pltpu.VMEM((2, 7, 2, ROWS, LANES), F32),
            pltpu.VMEM((COMPS, CX, 2, CY, LANES), F32),
            pltpu.SemaphoreType.DMA((4, 2)),
            pltpu.SemaphoreType.DMA((2, 2, COMPS)),
            pltpu.SemaphoreType.DMA((4, 2)),
        ],
        compiler_params=pltpu.CompilerParams(vmem_limit_bytes=46 * MIB),
        name="extend",
    )(parts, cur, weight, stress, *halos)


def on_device(level, velocity, stress, tiles):
    nx, ny = lax.axis_size("gx"), lax.axis_size("gy")

    def send(value, dx, dy):
        if dy == 0:
            return lax.ppermute(value, "gx", [(i, (i + dx) % nx) for i in range(nx)])
        if dx == 0:
            return lax.ppermute(value, "gy", [(i, (i + dy) % ny) for i in range(ny)])
        pairs = [
            (i * ny + j, (i + dx) % nx * ny + (j + dy) % ny) for i in range(nx) for j in range(ny)
        ]
        return lax.ppermute(value, ("gx", "gy"), pairs)

    to_xp, to_xn, to_yp, to_yn, to_syp, to_syn = cut(level, stress)
    xlo, xhi = send(to_xn, 1, 0), send(to_xp, -1, 0)
    ylo, yhi = send(to_yn, 0, 1), send(to_yp, 0, -1)
    drift = inner_drift(level, velocity)
    adv, to_xp, to_xn, to_yp, to_yn, tail_p, tail_n = advect(
        tiles, level, xlo, xhi, ylo, yhi, velocity, drift
    )
    axlo, axhi = send(to_xn, 1, 0), send(to_xp, -1, 0)
    aylo, ayhi = send(to_yn, 0, 1), send(to_yp, 0, -1)
    row = lax.broadcasted_iota(jnp.int32, (1, 8, 1), 1)

    def corners(rows, mark, tail):
        faces = [jnp.where(row == mark, f[DEEP:, rows], f[:DEEP, rows]) for f in (axlo, axhi)]
        return jnp.concatenate(faces + [tail], axis=0)

    clo = send(corners(slice(-8, None), 0, tail_n), 0, 1)
    chi = send(corners(slice(0, 8), 7, tail_p), 0, -1)
    to_syp, to_syn, aylo, ayhi, clo, chi = lax.optimization_barrier(
        (to_syp, to_syn, aylo, ayhi, clo, chi)
    )
    sylo, syhi = send(to_syn, 0, 1), send(to_syp, 0, -1)
    cur, weight, part = sweeps(tiles, adv, (axlo, axhi, aylo, ayhi, clo, chi), nx * ny)
    parts = lax.all_to_all(part, ("gx", "gy"), 0, 0, tiled=True)
    return extend(parts, cur, weight, stress, (xlo, xhi, sylo, syhi, clo, chi))


def solution(mesh):
    in_specs = (
        P("gx", "gy", None),
        P(None, "gx", "gy", None),
        P(None, "gx", "gy", None),
        P("gx", "gy", None),
    )
    out_specs = (P("gx", "gy", None), P(None, "gx", "gy", None))
    return jax.shard_map(
        on_device, mesh=mesh, in_specs=in_specs, out_specs=out_specs, check_vma=False
    )
```

```python
import functools

import jax
import jax.numpy as jnp
from jax import lax
from jax.experimental import pallas as pl
from jax.experimental.pallas import tpu as pltpu
from jax.sharding import PartitionSpec as P

TILE = 16
SWEEPS = 5
EPSILON = 1e-06
TIME_STEP = 0.4
PSEUDO_STEP = 0.3

CX = 32
CY = 32
LANES = 128
DEEP = 7
ROWS = 64
OWN = 16
UNIT = 16
COMPS = 6
F32 = jnp.float32
DOUBLED = 2.0 * 1.4426950408889634
MIB = 1024 * 1024
ANY = pl.BlockSpec(memory_space=pl.ANY)
VMEM = pl.BlockSpec(memory_space=pltpu.VMEM)
SMEM = pl.BlockSpec(memory_space=pltpu.SMEM)


def half(h):
    return pl.ds(h * LANES, LANES)


def recip(x):
    return pl.reciprocal(x, approx=True)


def lane_shift(pair, k):
    lane = lax.broadcasted_iota(jnp.int32, pair[0].shape, pair[0].ndim - 1)
    turned = [pltpu.roll(p, (-k) % LANES, p.ndim - 1) for p in pair]
    edge = lane >= LANES - k if k > 0 else lane < -k
    return [jnp.where(edge, turned[1 - h], turned[h]) for h in range(2)]


def weno(d, positive):
    v = [jnp.where(positive, d[k], d[5 - k]) for k in range(5)]
    d1, d2, d3, d4 = (v[k + 1] - v[k] for k in range(4))
    u1, u2, u3 = d2 - d1, d3 - d2, d4 - d3
    g1 = d2 + d2 + u1
    g2 = d2 + d3
    g3 = u3 - (d3 + d3)
    scale = 13.0 / 3.0
    a1 = recip(4.0 * EPSILON + (scale * u1 * u1 + g1 * g1))
    a2 = recip(4.0 * EPSILON + (scale * u2 * u2 + g2 * g2))
    a3 = recip(4.0 * EPSILON + (scale * u3 * u3 + g3 * g3))
    a1 = a1 * a1
    a2 = 6.0 * (a2 * a2)
    a3 = 3.0 * (a3 * a3)
    top = a1 * (u1 - u2) + 0.5 * (a3 * (u2 - u3))
    mid = v[2] + (d3 + d3 + d2) * (1.0 / 6.0)
    return mid + top * (recip(a1 + a2 + a3) * (1.0 / 3.0))


def band_table(tiles_ref):
    shape = (8, LANES)
    row = lax.broadcasted_iota(jnp.int32, shape, 0)
    lane = lax.broadcasted_iota(jnp.int32, shape, 1)
    numbers = (row // 2) * 16 + (row % 2) * 8 + lane // TILE
    flags = jnp.zeros(shape, F32)
    for slot in range(tiles_ref.shape[-1]):
        flags = jnp.where(numbers == tiles_ref[0, 0, slot], 1.0, flags)
    return flags


def derivative(line, speed):
    return speed * weno([line[k + 1] - line[k] for k in range(6)], speed > 0)


def along_x(pad, x, h, at, size):
    return [pad[x + k, h, pl.ds(at, size), :] for k in range(-3, 4)]


def along_y(pad, x, h, at, size):
    return [pad[x, h, pl.ds(at + k, size), :] for k in range(-3, 4)]


def cut_kernel(
    level, stress, to_xp, to_xn, to_yp, to_yn, to_syp, to_syn, faces, x_sems, y_sems
):
    copies = []
    for n, (out, at) in enumerate(((to_xp, 0), (to_xn, CX))):
        deep = lambda size: pl.ds(at and at - size, size)
        copies.append(pltpu.make_async_copy(level.at[deep(3)], out.at[pl.ds(0, 3)], x_sems.at[n, 0]))
        for c in range(COMPS):
            copies.append(
                pltpu.make_async_copy(
                    stress.at[c, deep(2)], out.at[pl.ds(3 + 2 * c, 2)], x_sems.at[n, 1 + c]
                )
            )
    for copy in copies:
        copy.start()
    sides = []
    for n, y in enumerate((0, CY - 8)):
        side = []
        for h in range(2):
            for m in range(1 + COMPS):
                src = stress.at[m - 1] if m else level
                side.append(
                    pltpu.make_async_copy(
                        src.at[:, pl.ds(y, 8), half(h)], faces.at[m, n, h], y_sems.at[m, n, h]
                    )
                )
        for copy in side:
            copy.start()
        sides.append(side)
    flat = faces.reshape(1 + COMPS, 2, 2, CX * 8, LANES)
    for n, outs in enumerate(((to_yp, to_syp), (to_yn, to_syn))):
        for copy in sides[n]:
            copy.wait()
        for h in range(2):
            for m in range(1 + COMPS):
                depth = 2 if m else 3
                out = outs[min(m, 1)]
                first = 2 * m - 2 if m else 0
                for k in range(depth):
                    row = k if n == 0 else 8 - depth + k
                    for x in range(0, CX, 8):
                        out[first + k, x : x + 8, half(h)] = flat[
                            m, n, h, pl.ds(8 * x + row, 8, stride=8), :
                        ]
    for copy in copies:
        copy.wait()


def cut(level, stress):
    message = lambda planes: jax.ShapeDtypeStruct((planes, CX, 2 * LANES), F32)
    return pl.pallas_call(
        cut_kernel,
        out_shape=[message(3 + 2 * COMPS)] * 2 + [message(3)] * 2 + [message(2 * COMPS)] * 2,
        in_specs=[ANY] * 2,
        out_specs=[VMEM] * 6,
        scratch_shapes=[
            pltpu.VMEM((1 + COMPS, 2, 2, CX, 8, LANES), F32),
            pltpu.SemaphoreType.DMA((2, 1 + COMPS)),
            pltpu.SemaphoreType.DMA((1 + COMPS, 2, 2)),
        ],
        compiler_params=pltpu.CompilerParams(vmem_limit_bytes=57 * MIB),
        name="cut",
    )(level, stress)


def inner_kernel(level, speed, drift, pad, sems):
    copies = [
        pltpu.make_async_copy(level.at[:, :, half(h)], pad.at[:, h], sems.at[h]) for h in range(2)
    ]
    for copy in copies:
        copy.start()
    for copy in copies:
        copy.wait()

    def plane(x, with_x):
        for unit in range(CY // UNIT):
            rows = pl.ds(unit * UNIT, UNIT)
            v = [[speed[d, x, rows, half(h)].astype(F32) for h in range(2)] for d in range(3)]
            for part in range(UNIT // 8):
                at = unit * UNIT + 8 * part
                cut = slice(8 * part, 8 * part + 8)
                center = [pad[x, h, pl.ds(at, 8), :] for h in range(2)]
                ups = [lane_shift(center, k) for k in (1, 2, 3)]
                downs = [lane_shift(center, -k) for k in (3, 2, 1)]
                for h in range(2):
                    line = [s[h] for s in downs] + [center[h]] + [s[h] for s in ups]
                    total = derivative(line, v[2][h][cut])
                    if with_x:
                        total = total + derivative(along_x(pad, x, h, at, 8), v[0][h][cut])
                    if 8 <= at < CY - 8:
                        total = total + derivative(along_y(pad, x, h, at, 8), v[1][h][cut])
                    drift[x, pl.ds(at, 8), half(h)] = total

    def inner(x, carry):
        plane(x, True)
        return carry

    def outer(x, carry):
        plane(x, False)
        plane(x + CX - 3, False)
        return carry

    lax.fori_loop(0, 3, outer, 0)
    lax.fori_loop(3, CX - 3, inner, 0, unroll=2)


def inner_drift(level, speed):
    return pl.pallas_call(
        inner_kernel,
        out_shape=jax.ShapeDtypeStruct(level.shape, F32),
        in_specs=[ANY, VMEM],
        out_specs=VMEM,
        scratch_shapes=[
            pltpu.VMEM((CX, 2, CY, LANES), F32),
            pltpu.SemaphoreType.DMA((2,)),
        ],
        compiler_params=pltpu.CompilerParams(vmem_limit_bytes=10 * MIB),
        cost_estimate=pl.CostEstimate(
            flops=180 * level.size, bytes_accessed=14 * level.size, transcendentals=9 * level.size
        ),
        name="inner_drift",
    )(level, speed)


def advect_kernel(
    tiles, level, xlo, xhi, ylo, yhi, speed, drift,
    adv, to_xp, to_xn, to_yp, to_yn, tail_p, tail_n,
    pad, table, faces, ends, sems, y_sems, end_sems,
):
    copies = []
    for h in range(2):
        for n, (src, at, size) in enumerate(((level, 3, CX), (xlo, 0, 3), (xhi, CX + 3, 3))):
            copies.append(
                pltpu.make_async_copy(
                    src.at[pl.ds(0, size), :, half(h)],
                    pad.at[pl.ds(at, size), h, pl.ds(8, CY), :],
                    sems.at[h, n],
                )
            )
    for n, src in enumerate((ylo, yhi)):
        copies.append(pltpu.make_async_copy(src, faces.at[n], y_sems.at[n]))
    for n, src in enumerate((xlo, xhi)):
        for m, y in enumerate((0, CY - 8)):
            copies.append(
                pltpu.make_async_copy(
                    src.at[pl.ds(3, 2 * COMPS), pl.ds(y, 8)], ends.at[n, m], end_sems.at[n, m]
                )
            )
    for copy in copies:
        copy.start()
    table[...] = band_table(tiles)
    for copy in copies:
        copy.wait()
    for m, (tail, row) in enumerate(((tail_p, 0), (tail_n, 7))):
        tail[...] = jnp.zeros(tail.shape, F32)
        for n in range(2):
            for c in range(COMPS):
                to = n * COMPS + c
                tail[to // 8, to % 8 : to % 8 + 1, :] = ends[n, m, 2 * c + 1 - n, row : row + 1, :]
    flat = pad.reshape((CX + 6) * 2 * 48, LANES)
    for n, row in enumerate((5, 8 + CY)):
        for h in range(2):
            for k in range(3):
                for x in range(0, CX, 8):
                    rows = pl.ds(((x + 3) * 2 + h) * 48 + row + k, 8, stride=96)
                    flat[rows, :] = faces[n, k, x : x + 8, half(h)]

    def plane(x, with_x):
        for unit in range(CY // UNIT):
            rows = pl.ds(unit * UNIT, UNIT)
            for h in range(2):
                vx = speed[0, x, rows, half(h)].astype(F32) if with_x else None
                vy = speed[1, x, rows, half(h)].astype(F32)
                for part in range(UNIT // 8):
                    at = unit * UNIT + 8 * part
                    cut = slice(8 * part, 8 * part + 8)
                    total = drift[x, pl.ds(at, 8), half(h)]
                    if with_x:
                        total = total + derivative(along_x(pad, x + 3, h, at + 8, 8), vx[cut])
                    if at in (0, CY - 8):
                        total = total + derivative(along_y(pad, x + 3, h, at + 8, 8), vy[cut])
                    adv[x, pl.ds(at, 8), half(h)] = (
                        pad[x + 3, h, pl.ds(at + 8, 8), :] - TIME_STEP * total
                    )

    def inner(x, carry):
        plane(x, False)
        return carry

    def outer(x, carry):
        plane(x, True)
        plane(x + CX - 3, True)
        return carry

    lax.fori_loop(0, 3, outer, 0)
    lax.fori_loop(3, CX - 3, inner, 0, unroll=2)
    low, high = CX - DEEP, CX
    to_xp[0:DEEP] = adv[0:DEEP]
    to_xn[0:DEEP] = adv[low:high]
    row8 = lax.broadcasted_iota(jnp.int32, (8, LANES), 0)
    for h in range(2):
        for j in range(2):
            rows = pl.ds(j * TILE, TILE)
            for i, face in ((0, to_xp), (1, to_xn)):
                r = i * 4 + j * 2 + h
                face[DEEP, rows, half(h)] = jnp.broadcast_to(table[r : r + 1, :], (TILE, LANES))
        for i in range(2):
            first = table[i * 4 + h : i * 4 + h + 1, :]
            last = table[i * 4 + 2 + h : i * 4 + 3 + h, :]
            for x in range(i * TILE, i * TILE + TILE):
                to_yp[x, :, half(h)] = jnp.where(row8 == 7, first, adv[x, 0:8, half(h)])
                to_yn[x, :, half(h)] = jnp.where(row8 == 0, last, adv[x, CY - 8 : CY, half(h)])


def advect(tiles, level, xlo, xhi, ylo, yhi, speed, drift):
    shape = lambda *s: jax.ShapeDtypeStruct(s, F32)
    z = 2 * LANES
    return pl.pallas_call(
        advect_kernel,
        out_shape=[shape(CX, CY, z)]
        + [shape(8, CY, z)] * 2
        + [shape(CX, 8, z)] * 2
        + [shape(2, 8, z)] * 2,
        in_specs=[SMEM, ANY, ANY, ANY, ANY, ANY, VMEM, VMEM],
        out_specs=[VMEM] * 7,
        scratch_shapes=[
            pltpu.VMEM((CX + 6, 2, 48, LANES), F32),
            pltpu.VMEM((8, LANES), F32),
            pltpu.VMEM((2, 3, CX, z), F32),
            pltpu.VMEM((2, 2, 2 * COMPS, 8, z), F32),
            pltpu.SemaphoreType.DMA((2, 3)),
            pltpu.SemaphoreType.DMA((2,)),
            pltpu.SemaphoreType.DMA((2, 2)),
        ],
        compiler_params=pltpu.CompilerParams(vmem_limit_bytes=12 * MIB),
        name="advect",
    )(tiles, level, xlo, xhi, ylo, yhi, speed, drift)


WIDE = CX + 2 * DEEP
INNER = 48
SPLIT = 2


def sweep_rows(src, factor, x, fx, start, stride, groups, store):
    span = pl.ds if stride == 1 else functools.partial(pl.ds, stride=stride)
    rows = [span(start + k, 8) for k in range(-1, groups + 1)]
    lines = [[src[x, h, r, :] for r in rows] for h in range(2)]
    for k in range(1, groups + 1):
        center = [lines[h][k] for h in range(2)]
        up, down = lane_shift(center, 1), lane_shift(center, -1)
        for h in range(2):
            c = center[h]
            step = factor[fx, h, rows[k], :]
            positive = step > 0
            pairs = (
                (src[x - 1, h, rows[k], :], src[x + 1, h, rows[k], :]),
                (lines[h][k - 1], lines[h][k + 1]),
                (down[h], up[h]),
            )
            total = None
            for l, r in pairs:
                low = jnp.minimum(jnp.minimum(l, r), c)
                high = jnp.maximum(jnp.maximum(l, r), c)
                diff = c - jnp.where(positive, low, high)
                total = diff * diff if total is None else total + diff * diff
            slope = total * lax.rsqrt(jnp.maximum(total, 1e-36))
            store(h, rows[k], c - step * (slope - 1.0))


def band_step(value, band):
    square = value * value
    weight = band * recip(1.0 + square * (1.0 / 36.0))
    return PSEUDO_STEP * (value * lax.rsqrt(square + 1.0)) * weight, weight


def inner_sweeps(source, factor, targets, first):
    for n, target in enumerate(targets):
        sweep = first + n

        def body(x, carry, source=source, target=target):
            def store(h, rows, value):
                target[x, h, rows, :] = value

            sweep_rows(source, factor, x, x, 8, CY // 8, CY // 8, store)
            return carry

        lax.fori_loop(sweep, CX - sweep, body, 0, unroll=2)
        source = target


def inner_first_kernel(tiles, adv, done, factor, weight, own, table, sems):
    copies = [
        pltpu.make_async_copy(adv.at[:, :, half(h)], own.at[:, h, pl.ds(8, CY), :], sems.at[h])
        for h in range(2)
    ]
    for copy in copies:
        copy.start()
    table[...] = band_table(tiles)
    for copy in copies:
        copy.wait()
    for i in range(2):

        def body(x, carry, i=i):
            for h in range(2):
                for group in range(CY // 8):
                    rows = pl.ds(8 + 8 * group, 8)
                    r = i * 4 + (group // 2) * 2 + h
                    band = jnp.broadcast_to(table[r : r + 1, :], (8, LANES))
                    step, value = band_step(own[x, h, rows, :], band)
                    factor[x, h, rows, :] = step
                    weight[x, h, rows, :] = value
            return carry

        lax.fori_loop(i * TILE, (i + 1) * TILE, body, 0, unroll=2)
    inner_sweeps(own, factor, [done.at[n] for n in range(SPLIT)], 1)


def inner_second_kernel(before, factor, done):
    inner_sweeps(before.at[SPLIT - 1], factor, [done.at[n] for n in range(SWEEPS - SPLIT)], SPLIT + 1)


def inner_first(tiles, adv):
    shape = lambda *s: jax.ShapeDtypeStruct(s + (CX, 2, INNER, LANES), F32)
    return pl.pallas_call(
        inner_first_kernel,
        out_shape=[shape(SPLIT), shape(), shape()],
        in_specs=[SMEM, ANY],
        out_specs=[VMEM] * 3,
        scratch_shapes=[
            pltpu.VMEM((CX, 2, INNER, LANES), F32),
            pltpu.VMEM((8, LANES), F32),
            pltpu.SemaphoreType.DMA((2,)),
        ],
        compiler_params=pltpu.CompilerParams(vmem_limit_bytes=12 * MIB),
        cost_estimate=pl.CostEstimate(
            flops=100 * adv.size, bytes_accessed=24 * adv.size, transcendentals=4 * adv.size
        ),
        name="inner_first",
    )(tiles, adv)


def inner_second(before, factor):
    return pl.pallas_call(
        inner_second_kernel,
        out_shape=jax.ShapeDtypeStruct((SWEEPS - SPLIT, CX, 2, INNER, LANES), F32),
        in_specs=[VMEM] * 2,
        out_specs=VMEM,
        compiler_params=pltpu.CompilerParams(vmem_limit_bytes=12 * MIB),
        cost_estimate=pl.CostEstimate(
            flops=60 * factor.size, bytes_accessed=24 * factor.size, transcendentals=2 * factor.size
        ),
        name="inner_second",
    )(before, factor)


def sweep_kernel(
    adv, inner1, inner2, own_factor, own_weight, xlo, xhi, ylo, yhi, clo, chi,
    cur_out, weight_out, part,
    bufs, factor, masks, sums, sems, x_sems,
):
    copies = []
    done = []
    for h in range(2):
        pieces = (
            (adv, DEEP, CX, OWN, CY),
            (xlo.at[pl.ds(0, DEEP)], 0, DEEP, OWN, CY),
            (xhi.at[pl.ds(0, DEEP)], DEEP + CX, DEEP, OWN, CY),
            (ylo, DEEP, CX, OWN - 8, 8),
            (yhi, DEEP, CX, OWN + CY, 8),
            (clo.at[pl.ds(0, DEEP)], 0, DEEP, OWN - 8, 8),
            (clo.at[pl.ds(DEEP, DEEP)], DEEP + CX, DEEP, OWN - 8, 8),
            (chi.at[pl.ds(0, DEEP)], 0, DEEP, OWN + CY, 8),
            (chi.at[pl.ds(DEEP, DEEP)], DEEP + CX, DEEP, OWN + CY, 8),
        )
        for n, (src, x, nx, y, ny) in enumerate(pieces):
            copies.append(
                pltpu.make_async_copy(
                    src.at[:, :, half(h)],
                    bufs.at[0, pl.ds(x, nx), h, pl.ds(y, ny), :],
                    sems.at[h, n],
                )
            )
        for n, src in enumerate((xlo, xhi)):
            copies.append(
                pltpu.make_async_copy(
                    src.at[pl.ds(DEEP, 1), :, half(h)], masks.at[pl.ds(n, 1), h], sems.at[h, 9 + n]
                )
            )
    own = lambda ref, x: ref.at[pl.ds(x, CX), :, pl.ds(OWN, CY), :]
    for n, (src, dst) in enumerate(
        [(own_factor, own(factor, DEEP)), (own_weight, own(weight_out, 1))]
        + [(inner1.at[n], own(bufs.at[n + 1], DEEP)) for n in range(SPLIT)]
        + [(inner2.at[n], own(bufs.at[n + 1 + SPLIT], DEEP)) for n in range(SWEEPS - 1 - SPLIT)]
        + [(inner2.at[SWEEPS - 1 - SPLIT], own(cur_out, 2))]
    ):
        done.append(pltpu.make_async_copy(src.at[:, :, pl.ds(8, CY), :], dst, x_sems.at[n]))
    for copy in copies + done:
        copy.start()
    sums[...] = jnp.zeros(sums.shape, F32)
    for copy in copies + done[:2]:
        copy.wait()

    def prepare(x, groups, bands, keep):
        for h in range(2):
            for group in groups:
                rows = pl.ds(OWN + 8 * group, 8)
                value = bufs[0, x, h, rows, :]
                if group == -1:
                    band = jnp.broadcast_to(value[0:1], value.shape)
                elif group == 4:
                    band = jnp.broadcast_to(value[7:8], value.shape)
                else:
                    band = masks[bands, h, pl.ds(8 * group, 8), :]
                step, weight = band_step(value, band)
                factor[x, h, rows, :] = step
                if keep:
                    weight_out[x - DEEP + 1, h, rows, :] = weight

    def run(start, stop, groups, bands, keep):
        def body(x, carry):
            prepare(x, groups, bands, keep)
            return carry

        lax.fori_loop(start, stop, body, 0, unroll=2)

    everything = tuple(range(-1, 5))
    run(1, DEEP - 1, everything, 0, False)
    prepare(DEEP - 1, everything, 0, True)
    run(DEEP, DEEP + CX, (-1, 4), 0, True)
    prepare(DEEP + CX, everything, 1, True)
    run(DEEP + CX + 1, WIDE - 1, everything, 1, False)

    for sweep in range(1, SWEEPS + 1):
        done[sweep + 1].wait()
        offset, target = (0, bufs.at[sweep]) if sweep < SWEEPS else (SWEEPS, cur_out)
        groups = 6 if DEEP - sweep > 4 else 5
        source = bufs.at[sweep - 1]

        def whole(x, source=source, target=target, offset=offset, groups=groups):
            def store(h, rows, value):
                target[x - offset, h, rows, :] = value

            start = OWN + CY // 2 - 4 * groups
            sweep_rows(source, factor, x, x, start, groups, groups, store)

        def ends(x, source=source, target=target, offset=offset, sweep=sweep):
            def store(h, rows, value):
                target[x - offset, h, rows, :] = value

            for start in (OWN + sweep - 8, OWN + CY - sweep):
                sweep_rows(source, factor, x, x, start, 1, 1, store)

        def outer(n, carry, whole=whole, sweep=sweep):
            whole(sweep + n)
            whole(WIDE - 1 - sweep - n)
            return carry

        def middle(x, carry, ends=ends):
            ends(x)
            return carry

        lax.fori_loop(0, DEEP, outer, 0)
        lax.fori_loop(DEEP + sweep, DEEP + CX - sweep, middle, 0, unroll=2)

    def count(x, carry):
        for h in range(2):
            for unit in range(CY // UNIT):
                rows = pl.ds(OWN + unit * UNIT, UNIT)
                after = jnp.tanh(cur_out[x + 2, h, rows, :])
                before = jnp.tanh(bufs[0, x + DEEP, h, rows, :])
                sums[0] += after - before
                sums[1] += 1.0 - after * after
        return carry

    lax.fori_loop(0, CX, count, 0, unroll=2)
    lane = lax.broadcasted_iota(jnp.int32, (1, LANES), 1)
    sums_row = jnp.where(lane < 64, jnp.sum(sums[0]), jnp.sum(sums[1]))
    part[...] = jnp.broadcast_to(sums_row, part.shape)


def sweeps(adv, inner1, inner2, factor, weight, halos, count):
    shape = lambda *s: jax.ShapeDtypeStruct(s, F32)
    return pl.pallas_call(
        sweep_kernel,
        out_shape=[
            shape(CX + 4, 2, ROWS, LANES), shape(CX + 2, 2, ROWS, LANES), shape(count, 1, LANES)
        ],
        in_specs=[ANY] * 11,
        out_specs=[VMEM] * 3,
        scratch_shapes=[
            pltpu.VMEM((SWEEPS, WIDE, 2, ROWS, LANES), F32),
            pltpu.VMEM((WIDE, 2, ROWS, LANES), F32),
            pltpu.VMEM((2, 2, CY, LANES), F32),
            pltpu.VMEM((2, UNIT, LANES), F32),
            pltpu.SemaphoreType.DMA((2, 11)),
            pltpu.SemaphoreType.DMA((2 + SWEEPS,)),
        ],
        compiler_params=pltpu.CompilerParams(vmem_limit_bytes=30 * MIB),
        name="sweeps",
    )(adv, inner1, inner2, factor, weight, *halos)


CHUNKS = ((0, 10), (10, 18), (18, 26), (26, 32))


def extend_kernel(
    parts, cur, weight, stress, xlo, xhi, ylo, yhi, clo, chi,
    level_out, stress_out,
    pad, ring, mix, stage, sems, x_sems, out_sems,
):
    def chunk(n):
        start, stop = CHUNKS[n]
        own = stress.at[:, pl.ds(start, stop - start)]
        copies = [
            pltpu.make_async_copy(
                own.at[:, :, :, half(h)],
                pad.at[:, pl.ds(start + 2, stop - start), h, pl.ds(OWN, CY), :],
                sems.at[n, h],
            )
            for h in range(2)
        ]
        for side, src in ((0, xlo), (3, xhi)):
            if n == side:
                at = 0 if n == 0 else CX + 2
                for h in range(2):
                    for c in range(COMPS):
                        copies.append(
                            pltpu.make_async_copy(
                                src.at[pl.ds(3 + 2 * c, 2), :, half(h)],
                                pad.at[c, pl.ds(at, 2), h, pl.ds(OWN, CY), :],
                                x_sems.at[side % 2, h, c],
                            )
                        )
        return copies

    chunks = [chunk(n) for n in range(len(CHUNKS))]
    for copies in chunks:
        for copy in copies:
            copy.start()
    sums = jnp.sum(parts[...], axis=0)
    shift = sums[:, 0:1] / sums[:, 64:65]
    flat = pad.reshape(COMPS, (CX + 4) * 2 * ROWS, LANES)
    for h in range(2):
        for c in range(COMPS):
            for face, row in ((ylo, OWN - 2), (yhi, OWN + CY)):
                for k in range(2):
                    for x in range(0, CX, 8):
                        at = ((x + 2) * 2 + h) * ROWS + row + k
                        flat[c, pl.ds(at, 8, stride=2 * ROWS), :] = face[
                            2 * c + k, x : x + 8, half(h)
                        ]
            for corner, row in ((clo, OWN - 1), (chi, OWN + CY)):
                for x, n in ((1, c), (CX + 2, COMPS + c)):
                    at = 2 * DEEP + n // 8
                    pad[c, x, h, row : row + 1, :] = corner[at, n % 8 : n % 8 + 1, half(h)]

    def blend(mixes, center, around):
        value = mixes[6] * center
        for n in range(6):
            value = value + mixes[n] * around[n]
        return value

    def neighbours(load, groups):
        start = OWN + CY // 2 - 4 * groups
        for k in range(groups):
            rows, below, above = (pl.ds(start + k + d, 8, stride=groups) for d in (0, -1, 1))
            center = [load(0, h, rows) for h in range(2)]
            up, down = lane_shift(center, 1), lane_shift(center, -1)
            yield rows, center, [
                [
                    load(-1, h, rows), load(1, h, rows), load(0, h, below), load(0, h, above),
                    down[h], up[h],
                ]
                for h in range(2)
            ]

    def first_step(i, slot, groups=5):
        levels = neighbours(lambda dx, h, r: cur[i + 1 + dx, h, r, :] * DOUBLED, groups)
        comps = [
            neighbours(lambda dx, h, r, c=c: pad[c, i + 1 + dx, h, r, :], groups)
            for c in range(COMPS)
        ]
        for rows, center, around in levels:
            mixes = []
            for h in range(2):
                c = center[h]
                w = [recip(1.0 + jnp.exp2(jnp.minimum(n - c, 125.5))) for n in around[h]]
                total = w[0] + w[1] + w[2] + w[3] + w[4] + w[5]
                gate = weight[i, h, rows, :] * 0.5 * (
                    1.0 + jnp.tanh(c * (2.0 / DOUBLED) - 2.0 * shift)
                )
                scaled = gate * recip(total)
                w = [scaled * n for n in w] + [1.0 - gate]
                mixes.append(w)
                for n in range(7):
                    mix[slot % 2, n, h, rows, :] = w[n]
            for comp in range(COMPS):
                _, center, around = next(comps[comp])
                for h in range(2):
                    ring[slot, comp, h, rows, :] = blend(mixes[h], center[h], around[h])

    def second_step(x, slot):
        slots = {dx: (slot + dx) % 4 for dx in (-1, 0, 1)}
        groups = CY // 8
        comps = [
            neighbours(lambda dx, h, r, c=c: ring[slots[dx], c, h, r, :], groups)
            for c in range(COMPS)
        ]
        for k in range(groups):
            rows = pl.ds(OWN + k, 8, stride=groups)
            mixes = [[mix[slot % 2, n, h, rows, :] for n in range(7)] for h in range(2)]
            for comp in range(COMPS):
                _, center, around = next(comps[comp])
                for h in range(2):
                    stage[comp, x, h, pl.ds(k, 8, stride=groups), :] = blend(
                        mixes[h], center[h], around[h]
                    )
        for h in range(2):
            level_out[x, :, half(h)] = cur[x + 2, h, OWN : OWN + CY, :] - shift

    outs = []
    for n in range(len(CHUNKS)):
        for copy in chunks[n]:
            copy.wait()
        if n == 0:
            first_step(0, 0, groups=4)
            first_step(1, 1)

        def body(group, carry):
            for k in range(4):
                i = group * 4 + k + 2
                first_step(i, (k + 2) % 4)
                second_step(i - 2, (k + 1) % 4)
            return carry

        lax.fori_loop(2 * n, 2 * n + 2, body, 0)
        planes = pl.ds(8 * n, 8)
        for h in range(2):
            copy = pltpu.make_async_copy(
                stage.at[:, planes, h], stress_out.at[:, planes, :, half(h)], out_sems.at[n, h]
            )
            copy.start()
            outs.append(copy)
    for copy in outs:
        copy.wait()


def extend(parts, cur, weight, stress, halos):
    shape = lambda *s: jax.ShapeDtypeStruct(s, F32)
    z = 2 * LANES
    return pl.pallas_call(
        extend_kernel,
        out_shape=[shape(CX, CY, z), shape(COMPS, CX, CY, z)],
        in_specs=[VMEM, VMEM, VMEM, ANY, ANY, ANY, VMEM, VMEM, VMEM, VMEM],
        out_specs=[VMEM, ANY],
        scratch_shapes=[
            pltpu.VMEM((COMPS, CX + 4, 2, ROWS, LANES), F32),
            pltpu.VMEM((4, COMPS, 2, ROWS, LANES), F32),
            pltpu.VMEM((2, 7, 2, ROWS, LANES), F32),
            pltpu.VMEM((COMPS, CX, 2, CY, LANES), F32),
            pltpu.SemaphoreType.DMA((4, 2)),
            pltpu.SemaphoreType.DMA((2, 2, COMPS)),
            pltpu.SemaphoreType.DMA((4, 2)),
        ],
        compiler_params=pltpu.CompilerParams(vmem_limit_bytes=46 * MIB),
        name="extend",
    )(parts, cur, weight, stress, *halos)


def on_device(level, velocity, stress, tiles):
    nx, ny = lax.axis_size("gx"), lax.axis_size("gy")

    def send(value, dx, dy):
        if dy == 0:
            return lax.ppermute(value, "gx", [(i, (i + dx) % nx) for i in range(nx)])
        if dx == 0:
            return lax.ppermute(value, "gy", [(i, (i + dy) % ny) for i in range(ny)])
        pairs = [
            (i * ny + j, (i + dx) % nx * ny + (j + dy) % ny) for i in range(nx) for j in range(ny)
        ]
        return lax.ppermute(value, ("gx", "gy"), pairs)

    to_xp, to_xn, to_yp, to_yn, to_syp, to_syn = cut(level, stress)
    xlo, xhi = send(to_xn, 1, 0), send(to_xp, -1, 0)
    ylo, yhi = send(to_yn, 0, 1), send(to_yp, 0, -1)
    drift = inner_drift(level, velocity)
    adv, to_xp, to_xn, to_yp, to_yn, tail_p, tail_n = advect(
        tiles, level, xlo, xhi, ylo, yhi, velocity, drift
    )
    axlo, axhi = send(to_xn, 1, 0), send(to_xp, -1, 0)
    aylo, ayhi = send(to_yn, 0, 1), send(to_yp, 0, -1)
    row = lax.broadcasted_iota(jnp.int32, (1, 8, 1), 1)

    def corners(rows, mark, tail):
        faces = [jnp.where(row == mark, f[DEEP:, rows], f[:DEEP, rows]) for f in (axlo, axhi)]
        return jnp.concatenate(faces + [tail], axis=0)

    inner1, factor, weight = inner_first(tiles, adv)
    inner1, axlo, axhi = lax.optimization_barrier((inner1, axlo, axhi))
    inner2 = inner_second(inner1, factor)
    clo = send(corners(slice(-8, None), 0, tail_n), 0, 1)
    chi = send(corners(slice(0, 8), 7, tail_p), 0, -1)
    to_syp, to_syn, aylo, ayhi, clo, chi, inner2 = lax.optimization_barrier(
        (to_syp, to_syn, aylo, ayhi, clo, chi, inner2)
    )
    sylo, syhi = send(to_syn, 0, 1), send(to_syp, 0, -1)
    cur, weight, part = sweeps(
        adv, inner1, inner2, factor, weight, (axlo, axhi, aylo, ayhi, clo, chi), nx * ny
    )
    parts = lax.all_to_all(part, ("gx", "gy"), 0, 0, tiled=True)
    return extend(parts, cur, weight, stress, (xlo, xhi, sylo, syhi, clo, chi))


def solution(mesh):
    in_specs = (
        P("gx", "gy", None),
        P(None, "gx", "gy", None),
        P(None, "gx", "gy", None),
        P("gx", "gy", None),
    )
    out_specs = (P("gx", "gy", None), P(None, "gx", "gy", None))
    return jax.shard_map(
        on_device, mesh=mesh, in_specs=in_specs, out_specs=out_specs, check_vma=False
    )
```

```python
import functools

import jax
import jax.numpy as jnp
from jax import lax
from jax.experimental import pallas as pl
from jax.experimental.pallas import tpu as pltpu
from jax.sharding import PartitionSpec as P

TILE = 16
SWEEPS = 5
EPSILON = 1e-06
TIME_STEP = 0.4
PSEUDO_STEP = 0.3

CX = 32
CY = 32
LANES = 128
DEEP = 7
ROWS = 64
OWN = 16
UNIT = 16
COMPS = 6
F32 = jnp.float32
DOUBLED = 2.0 * 1.4426950408889634
MIB = 1024 * 1024
ANY = pl.BlockSpec(memory_space=pl.ANY)
VMEM = pl.BlockSpec(memory_space=pltpu.VMEM)
SMEM = pl.BlockSpec(memory_space=pltpu.SMEM)


def half(h):
    return pl.ds(h * LANES, LANES)


def recip(x):
    return pl.reciprocal(x, approx=True)


def lane_shift(pair, k):
    lane = lax.broadcasted_iota(jnp.int32, pair[0].shape, pair[0].ndim - 1)
    turned = [pltpu.roll(p, (-k) % LANES, p.ndim - 1) for p in pair]
    edge = lane >= LANES - k if k > 0 else lane < -k
    return [jnp.where(edge, turned[1 - h], turned[h]) for h in range(2)]


def weno(d, positive):
    v = [jnp.where(positive, d[k], d[5 - k]) for k in range(5)]
    d1, d2, d3, d4 = (v[k + 1] - v[k] for k in range(4))
    u1, u2, u3 = d2 - d1, d3 - d2, d4 - d3
    g1 = d2 + d2 + u1
    g2 = d2 + d3
    g3 = u3 - (d3 + d3)
    scale = 13.0 / 3.0
    a1 = recip(4.0 * EPSILON + (scale * u1 * u1 + g1 * g1))
    a2 = recip(4.0 * EPSILON + (scale * u2 * u2 + g2 * g2))
    a3 = recip(4.0 * EPSILON + (scale * u3 * u3 + g3 * g3))
    a1 = a1 * a1
    a2 = 6.0 * (a2 * a2)
    a3 = 3.0 * (a3 * a3)
    top = a1 * (u1 - u2) + 0.5 * (a3 * (u2 - u3))
    mid = v[2] + (d3 + d3 + d2) * (1.0 / 6.0)
    return mid + top * (recip(a1 + a2 + a3) * (1.0 / 3.0))


def band_table(tiles_ref):
    shape = (8, LANES)
    row = lax.broadcasted_iota(jnp.int32, shape, 0)
    lane = lax.broadcasted_iota(jnp.int32, shape, 1)
    numbers = (row // 2) * 16 + (row % 2) * 8 + lane // TILE
    flags = jnp.zeros(shape, F32)
    for slot in range(tiles_ref.shape[-1]):
        flags = jnp.where(numbers == tiles_ref[0, 0, slot], 1.0, flags)
    return flags


def derivative(line, speed):
    return speed * weno([line[k + 1] - line[k] for k in range(6)], speed > 0)


def along_x(pad, x, h, at, size):
    return [pad[x + k, h, pl.ds(at, size), :] for k in range(-3, 4)]


def along_y(pad, x, h, at, size):
    return [pad[x, h, pl.ds(at + k, size), :] for k in range(-3, 4)]


def cut_kernel(
    level, stress, to_xp, to_xn, to_yp, to_yn, to_syp, to_syn, faces, x_sems, y_sems
):
    copies = []
    for n, (out, at) in enumerate(((to_xp, 0), (to_xn, CX))):
        deep = lambda size: pl.ds(at and at - size, size)
        copies.append(pltpu.make_async_copy(level.at[deep(3)], out.at[pl.ds(0, 3)], x_sems.at[n, 0]))
        for c in range(COMPS):
            copies.append(
                pltpu.make_async_copy(
                    stress.at[c, deep(2)], out.at[pl.ds(3 + 2 * c, 2)], x_sems.at[n, 1 + c]
                )
            )
    for copy in copies:
        copy.start()
    sides = []
    for n, y in enumerate((0, CY - 8)):
        side = []
        for h in range(2):
            for m in range(1 + COMPS):
                src = stress.at[m - 1] if m else level
                side.append(
                    pltpu.make_async_copy(
                        src.at[:, pl.ds(y, 8), half(h)], faces.at[m, n, h], y_sems.at[m, n, h]
                    )
                )
        for copy in side:
            copy.start()
        sides.append(side)
    flat = faces.reshape(1 + COMPS, 2, 2, CX * 8, LANES)
    for n, outs in enumerate(((to_yp, to_syp), (to_yn, to_syn))):
        for copy in sides[n]:
            copy.wait()
        for h in range(2):
            for m in range(1 + COMPS):
                depth = 2 if m else 3
                out = outs[min(m, 1)]
                first = 2 * m - 2 if m else 0
                for k in range(depth):
                    row = k if n == 0 else 8 - depth + k
                    for x in range(0, CX, 8):
                        out[first + k, x : x + 8, half(h)] = flat[
                            m, n, h, pl.ds(8 * x + row, 8, stride=8), :
                        ]
    for copy in copies:
        copy.wait()


def cut(level, stress):
    message = lambda planes: jax.ShapeDtypeStruct((planes, CX, 2 * LANES), F32)
    return pl.pallas_call(
        cut_kernel,
        out_shape=[message(3 + 2 * COMPS)] * 2 + [message(3)] * 2 + [message(2 * COMPS)] * 2,
        in_specs=[ANY] * 2,
        out_specs=[VMEM] * 6,
        scratch_shapes=[
            pltpu.VMEM((1 + COMPS, 2, 2, CX, 8, LANES), F32),
            pltpu.SemaphoreType.DMA((2, 1 + COMPS)),
            pltpu.SemaphoreType.DMA((1 + COMPS, 2, 2)),
        ],
        compiler_params=pltpu.CompilerParams(vmem_limit_bytes=57 * MIB),
        name="cut",
    )(level, stress)


def inner_kernel(level, speed, drift, pad, sems):
    copies = [
        pltpu.make_async_copy(level.at[:, :, half(h)], pad.at[:, h], sems.at[h]) for h in range(2)
    ]
    for copy in copies:
        copy.start()
    for copy in copies:
        copy.wait()

    def plane(x, with_x):
        for unit in range(CY // UNIT):
            rows = pl.ds(unit * UNIT, UNIT)
            v = [[speed[d, x, rows, half(h)].astype(F32) for h in range(2)] for d in range(3)]
            for part in range(UNIT // 8):
                at = unit * UNIT + 8 * part
                cut = slice(8 * part, 8 * part + 8)
                center = [pad[x, h, pl.ds(at, 8), :] for h in range(2)]
                ups = [lane_shift(center, k) for k in (1, 2, 3)]
                downs = [lane_shift(center, -k) for k in (3, 2, 1)]
                for h in range(2):
                    line = [s[h] for s in downs] + [center[h]] + [s[h] for s in ups]
                    total = derivative(line, v[2][h][cut])
                    if with_x:
                        total = total + derivative(along_x(pad, x, h, at, 8), v[0][h][cut])
                    if 8 <= at < CY - 8:
                        total = total + derivative(along_y(pad, x, h, at, 8), v[1][h][cut])
                    drift[x, pl.ds(at, 8), half(h)] = total

    def inner(x, carry):
        plane(x, True)
        return carry

    def outer(x, carry):
        plane(x, False)
        plane(x + CX - 3, False)
        return carry

    lax.fori_loop(0, 3, outer, 0)
    lax.fori_loop(3, CX - 3, inner, 0, unroll=2)


def inner_drift(level, speed):
    return pl.pallas_call(
        inner_kernel,
        out_shape=jax.ShapeDtypeStruct(level.shape, F32),
        in_specs=[ANY, VMEM],
        out_specs=VMEM,
        scratch_shapes=[
            pltpu.VMEM((CX, 2, CY, LANES), F32),
            pltpu.SemaphoreType.DMA((2,)),
        ],
        compiler_params=pltpu.CompilerParams(vmem_limit_bytes=10 * MIB),
        cost_estimate=pl.CostEstimate(
            flops=180 * level.size, bytes_accessed=14 * level.size, transcendentals=9 * level.size
        ),
        name="inner_drift",
    )(level, speed)


def advect_kernel(
    tiles, level, xlo, xhi, ylo, yhi, speed, drift,
    adv, to_xp, to_xn, to_yp, to_yn, tail_p, tail_n,
    pad, table, faces, ends, sems, y_sems, end_sems,
):
    copies = []
    for h in range(2):
        for n, (src, at, size) in enumerate(((level, 3, CX), (xlo, 0, 3), (xhi, CX + 3, 3))):
            copies.append(
                pltpu.make_async_copy(
                    src.at[pl.ds(0, size), :, half(h)],
                    pad.at[pl.ds(at, size), h, pl.ds(8, CY), :],
                    sems.at[h, n],
                )
            )
    for n, src in enumerate((ylo, yhi)):
        copies.append(pltpu.make_async_copy(src, faces.at[n], y_sems.at[n]))
    for n, src in enumerate((xlo, xhi)):
        for m, y in enumerate((0, CY - 8)):
            copies.append(
                pltpu.make_async_copy(
                    src.at[pl.ds(3, 2 * COMPS), pl.ds(y, 8)], ends.at[n, m], end_sems.at[n, m]
                )
            )
    for copy in copies:
        copy.start()
    table[...] = band_table(tiles)
    for copy in copies:
        copy.wait()
    for m, (tail, row) in enumerate(((tail_p, 0), (tail_n, 7))):
        tail[...] = jnp.zeros(tail.shape, F32)
        for n in range(2):
            for c in range(COMPS):
                to = n * COMPS + c
                tail[to // 8, to % 8 : to % 8 + 1, :] = ends[n, m, 2 * c + 1 - n, row : row + 1, :]
    flat = pad.reshape((CX + 6) * 2 * 48, LANES)
    for n, row in enumerate((5, 8 + CY)):
        for h in range(2):
            for k in range(3):
                for x in range(0, CX, 8):
                    rows = pl.ds(((x + 3) * 2 + h) * 48 + row + k, 8, stride=96)
                    flat[rows, :] = faces[n, k, x : x + 8, half(h)]

    def plane(x, with_x):
        for unit in range(CY // UNIT):
            rows = pl.ds(unit * UNIT, UNIT)
            for h in range(2):
                vx = speed[0, x, rows, half(h)].astype(F32) if with_x else None
                vy = speed[1, x, rows, half(h)].astype(F32)
                for part in range(UNIT // 8):
                    at = unit * UNIT + 8 * part
                    cut = slice(8 * part, 8 * part + 8)
                    total = drift[x, pl.ds(at, 8), half(h)]
                    if with_x:
                        total = total + derivative(along_x(pad, x + 3, h, at + 8, 8), vx[cut])
                    if at in (0, CY - 8):
                        total = total + derivative(along_y(pad, x + 3, h, at + 8, 8), vy[cut])
                    adv[x, pl.ds(at, 8), half(h)] = (
                        pad[x + 3, h, pl.ds(at + 8, 8), :] - TIME_STEP * total
                    )

    def inner(x, carry):
        plane(x, False)
        return carry

    def outer(x, carry):
        plane(x, True)
        plane(x + CX - 3, True)
        return carry

    lax.fori_loop(0, 3, outer, 0)
    lax.fori_loop(3, CX - 3, inner, 0, unroll=2)
    low, high = CX - DEEP, CX
    to_xp[0:DEEP] = adv[0:DEEP]
    to_xn[0:DEEP] = adv[low:high]
    row8 = lax.broadcasted_iota(jnp.int32, (8, LANES), 0)
    for h in range(2):
        for j in range(2):
            rows = pl.ds(j * TILE, TILE)
            for i, face in ((0, to_xp), (1, to_xn)):
                r = i * 4 + j * 2 + h
                face[DEEP, rows, half(h)] = jnp.broadcast_to(table[r : r + 1, :], (TILE, LANES))
        for i in range(2):
            first = table[i * 4 + h : i * 4 + h + 1, :]
            last = table[i * 4 + 2 + h : i * 4 + 3 + h, :]
            for x in range(i * TILE, i * TILE + TILE):
                to_yp[x, :, half(h)] = jnp.where(row8 == 7, first, adv[x, 0:8, half(h)])
                to_yn[x, :, half(h)] = jnp.where(row8 == 0, last, adv[x, CY - 8 : CY, half(h)])


def advect(tiles, level, xlo, xhi, ylo, yhi, speed, drift):
    shape = lambda *s: jax.ShapeDtypeStruct(s, F32)
    z = 2 * LANES
    return pl.pallas_call(
        advect_kernel,
        out_shape=[shape(CX, CY, z)]
        + [shape(8, CY, z)] * 2
        + [shape(CX, 8, z)] * 2
        + [shape(2, 8, z)] * 2,
        in_specs=[SMEM, ANY, ANY, ANY, ANY, ANY, VMEM, VMEM],
        out_specs=[VMEM] * 7,
        scratch_shapes=[
            pltpu.VMEM((CX + 6, 2, 48, LANES), F32),
            pltpu.VMEM((8, LANES), F32),
            pltpu.VMEM((2, 3, CX, z), F32),
            pltpu.VMEM((2, 2, 2 * COMPS, 8, z), F32),
            pltpu.SemaphoreType.DMA((2, 3)),
            pltpu.SemaphoreType.DMA((2,)),
            pltpu.SemaphoreType.DMA((2, 2)),
        ],
        compiler_params=pltpu.CompilerParams(vmem_limit_bytes=12 * MIB),
        name="advect",
    )(tiles, level, xlo, xhi, ylo, yhi, speed, drift)


WIDE = CX + 2 * DEEP
INNER = 48
SPLIT = 2


def sweep_rows(src, factor, x, fx, start, stride, groups, store):
    span = pl.ds if stride == 1 else functools.partial(pl.ds, stride=stride)
    rows = [span(start + k, 8) for k in range(-1, groups + 1)]
    lines = [[src[x, h, r, :] for r in rows] for h in range(2)]
    for k in range(1, groups + 1):
        center = [lines[h][k] for h in range(2)]
        up, down = lane_shift(center, 1), lane_shift(center, -1)
        for h in range(2):
            c = center[h]
            step = factor[fx, h, rows[k], :]
            positive = step > 0
            pairs = (
                (src[x - 1, h, rows[k], :], src[x + 1, h, rows[k], :]),
                (lines[h][k - 1], lines[h][k + 1]),
                (down[h], up[h]),
            )
            total = None
            for l, r in pairs:
                low = jnp.minimum(jnp.minimum(l, r), c)
                high = jnp.maximum(jnp.maximum(l, r), c)
                diff = c - jnp.where(positive, low, high)
                total = diff * diff if total is None else total + diff * diff
            slope = total * lax.rsqrt(jnp.maximum(total, 1e-36))
            store(h, rows[k], c - step * (slope - 1.0))


def band_step(value, band):
    square = value * value
    weight = band * recip(1.0 + square * (1.0 / 36.0))
    return PSEUDO_STEP * (value * lax.rsqrt(square + 1.0)) * weight, weight


def inner_sweeps(source, factor, targets, first):
    for n, target in enumerate(targets):
        sweep = first + n

        def body(x, carry, source=source, target=target):
            def store(h, rows, value):
                target[x, h, rows, :] = value

            sweep_rows(source, factor, x, x, 8, CY // 8, CY // 8, store)
            return carry

        lax.fori_loop(sweep, CX - sweep, body, 0, unroll=2)
        source = target


def inner_first_kernel(tiles, adv, done1, done2, factor, weight, own, table, sems):
    copies = [
        pltpu.make_async_copy(adv.at[:, :, half(h)], own.at[:, h, pl.ds(8, CY), :], sems.at[h])
        for h in range(2)
    ]
    for copy in copies:
        copy.start()
    table[...] = band_table(tiles)
    for copy in copies:
        copy.wait()
    for i in range(2):

        def body(x, carry, i=i):
            for h in range(2):
                for group in range(CY // 8):
                    rows = pl.ds(8 + 8 * group, 8)
                    r = i * 4 + (group // 2) * 2 + h
                    band = jnp.broadcast_to(table[r : r + 1, :], (8, LANES))
                    step, value = band_step(own[x, h, rows, :], band)
                    factor[x, h, rows, :] = step
                    weight[x, h, rows, :] = value
            return carry

        lax.fori_loop(i * TILE, (i + 1) * TILE, body, 0, unroll=2)
    inner_sweeps(own, factor, (done1, done2), 1)


def inner_second_kernel(before, factor, *done):
    inner_sweeps(before, factor, done, SPLIT + 1)


def inner_first(tiles, adv):
    return pl.pallas_call(
        inner_first_kernel,
        out_shape=[jax.ShapeDtypeStruct((CX, 2, INNER, LANES), F32)] * (SPLIT + 2),
        in_specs=[SMEM, ANY],
        out_specs=[VMEM] * (SPLIT + 2),
        scratch_shapes=[
            pltpu.VMEM((CX, 2, INNER, LANES), F32),
            pltpu.VMEM((8, LANES), F32),
            pltpu.SemaphoreType.DMA((2,)),
        ],
        compiler_params=pltpu.CompilerParams(vmem_limit_bytes=12 * MIB),
        cost_estimate=pl.CostEstimate(
            flops=100 * adv.size, bytes_accessed=24 * adv.size, transcendentals=4 * adv.size
        ),
        name="inner_first",
    )(tiles, adv)


def inner_second(before, factor):
    return pl.pallas_call(
        inner_second_kernel,
        out_shape=[jax.ShapeDtypeStruct((CX, 2, INNER, LANES), F32)] * (SWEEPS - SPLIT),
        in_specs=[VMEM] * 2,
        out_specs=[VMEM] * (SWEEPS - SPLIT),
        compiler_params=pltpu.CompilerParams(vmem_limit_bytes=12 * MIB),
        cost_estimate=pl.CostEstimate(
            flops=60 * factor.size, bytes_accessed=24 * factor.size, transcendentals=2 * factor.size
        ),
        name="inner_second",
    )(before, factor)


def sweep_kernel(
    adv, in1, in2, in3, in4, in5, own_factor, own_weight, xlo, xhi, ylo, yhi, clo, chi,
    cur_out, weight_out, part,
    buf0, buf1, buf2, buf3, buf4, factor, masks, sums, sems, x_sems,
):
    bufs = (buf0, buf1, buf2, buf3, buf4)
    copies = []
    done = []
    for h in range(2):
        pieces = (
            (adv, DEEP, CX, OWN, CY),
            (xlo.at[pl.ds(0, DEEP)], 0, DEEP, OWN, CY),
            (xhi.at[pl.ds(0, DEEP)], DEEP + CX, DEEP, OWN, CY),
            (ylo, DEEP, CX, OWN - 8, 8),
            (yhi, DEEP, CX, OWN + CY, 8),
            (clo.at[pl.ds(0, DEEP)], 0, DEEP, OWN - 8, 8),
            (clo.at[pl.ds(DEEP, DEEP)], DEEP + CX, DEEP, OWN - 8, 8),
            (chi.at[pl.ds(0, DEEP)], 0, DEEP, OWN + CY, 8),
            (chi.at[pl.ds(DEEP, DEEP)], DEEP + CX, DEEP, OWN + CY, 8),
        )
        for n, (src, x, nx, y, ny) in enumerate(pieces):
            copies.append(
                pltpu.make_async_copy(
                    src.at[:, :, half(h)],
                    buf0.at[pl.ds(x, nx), h, pl.ds(y, ny), :],
                    sems.at[h, n],
                )
            )
        for n, src in enumerate((xlo, xhi)):
            copies.append(
                pltpu.make_async_copy(
                    src.at[pl.ds(DEEP, 1), :, half(h)], masks.at[pl.ds(n, 1), h], sems.at[h, 9 + n]
                )
            )
    own = lambda ref, x: ref.at[pl.ds(x, CX), :, pl.ds(OWN, CY), :]
    for n, (src, dst) in enumerate(
        [(own_factor, own(factor, DEEP)), (own_weight, own(weight_out, 1))]
        + [(src, own(buf, DEEP)) for src, buf in zip((in1, in2, in3, in4), bufs[1:])]
        + [(in5, own(cur_out, 2))]
    ):
        done.append(pltpu.make_async_copy(src.at[:, :, pl.ds(8, CY), :], dst, x_sems.at[n]))
    for copy in copies + done:
        copy.start()
    sums[...] = jnp.zeros(sums.shape, F32)
    for copy in copies + done[:2]:
        copy.wait()

    def prepare(x, groups, bands, keep):
        for h in range(2):
            for group in groups:
                rows = pl.ds(OWN + 8 * group, 8)
                value = buf0[x, h, rows, :]
                if group == -1:
                    band = jnp.broadcast_to(value[0:1], value.shape)
                elif group == 4:
                    band = jnp.broadcast_to(value[7:8], value.shape)
                else:
                    band = masks[bands, h, pl.ds(8 * group, 8), :]
                step, weight = band_step(value, band)
                factor[x, h, rows, :] = step
                if keep:
                    weight_out[x - DEEP + 1, h, rows, :] = weight

    def run(start, stop, groups, bands, keep):
        def body(x, carry):
            prepare(x, groups, bands, keep)
            return carry

        lax.fori_loop(start, stop, body, 0, unroll=2)

    everything = tuple(range(-1, 5))
    run(1, DEEP - 1, everything, 0, False)
    prepare(DEEP - 1, everything, 0, True)
    run(DEEP, DEEP + CX, (-1, 4), 0, True)
    prepare(DEEP + CX, everything, 1, True)
    run(DEEP + CX + 1, WIDE - 1, everything, 1, False)

    for sweep in range(1, SWEEPS + 1):
        done[sweep + 1].wait()
        offset, target = (0, bufs[sweep]) if sweep < SWEEPS else (SWEEPS, cur_out)
        groups = 6 if DEEP - sweep > 4 else 5
        source = bufs[sweep - 1]

        def whole(x, source=source, target=target, offset=offset, groups=groups):
            def store(h, rows, value):
                target[x - offset, h, rows, :] = value

            start = OWN + CY // 2 - 4 * groups
            sweep_rows(source, factor, x, x, start, groups, groups, store)

        def ends(x, source=source, target=target, offset=offset, sweep=sweep):
            def store(h, rows, value):
                target[x - offset, h, rows, :] = value

            for start in (OWN + sweep - 8, OWN + CY - sweep):
                sweep_rows(source, factor, x, x, start, 1, 1, store)

        def outer(n, carry, whole=whole, sweep=sweep):
            whole(sweep + n)
            whole(WIDE - 1 - sweep - n)
            return carry

        def middle(x, carry, ends=ends):
            ends(x)
            return carry

        lax.fori_loop(0, DEEP, outer, 0)
        lax.fori_loop(DEEP + sweep, DEEP + CX - sweep, middle, 0, unroll=2)

    def count(x, carry):
        for h in range(2):
            for unit in range(CY // UNIT):
                rows = pl.ds(OWN + unit * UNIT, UNIT)
                after = jnp.tanh(cur_out[x + 2, h, rows, :])
                before = jnp.tanh(buf0[x + DEEP, h, rows, :])
                sums[0] += after - before
                sums[1] += 1.0 - after * after
        return carry

    lax.fori_loop(0, CX, count, 0, unroll=2)
    lane = lax.broadcasted_iota(jnp.int32, (1, LANES), 1)
    sums_row = jnp.where(lane < 64, jnp.sum(sums[0]), jnp.sum(sums[1]))
    part[...] = jnp.broadcast_to(sums_row, part.shape)


def sweeps(adv, inner, factor, weight, halos, count):
    shape = lambda *s: jax.ShapeDtypeStruct(s, F32)
    return pl.pallas_call(
        sweep_kernel,
        out_shape=[
            shape(CX + 4, 2, ROWS, LANES), shape(CX + 2, 2, ROWS, LANES), shape(count, 1, LANES)
        ],
        in_specs=[ANY] * (SWEEPS + 9),
        out_specs=[VMEM] * 3,
        scratch_shapes=[pltpu.VMEM((WIDE, 2, ROWS, LANES), F32)] * SWEEPS
        + [
            pltpu.VMEM((WIDE, 2, ROWS, LANES), F32),
            pltpu.VMEM((2, 2, CY, LANES), F32),
            pltpu.VMEM((2, UNIT, LANES), F32),
            pltpu.SemaphoreType.DMA((2, 11)),
            pltpu.SemaphoreType.DMA((2 + SWEEPS,)),
        ],
        compiler_params=pltpu.CompilerParams(vmem_limit_bytes=30 * MIB),
        name="sweeps",
    )(adv, *inner, factor, weight, *halos)


CHUNKS = ((0, 10), (10, 18), (18, 26), (26, 32))


def extend_kernel(
    parts, cur, weight, stress, xlo, xhi, ylo, yhi, clo, chi,
    level_out, stress_out,
    pad, ring0, ring1, ring2, ring3, mix0, mix1, stage, sems, x_sems, out_sems,
):
    ring, mix = (ring0, ring1, ring2, ring3), (mix0, mix1)

    def chunk(n):
        start, stop = CHUNKS[n]
        own = stress.at[:, pl.ds(start, stop - start)]
        copies = [
            pltpu.make_async_copy(
                own.at[:, :, :, half(h)],
                pad.at[:, pl.ds(start + 2, stop - start), h, pl.ds(OWN, CY), :],
                sems.at[n, h],
            )
            for h in range(2)
        ]
        for side, src in ((0, xlo), (3, xhi)):
            if n == side:
                at = 0 if n == 0 else CX + 2
                for h in range(2):
                    for c in range(COMPS):
                        copies.append(
                            pltpu.make_async_copy(
                                src.at[pl.ds(3 + 2 * c, 2), :, half(h)],
                                pad.at[c, pl.ds(at, 2), h, pl.ds(OWN, CY), :],
                                x_sems.at[side % 2, h, c],
                            )
                        )
        return copies

    chunks = [chunk(n) for n in range(len(CHUNKS))]
    for copies in chunks:
        for copy in copies:
            copy.start()
    sums = jnp.sum(parts[...], axis=0)
    shift = sums[:, 0:1] / sums[:, 64:65]
    flat = pad.reshape(COMPS, (CX + 4) * 2 * ROWS, LANES)
    for h in range(2):
        for c in range(COMPS):
            for face, row in ((ylo, OWN - 2), (yhi, OWN + CY)):
                for k in range(2):
                    for x in range(0, CX, 8):
                        at = ((x + 2) * 2 + h) * ROWS + row + k
                        flat[c, pl.ds(at, 8, stride=2 * ROWS), :] = face[
                            2 * c + k, x : x + 8, half(h)
                        ]
            for corner, row in ((clo, OWN - 1), (chi, OWN + CY)):
                for x, n in ((1, c), (CX + 2, COMPS + c)):
                    at = 2 * DEEP + n // 8
                    pad[c, x, h, row : row + 1, :] = corner[at, n % 8 : n % 8 + 1, half(h)]

    def blend(mixes, center, around):
        value = mixes[6] * center
        for n in range(6):
            value = value + mixes[n] * around[n]
        return value

    def neighbours(load, groups):
        start = OWN + CY // 2 - 4 * groups
        for k in range(groups):
            rows, below, above = (pl.ds(start + k + d, 8, stride=groups) for d in (0, -1, 1))
            center = [load(0, h, rows) for h in range(2)]
            up, down = lane_shift(center, 1), lane_shift(center, -1)
            yield rows, center, [
                [
                    load(-1, h, rows), load(1, h, rows), load(0, h, below), load(0, h, above),
                    down[h], up[h],
                ]
                for h in range(2)
            ]

    def first_step(i, slot, groups=5):
        levels = neighbours(lambda dx, h, r: cur[i + 1 + dx, h, r, :] * DOUBLED, groups)
        comps = [
            neighbours(lambda dx, h, r, c=c: pad[c, i + 1 + dx, h, r, :], groups)
            for c in range(COMPS)
        ]
        for rows, center, around in levels:
            mixes = []
            for h in range(2):
                c = center[h]
                w = [recip(1.0 + jnp.exp2(jnp.minimum(n - c, 125.5))) for n in around[h]]
                total = w[0] + w[1] + w[2] + w[3] + w[4] + w[5]
                gate = weight[i, h, rows, :] * 0.5 * (
                    1.0 + jnp.tanh(c * (2.0 / DOUBLED) - 2.0 * shift)
                )
                scaled = gate * recip(total)
                w = [scaled * n for n in w] + [1.0 - gate]
                mixes.append(w)
                for n in range(7):
                    mix[slot % 2][n, h, rows, :] = w[n]
            for comp in range(COMPS):
                _, center, around = next(comps[comp])
                for h in range(2):
                    ring[slot][comp, h, rows, :] = blend(mixes[h], center[h], around[h])

    def second_step(x, slot):
        slots = {dx: (slot + dx) % 4 for dx in (-1, 0, 1)}
        groups = CY // 8
        comps = [
            neighbours(lambda dx, h, r, c=c: ring[slots[dx]][c, h, r, :], groups)
            for c in range(COMPS)
        ]
        for k in range(groups):
            rows = pl.ds(OWN + k, 8, stride=groups)
            mixes = [[mix[slot % 2][n, h, rows, :] for n in range(7)] for h in range(2)]
            for comp in range(COMPS):
                _, center, around = next(comps[comp])
                for h in range(2):
                    stage[comp, x, h, pl.ds(k, 8, stride=groups), :] = blend(
                        mixes[h], center[h], around[h]
                    )
        for h in range(2):
            level_out[x, :, half(h)] = cur[x + 2, h, OWN : OWN + CY, :] - shift

    outs = []
    for n in range(len(CHUNKS)):
        for copy in chunks[n]:
            copy.wait()
        if n == 0:
            first_step(0, 0, groups=4)
            first_step(1, 1)

        def body(group, carry):
            for k in range(4):
                i = group * 4 + k + 2
                first_step(i, (k + 2) % 4)
                second_step(i - 2, (k + 1) % 4)
            return carry

        lax.fori_loop(2 * n, 2 * n + 2, body, 0)
        planes = pl.ds(8 * n, 8)
        for h in range(2):
            copy = pltpu.make_async_copy(
                stage.at[:, planes, h], stress_out.at[:, planes, :, half(h)], out_sems.at[n, h]
            )
            copy.start()
            outs.append(copy)
    for copy in outs:
        copy.wait()


def extend(parts, cur, weight, stress, halos):
    shape = lambda *s: jax.ShapeDtypeStruct(s, F32)
    z = 2 * LANES
    return pl.pallas_call(
        extend_kernel,
        out_shape=[shape(CX, CY, z), shape(COMPS, CX, CY, z)],
        in_specs=[VMEM, VMEM, VMEM, ANY, ANY, ANY, VMEM, VMEM, VMEM, VMEM],
        out_specs=[VMEM, ANY],
        scratch_shapes=[
            pltpu.VMEM((COMPS, CX + 4, 2, ROWS, LANES), F32),
            *[pltpu.VMEM((COMPS, 2, ROWS, LANES), F32)] * 4,
            *[pltpu.VMEM((7, 2, ROWS, LANES), F32)] * 2,
            pltpu.VMEM((COMPS, CX, 2, CY, LANES), F32),
            pltpu.SemaphoreType.DMA((4, 2)),
            pltpu.SemaphoreType.DMA((2, 2, COMPS)),
            pltpu.SemaphoreType.DMA((4, 2)),
        ],
        compiler_params=pltpu.CompilerParams(vmem_limit_bytes=46 * MIB),
        name="extend",
    )(parts, cur, weight, stress, *halos)


def on_device(level, velocity, stress, tiles):
    nx, ny = lax.axis_size("gx"), lax.axis_size("gy")

    def send(value, dx, dy):
        if dy == 0:
            return lax.ppermute(value, "gx", [(i, (i + dx) % nx) for i in range(nx)])
        if dx == 0:
            return lax.ppermute(value, "gy", [(i, (i + dy) % ny) for i in range(ny)])
        pairs = [
            (i * ny + j, (i + dx) % nx * ny + (j + dy) % ny) for i in range(nx) for j in range(ny)
        ]
        return lax.ppermute(value, ("gx", "gy"), pairs)

    to_xp, to_xn, to_yp, to_yn, to_syp, to_syn = cut(level, stress)
    xlo, xhi = send(to_xn, 1, 0), send(to_xp, -1, 0)
    ylo, yhi = send(to_yn, 0, 1), send(to_yp, 0, -1)
    drift = inner_drift(level, velocity)
    adv, to_xp, to_xn, to_yp, to_yn, tail_p, tail_n = advect(
        tiles, level, xlo, xhi, ylo, yhi, velocity, drift
    )
    axlo, axhi = send(to_xn, 1, 0), send(to_xp, -1, 0)
    aylo, ayhi = send(to_yn, 0, 1), send(to_yp, 0, -1)
    row = lax.broadcasted_iota(jnp.int32, (1, 8, 1), 1)

    def corners(rows, mark, tail):
        faces = [jnp.where(row == mark, f[DEEP:, rows], f[:DEEP, rows]) for f in (axlo, axhi)]
        return jnp.concatenate(faces + [tail], axis=0)

    *inner, factor, weight = inner_first(tiles, adv)
    last, axlo, axhi = lax.optimization_barrier((inner[-1], axlo, axhi))
    more = inner_second(last, factor)
    clo = send(corners(slice(-8, None), 0, tail_n), 0, 1)
    chi = send(corners(slice(0, 8), 7, tail_p), 0, -1)
    to_syp, to_syn, aylo, ayhi, clo, chi, more = lax.optimization_barrier(
        (to_syp, to_syn, aylo, ayhi, clo, chi, more)
    )
    sylo, syhi = send(to_syn, 0, 1), send(to_syp, 0, -1)
    cur, weight, part = sweeps(
        adv, (*inner, *more), factor, weight, (axlo, axhi, aylo, ayhi, clo, chi), nx * ny
    )
    parts = lax.all_to_all(part, ("gx", "gy"), 0, 0, tiled=True)
    return extend(parts, cur, weight, stress, (xlo, xhi, sylo, syhi, clo, chi))


def solution(mesh):
    in_specs = (
        P("gx", "gy", None),
        P(None, "gx", "gy", None),
        P(None, "gx", "gy", None),
        P("gx", "gy", None),
    )
    out_specs = (P("gx", "gy", None), P(None, "gx", "gy", None))
    return jax.shard_map(
        on_device, mesh=mesh, in_specs=in_specs, out_specs=out_specs, check_vma=False
    )
```

```python
import functools

import jax
import jax.numpy as jnp
from jax import lax
from jax.experimental import pallas as pl
from jax.experimental.pallas import tpu as pltpu
from jax.sharding import PartitionSpec as P

TILE = 16
SWEEPS = 5
EPSILON = 1e-06
TIME_STEP = 0.4
PSEUDO_STEP = 0.3

CX = 32
CY = 32
LANES = 128
DEEP = 7
ROWS = 64
OWN = 16
UNIT = 16
COMPS = 6
F32 = jnp.float32
DOUBLED = 2.0 * 1.4426950408889634
MIB = 1024 * 1024
ANY = pl.BlockSpec(memory_space=pl.ANY)
VMEM = pl.BlockSpec(memory_space=pltpu.VMEM)
SMEM = pl.BlockSpec(memory_space=pltpu.SMEM)


def half(h):
    return pl.ds(h * LANES, LANES)


def recip(x):
    return pl.reciprocal(x, approx=True)


def lane_shift(pair, k):
    lane = lax.broadcasted_iota(jnp.int32, pair[0].shape, pair[0].ndim - 1)
    turned = [pltpu.roll(p, (-k) % LANES, p.ndim - 1) for p in pair]
    edge = lane >= LANES - k if k > 0 else lane < -k
    return [jnp.where(edge, turned[1 - h], turned[h]) for h in range(2)]


def weno(d, positive):
    v = [jnp.where(positive, d[k], d[5 - k]) for k in range(5)]
    d1, d2, d3, d4 = (v[k + 1] - v[k] for k in range(4))
    u1, u2, u3 = d2 - d1, d3 - d2, d4 - d3
    g1 = d2 + d2 + u1
    g2 = d2 + d3
    g3 = u3 - (d3 + d3)
    scale = 13.0 / 3.0
    a1 = recip(4.0 * EPSILON + (scale * u1 * u1 + g1 * g1))
    a2 = recip(4.0 * EPSILON + (scale * u2 * u2 + g2 * g2))
    a3 = recip(4.0 * EPSILON + (scale * u3 * u3 + g3 * g3))
    a1 = a1 * a1
    a2 = 6.0 * (a2 * a2)
    a3 = 3.0 * (a3 * a3)
    top = a1 * (u1 - u2) + 0.5 * (a3 * (u2 - u3))
    mid = v[2] + (d3 + d3 + d2) * (1.0 / 6.0)
    return mid + top * (recip(a1 + a2 + a3) * (1.0 / 3.0))


def band_table(tiles_ref):
    shape = (8, LANES)
    row = lax.broadcasted_iota(jnp.int32, shape, 0)
    lane = lax.broadcasted_iota(jnp.int32, shape, 1)
    numbers = (row // 2) * 16 + (row % 2) * 8 + lane // TILE
    flags = jnp.zeros(shape, F32)
    for slot in range(tiles_ref.shape[-1]):
        flags = jnp.where(numbers == tiles_ref[0, 0, slot], 1.0, flags)
    return flags


def derivative(line, speed):
    return speed * weno([line[k + 1] - line[k] for k in range(6)], speed > 0)


def along_x(pad, x, h, at, size):
    return [pad[x + k, h, pl.ds(at, size), :] for k in range(-3, 4)]


def along_y(pad, x, h, at, size):
    return [pad[x, h, pl.ds(at + k, size), :] for k in range(-3, 4)]


def cut_kernel(
    level, stress, to_xp, to_xn, to_yp, to_yn, to_syp, to_syn, faces, x_sems, y_sems
):
    copies = []
    for n, (out, at) in enumerate(((to_xp, 0), (to_xn, CX))):
        deep = lambda size: pl.ds(at and at - size, size)
        copies.append(pltpu.make_async_copy(level.at[deep(3)], out.at[pl.ds(0, 3)], x_sems.at[n, 0]))
        for c in range(COMPS):
            copies.append(
                pltpu.make_async_copy(
                    stress.at[c, deep(2)], out.at[pl.ds(3 + 2 * c, 2)], x_sems.at[n, 1 + c]
                )
            )
    for copy in copies:
        copy.start()
    sides = []
    for n, y in enumerate((0, CY - 8)):
        side = []
        for h in range(2):
            for m in range(1 + COMPS):
                src = stress.at[m - 1] if m else level
                side.append(
                    pltpu.make_async_copy(
                        src.at[:, pl.ds(y, 8), half(h)], faces.at[m, n, h], y_sems.at[m, n, h]
                    )
                )
        for copy in side:
            copy.start()
        sides.append(side)
    flat = faces.reshape(1 + COMPS, 2, 2, CX * 8, LANES)
    for n, outs in enumerate(((to_yp, to_syp), (to_yn, to_syn))):
        for copy in sides[n]:
            copy.wait()
        for h in range(2):
            for m in range(1 + COMPS):
                depth = 2 if m else 3
                out = outs[min(m, 1)]
                first = 2 * m - 2 if m else 0
                for k in range(depth):
                    row = k if n == 0 else 8 - depth + k
                    for x in range(0, CX, 8):
                        out[first + k, x : x + 8, half(h)] = flat[
                            m, n, h, pl.ds(8 * x + row, 8, stride=8), :
                        ]
    for copy in copies:
        copy.wait()


def cut(level, stress):
    message = lambda planes: jax.ShapeDtypeStruct((planes, CX, 2 * LANES), F32)
    return pl.pallas_call(
        cut_kernel,
        out_shape=[message(3 + 2 * COMPS)] * 2 + [message(3)] * 2 + [message(2 * COMPS)] * 2,
        in_specs=[ANY] * 2,
        out_specs=[VMEM] * 6,
        scratch_shapes=[
            pltpu.VMEM((1 + COMPS, 2, 2, CX, 8, LANES), F32),
            pltpu.SemaphoreType.DMA((2, 1 + COMPS)),
            pltpu.SemaphoreType.DMA((1 + COMPS, 2, 2)),
        ],
        compiler_params=pltpu.CompilerParams(vmem_limit_bytes=57 * MIB),
        name="cut",
    )(level, stress)


def inner_kernel(level, speed, drift, pad, sems):
    copies = [
        pltpu.make_async_copy(level.at[:, :, half(h)], pad.at[:, h], sems.at[h]) for h in range(2)
    ]
    for copy in copies:
        copy.start()
    for copy in copies:
        copy.wait()

    def plane(x, with_x):
        for unit in range(CY // UNIT):
            rows = pl.ds(unit * UNIT, UNIT)
            v = [[speed[d, x, rows, half(h)].astype(F32) for h in range(2)] for d in range(3)]
            for part in range(UNIT // 8):
                at = unit * UNIT + 8 * part
                cut = slice(8 * part, 8 * part + 8)
                center = [pad[x, h, pl.ds(at, 8), :] for h in range(2)]
                ups = [lane_shift(center, k) for k in (1, 2, 3)]
                downs = [lane_shift(center, -k) for k in (3, 2, 1)]
                for h in range(2):
                    line = [s[h] for s in downs] + [center[h]] + [s[h] for s in ups]
                    total = derivative(line, v[2][h][cut])
                    if with_x:
                        total = total + derivative(along_x(pad, x, h, at, 8), v[0][h][cut])
                    if 8 <= at < CY - 8:
                        total = total + derivative(along_y(pad, x, h, at, 8), v[1][h][cut])
                    drift[x, pl.ds(at, 8), half(h)] = total

    def inner(x, carry):
        plane(x, True)
        return carry

    def outer(x, carry):
        plane(x, False)
        plane(x + CX - 3, False)
        return carry

    lax.fori_loop(0, 3, outer, 0)
    lax.fori_loop(3, CX - 3, inner, 0, unroll=2)


def inner_drift(level, speed):
    return pl.pallas_call(
        inner_kernel,
        out_shape=jax.ShapeDtypeStruct(level.shape, F32),
        in_specs=[ANY, VMEM],
        out_specs=VMEM,
        scratch_shapes=[
            pltpu.VMEM((CX, 2, CY, LANES), F32),
            pltpu.SemaphoreType.DMA((2,)),
        ],
        compiler_params=pltpu.CompilerParams(vmem_limit_bytes=10 * MIB),
        cost_estimate=pl.CostEstimate(
            flops=180 * level.size, bytes_accessed=14 * level.size, transcendentals=9 * level.size
        ),
        name="inner_drift",
    )(level, speed)


def advect_kernel(
    tiles, level, xlo, xhi, ylo, yhi, speed, drift, stress_p, stress_n,
    adv, to_xp, to_xn, to_yp, to_yn, tail_p, tail_n,
    pad, table, faces, ends, sems, y_sems, end_sems, ride_sems,
):
    riders = [
        pltpu.make_async_copy(src, out.at[pl.ds(CX, 8 * COMPS)], ride_sems.at[n])
        for n, (src, out) in enumerate(((stress_p, to_yp), (stress_n, to_yn)))
    ]
    copies = []
    for h in range(2):
        for n, (src, at, size) in enumerate(((level, 3, CX), (xlo, 0, 3), (xhi, CX + 3, 3))):
            copies.append(
                pltpu.make_async_copy(
                    src.at[pl.ds(0, size), :, half(h)],
                    pad.at[pl.ds(at, size), h, pl.ds(8, CY), :],
                    sems.at[h, n],
                )
            )
    for n, src in enumerate((ylo, yhi)):
        copies.append(pltpu.make_async_copy(src, faces.at[n], y_sems.at[n]))
    for n, src in enumerate((xlo, xhi)):
        for m, y in enumerate((0, CY - 8)):
            copies.append(
                pltpu.make_async_copy(
                    src.at[pl.ds(3, 2 * COMPS), pl.ds(y, 8)], ends.at[n, m], end_sems.at[n, m]
                )
            )
    for copy in copies + riders:
        copy.start()
    table[...] = band_table(tiles)
    for copy in copies:
        copy.wait()
    for m, (tail, row) in enumerate(((tail_p, 0), (tail_n, 7))):
        tail[...] = jnp.zeros(tail.shape, F32)
        for n in range(2):
            for c in range(COMPS):
                to = n * COMPS + c
                tail[to // 8, to % 8 : to % 8 + 1, :] = ends[n, m, 2 * c + 1 - n, row : row + 1, :]
    flat = pad.reshape((CX + 6) * 2 * 48, LANES)
    for n, row in enumerate((5, 8 + CY)):
        for h in range(2):
            for k in range(3):
                for x in range(0, CX, 8):
                    rows = pl.ds(((x + 3) * 2 + h) * 48 + row + k, 8, stride=96)
                    flat[rows, :] = faces[n, k, x : x + 8, half(h)]

    def plane(x, with_x):
        for unit in range(CY // UNIT):
            rows = pl.ds(unit * UNIT, UNIT)
            for h in range(2):
                vx = speed[0, x, rows, half(h)].astype(F32) if with_x else None
                vy = speed[1, x, rows, half(h)].astype(F32)
                for part in range(UNIT // 8):
                    at = unit * UNIT + 8 * part
                    cut = slice(8 * part, 8 * part + 8)
                    total = drift[x, pl.ds(at, 8), half(h)]
                    if with_x:
                        total = total + derivative(along_x(pad, x + 3, h, at + 8, 8), vx[cut])
                    if at in (0, CY - 8):
                        total = total + derivative(along_y(pad, x + 3, h, at + 8, 8), vy[cut])
                    adv[x, pl.ds(at, 8), half(h)] = (
                        pad[x + 3, h, pl.ds(at + 8, 8), :] - TIME_STEP * total
                    )

    def inner(x, carry):
        plane(x, False)
        return carry

    def outer(x, carry):
        plane(x, True)
        plane(x + CX - 3, True)
        return carry

    lax.fori_loop(0, 3, outer, 0)
    lax.fori_loop(3, CX - 3, inner, 0, unroll=2)
    low, high = CX - DEEP, CX
    to_xp[0:DEEP] = adv[0:DEEP]
    to_xn[0:DEEP] = adv[low:high]
    row8 = lax.broadcasted_iota(jnp.int32, (8, LANES), 0)
    for h in range(2):
        for j in range(2):
            rows = pl.ds(j * TILE, TILE)
            for i, face in ((0, to_xp), (1, to_xn)):
                r = i * 4 + j * 2 + h
                face[DEEP, rows, half(h)] = jnp.broadcast_to(table[r : r + 1, :], (TILE, LANES))
        for i in range(2):
            first = table[i * 4 + h : i * 4 + h + 1, :]
            last = table[i * 4 + 2 + h : i * 4 + 3 + h, :]
            for x in range(i * TILE, i * TILE + TILE):
                to_yp[x, :, half(h)] = jnp.where(row8 == 7, first, adv[x, 0:8, half(h)])
                to_yn[x, :, half(h)] = jnp.where(row8 == 0, last, adv[x, CY - 8 : CY, half(h)])
    for copy in riders:
        copy.wait()


def advect(tiles, level, xlo, xhi, ylo, yhi, speed, drift, stress_p, stress_n):
    shape = lambda *s: jax.ShapeDtypeStruct(s, F32)
    z = 2 * LANES
    return pl.pallas_call(
        advect_kernel,
        out_shape=[shape(CX, CY, z)]
        + [shape(8, CY, z)] * 2
        + [shape(CX + 8 * COMPS, 8, z)] * 2
        + [shape(2, 8, z)] * 2,
        in_specs=[SMEM, ANY, ANY, ANY, ANY, ANY, VMEM, VMEM, ANY, ANY],
        out_specs=[VMEM] * 7,
        scratch_shapes=[
            pltpu.VMEM((CX + 6, 2, 48, LANES), F32),
            pltpu.VMEM((8, LANES), F32),
            pltpu.VMEM((2, 3, CX, z), F32),
            pltpu.VMEM((2, 2, 2 * COMPS, 8, z), F32),
            pltpu.SemaphoreType.DMA((2, 3)),
            pltpu.SemaphoreType.DMA((2,)),
            pltpu.SemaphoreType.DMA((2, 2)),
            pltpu.SemaphoreType.DMA((2,)),
        ],
        compiler_params=pltpu.CompilerParams(vmem_limit_bytes=12 * MIB),
        name="advect",
    )(tiles, level, xlo, xhi, ylo, yhi, speed, drift, stress_p, stress_n)


WIDE = CX + 2 * DEEP
INNER = 48
SPLIT = 2


def sweep_rows(src, factor, x, fx, start, stride, groups, store):
    span = pl.ds if stride == 1 else functools.partial(pl.ds, stride=stride)
    rows = [span(start + k, 8) for k in range(-1, groups + 1)]
    lines = [[src[x, h, r, :] for r in rows] for h in range(2)]
    for k in range(1, groups + 1):
        center = [lines[h][k] for h in range(2)]
        up, down = lane_shift(center, 1), lane_shift(center, -1)
        for h in range(2):
            c = center[h]
            step = factor[fx, h, rows[k], :]
            positive = step > 0
            pairs = (
                (src[x - 1, h, rows[k], :], src[x + 1, h, rows[k], :]),
                (lines[h][k - 1], lines[h][k + 1]),
                (down[h], up[h]),
            )
            total = None
            for l, r in pairs:
                low = jnp.minimum(jnp.minimum(l, r), c)
                high = jnp.maximum(jnp.maximum(l, r), c)
                diff = c - jnp.where(positive, low, high)
                total = diff * diff if total is None else total + diff * diff
            slope = total * lax.rsqrt(jnp.maximum(total, 1e-36))
            store(h, rows[k], c - step * (slope - 1.0))


def band_step(value, band):
    square = value * value
    weight = band * recip(1.0 + square * (1.0 / 36.0))
    return PSEUDO_STEP * (value * lax.rsqrt(square + 1.0)) * weight, weight


def inner_sweeps(source, factor, targets, first):
    for n, target in enumerate(targets):
        sweep = first + n

        def body(x, carry, source=source, target=target):
            def store(h, rows, value):
                target[x, h, rows, :] = value

            sweep_rows(source, factor, x, x, 8, CY // 8, CY // 8, store)
            return carry

        lax.fori_loop(sweep, CX - sweep, body, 0, unroll=2)
        source = target


def inner_first_kernel(tiles, adv, done1, done2, factor, weight, own, table, sems):
    copies = [
        pltpu.make_async_copy(adv.at[:, :, half(h)], own.at[:, h, pl.ds(8, CY), :], sems.at[h])
        for h in range(2)
    ]
    for copy in copies:
        copy.start()
    table[...] = band_table(tiles)
    for copy in copies:
        copy.wait()
    for i in range(2):

        def body(x, carry, i=i):
            for h in range(2):
                for group in range(CY // 8):
                    rows = pl.ds(8 + 8 * group, 8)
                    r = i * 4 + (group // 2) * 2 + h
                    band = jnp.broadcast_to(table[r : r + 1, :], (8, LANES))
                    step, value = band_step(own[x, h, rows, :], band)
                    factor[x, h, rows, :] = step
                    weight[x, h, rows, :] = value
            return carry

        lax.fori_loop(i * TILE, (i + 1) * TILE, body, 0, unroll=2)
    inner_sweeps(own, factor, (done1, done2), 1)


def inner_second_kernel(before, factor, *done):
    inner_sweeps(before, factor, done, SPLIT + 1)


def inner_first(tiles, adv):
    return pl.pallas_call(
        inner_first_kernel,
        out_shape=[jax.ShapeDtypeStruct((CX, 2, INNER, LANES), F32)] * (SPLIT + 2),
        in_specs=[SMEM, ANY],
        out_specs=[VMEM] * (SPLIT + 2),
        scratch_shapes=[
            pltpu.VMEM((CX, 2, INNER, LANES), F32),
            pltpu.VMEM((8, LANES), F32),
            pltpu.SemaphoreType.DMA((2,)),
        ],
        compiler_params=pltpu.CompilerParams(vmem_limit_bytes=12 * MIB),
        cost_estimate=pl.CostEstimate(
            flops=100 * adv.size, bytes_accessed=24 * adv.size, transcendentals=4 * adv.size
        ),
        name="inner_first",
    )(tiles, adv)


def inner_second(before, factor):
    return pl.pallas_call(
        inner_second_kernel,
        out_shape=[jax.ShapeDtypeStruct((CX, 2, INNER, LANES), F32)] * (SWEEPS - SPLIT),
        in_specs=[VMEM] * 2,
        out_specs=[VMEM] * (SWEEPS - SPLIT),
        compiler_params=pltpu.CompilerParams(vmem_limit_bytes=12 * MIB),
        cost_estimate=pl.CostEstimate(
            flops=60 * factor.size, bytes_accessed=24 * factor.size, transcendentals=2 * factor.size
        ),
        name="inner_second",
    )(before, factor)


def sweep_kernel(
    adv, in1, in2, in3, in4, in5, own_factor, own_weight, xlo, xhi, ylo, yhi, clo, chi,
    cur_out, weight_out, part,
    buf0, buf1, buf2, buf3, buf4, factor, masks, sums, sems, x_sems,
):
    bufs = (buf0, buf1, buf2, buf3, buf4)
    copies = []
    done = []
    for h in range(2):
        pieces = (
            (adv, DEEP, CX, OWN, CY),
            (xlo.at[pl.ds(0, DEEP)], 0, DEEP, OWN, CY),
            (xhi.at[pl.ds(0, DEEP)], DEEP + CX, DEEP, OWN, CY),
            (ylo.at[pl.ds(0, CX)], DEEP, CX, OWN - 8, 8),
            (yhi.at[pl.ds(0, CX)], DEEP, CX, OWN + CY, 8),
            (clo.at[pl.ds(0, DEEP)], 0, DEEP, OWN - 8, 8),
            (clo.at[pl.ds(DEEP, DEEP)], DEEP + CX, DEEP, OWN - 8, 8),
            (chi.at[pl.ds(0, DEEP)], 0, DEEP, OWN + CY, 8),
            (chi.at[pl.ds(DEEP, DEEP)], DEEP + CX, DEEP, OWN + CY, 8),
        )
        for n, (src, x, nx, y, ny) in enumerate(pieces):
            copies.append(
                pltpu.make_async_copy(
                    src.at[:, :, half(h)],
                    buf0.at[pl.ds(x, nx), h, pl.ds(y, ny), :],
                    sems.at[h, n],
                )
            )
        for n, src in enumerate((xlo, xhi)):
            copies.append(
                pltpu.make_async_copy(
                    src.at[pl.ds(DEEP, 1), :, half(h)], masks.at[pl.ds(n, 1), h], sems.at[h, 9 + n]
                )
            )
    own = lambda ref, x: ref.at[pl.ds(x, CX), :, pl.ds(OWN, CY), :]
    for n, (src, dst) in enumerate(
        [(own_factor, own(factor, DEEP)), (own_weight, own(weight_out, 1))]
        + [(src, own(buf, DEEP)) for src, buf in zip((in1, in2, in3, in4), bufs[1:])]
        + [(in5, own(cur_out, 2))]
    ):
        done.append(pltpu.make_async_copy(src.at[:, :, pl.ds(8, CY), :], dst, x_sems.at[n]))
    for copy in copies + done[:1]:
        copy.start()
    sums[...] = jnp.zeros(sums.shape, F32)
    for copy in copies + done[:1]:
        copy.wait()
    for copy in done[2:] + done[1:2]:
        copy.start()

    def prepare(x, groups, bands, keep):
        for h in range(2):
            for group in groups:
                rows = pl.ds(OWN + 8 * group, 8)
                value = buf0[x, h, rows, :]
                if group == -1:
                    band = jnp.broadcast_to(value[0:1], value.shape)
                elif group == 4:
                    band = jnp.broadcast_to(value[7:8], value.shape)
                else:
                    band = masks[bands, h, pl.ds(8 * group, 8), :]
                step, weight = band_step(value, band)
                factor[x, h, rows, :] = step
                if keep:
                    weight_out[x - DEEP + 1, h, rows, :] = weight

    def run(start, stop, groups, bands, keep):
        def body(x, carry):
            prepare(x, groups, bands, keep)
            return carry

        lax.fori_loop(start, stop, body, 0, unroll=2)

    everything = tuple(range(-1, 5))
    run(1, DEEP - 1, everything, 0, False)
    prepare(DEEP - 1, everything, 0, True)
    run(DEEP, DEEP + CX, (-1, 4), 0, True)
    prepare(DEEP + CX, everything, 1, True)
    run(DEEP + CX + 1, WIDE - 1, everything, 1, False)

    for sweep in range(1, SWEEPS + 1):
        done[sweep + 1].wait()
        offset, target = (0, bufs[sweep]) if sweep < SWEEPS else (SWEEPS, cur_out)
        groups = 6 if DEEP - sweep > 4 else 5
        source = bufs[sweep - 1]

        def whole(x, source=source, target=target, offset=offset, groups=groups):
            def store(h, rows, value):
                target[x - offset, h, rows, :] = value

            start = OWN + CY // 2 - 4 * groups
            sweep_rows(source, factor, x, x, start, groups, groups, store)

        def ends(x, source=source, target=target, offset=offset, sweep=sweep):
            def store(h, rows, value):
                target[x - offset, h, rows, :] = value

            for start in (OWN + sweep - 8, OWN + CY - sweep):
                sweep_rows(source, factor, x, x, start, 1, 1, store)

        def outer(n, carry, whole=whole, sweep=sweep):
            whole(sweep + n)
            whole(WIDE - 1 - sweep - n)
            return carry

        def middle(x, carry, ends=ends):
            ends(x)
            return carry

        lax.fori_loop(0, DEEP, outer, 0)
        count_x = CX - 2 * sweep
        at_once = max(k for k in range(2, 14) if count_x % k == 0)
        lax.fori_loop(DEEP + sweep, DEEP + CX - sweep, middle, 0, unroll=at_once)

    def count(x, carry):
        for h in range(2):
            for unit in range(CY // UNIT):
                rows = pl.ds(OWN + unit * UNIT, UNIT)
                after = jnp.tanh(cur_out[x + 2, h, rows, :])
                before = jnp.tanh(buf0[x + DEEP, h, rows, :])
                sums[0] += after - before
                sums[1] += 1.0 - after * after
        return carry

    lax.fori_loop(0, CX, count, 0, unroll=2)
    done[1].wait()
    lane = lax.broadcasted_iota(jnp.int32, (1, LANES), 1)
    sums_row = jnp.where(lane < 64, jnp.sum(sums[0]), jnp.sum(sums[1]))
    part[...] = jnp.broadcast_to(sums_row, part.shape)


def sweeps(adv, inner, factor, weight, halos, count):
    shape = lambda *s: jax.ShapeDtypeStruct(s, F32)
    return pl.pallas_call(
        sweep_kernel,
        out_shape=[
            shape(CX + 4, 2, ROWS, LANES), shape(CX + 2, 2, ROWS, LANES), shape(count, 1, LANES)
        ],
        in_specs=[ANY] * (SWEEPS + 9),
        out_specs=[VMEM] * 3,
        scratch_shapes=[pltpu.VMEM((WIDE, 2, ROWS, LANES), F32)] * SWEEPS
        + [
            pltpu.VMEM((WIDE, 2, ROWS, LANES), F32),
            pltpu.VMEM((2, 2, CY, LANES), F32),
            pltpu.VMEM((2, UNIT, LANES), F32),
            pltpu.SemaphoreType.DMA((2, 11)),
            pltpu.SemaphoreType.DMA((2 + SWEEPS,)),
        ],
        compiler_params=pltpu.CompilerParams(vmem_limit_bytes=30 * MIB),
        name="sweeps",
    )(adv, *inner, factor, weight, *halos)


CHUNKS = ((0, 10), (10, 18), (18, 26), (26, 32))


def extend_kernel(
    parts, cur, weight, stress, xlo, xhi, ylo, yhi, clo, chi,
    level_out, stress_out,
    pad, ring0, ring1, ring2, ring3, mix0, mix1, stage, sems, x_sems, out_sems,
):
    ring, mix = (ring0, ring1, ring2, ring3), (mix0, mix1)

    def chunk(n):
        start, stop = CHUNKS[n]
        own = stress.at[:, pl.ds(start, stop - start)]
        copies = [
            pltpu.make_async_copy(
                own.at[:, :, :, half(h)],
                pad.at[:, pl.ds(start + 2, stop - start), h, pl.ds(OWN, CY), :],
                sems.at[n, h],
            )
            for h in range(2)
        ]
        for side, src in ((0, xlo), (3, xhi)):
            if n == side:
                at = 0 if n == 0 else CX + 2
                for h in range(2):
                    for c in range(COMPS):
                        copies.append(
                            pltpu.make_async_copy(
                                src.at[pl.ds(3 + 2 * c, 2), :, half(h)],
                                pad.at[c, pl.ds(at, 2), h, pl.ds(OWN, CY), :],
                                x_sems.at[side % 2, h, c],
                            )
                        )
        return copies

    chunks = [chunk(n) for n in range(len(CHUNKS))]
    for copies in chunks:
        for copy in copies:
            copy.start()
    sums = jnp.sum(parts[...], axis=0)
    shift = sums[:, 0:1] / sums[:, 64:65]
    flat = pad.reshape(COMPS, (CX + 4) * 2 * ROWS, LANES)
    for h in range(2):
        for c in range(COMPS):
            for face, row in ((ylo, OWN - 2), (yhi, OWN + CY)):
                for k in range(2):
                    for x in range(0, CX, 8):
                        at = ((x + 2) * 2 + h) * ROWS + row + k
                        flat[c, pl.ds(at, 8, stride=2 * ROWS), :] = face[
                            CX + 4 * (2 * c + k) + x // 8, :, half(h)
                        ]
            for corner, row in ((clo, OWN - 1), (chi, OWN + CY)):
                for x, n in ((1, c), (CX + 2, COMPS + c)):
                    at = 2 * DEEP + n // 8
                    pad[c, x, h, row : row + 1, :] = corner[at, n % 8 : n % 8 + 1, half(h)]

    def blend(mixes, center, around):
        value = mixes[6] * center
        for n in range(6):
            value = value + mixes[n] * around[n]
        return value

    def neighbours(load, groups):
        start = OWN + CY // 2 - 4 * groups
        for k in range(groups):
            rows, below, above = (pl.ds(start + k + d, 8, stride=groups) for d in (0, -1, 1))
            center = [load(0, h, rows) for h in range(2)]
            up, down = lane_shift(center, 1), lane_shift(center, -1)
            yield rows, center, [
                [
                    load(-1, h, rows), load(1, h, rows), load(0, h, below), load(0, h, above),
                    down[h], up[h],
                ]
                for h in range(2)
            ]

    def first_step(i, slot, groups=5):
        levels = neighbours(lambda dx, h, r: cur[i + 1 + dx, h, r, :] * DOUBLED, groups)
        comps = [
            neighbours(lambda dx, h, r, c=c: pad[c, i + 1 + dx, h, r, :], groups)
            for c in range(COMPS)
        ]
        for rows, center, around in levels:
            mixes = []
            for h in range(2):
                c = center[h]
                w = [recip(1.0 + jnp.exp2(jnp.minimum(n - c, 125.5))) for n in around[h]]
                total = w[0] + w[1] + w[2] + w[3] + w[4] + w[5]
                gate = weight[i, h, rows, :] * 0.5 * (
                    1.0 + jnp.tanh(c * (2.0 / DOUBLED) - 2.0 * shift)
                )
                scaled = gate * recip(total)
                w = [scaled * n for n in w] + [1.0 - gate]
                mixes.append(w)
                for n in range(7):
                    mix[slot % 2][n, h, rows, :] = w[n]
            for comp in range(COMPS):
                _, center, around = next(comps[comp])
                for h in range(2):
                    ring[slot][comp, h, rows, :] = blend(mixes[h], center[h], around[h])

    def second_step(x, slot):
        slots = {dx: (slot + dx) % 4 for dx in (-1, 0, 1)}
        groups = CY // 8
        comps = [
            neighbours(lambda dx, h, r, c=c: ring[slots[dx]][c, h, r, :], groups)
            for c in range(COMPS)
        ]
        for k in range(groups):
            rows = pl.ds(OWN + k, 8, stride=groups)
            mixes = [[mix[slot % 2][n, h, rows, :] for n in range(7)] for h in range(2)]
            for comp in range(COMPS):
                _, center, around = next(comps[comp])
                for h in range(2):
                    stage[comp, x, h, pl.ds(k, 8, stride=groups), :] = blend(
                        mixes[h], center[h], around[h]
                    )
        for h in range(2):
            level_out[x, :, half(h)] = cur[x + 2, h, OWN : OWN + CY, :] - shift

    outs = []
    for n in range(len(CHUNKS)):
        for copy in chunks[n]:
            copy.wait()
        if n == 0:
            first_step(0, 0, groups=4)
            first_step(1, 1)

        def body(group, carry):
            for k in range(4):
                i = group * 4 + k + 2
                first_step(i, (k + 2) % 4)
                second_step(i - 2, (k + 1) % 4)
            return carry

        lax.fori_loop(2 * n, 2 * n + 2, body, 0)
        planes = pl.ds(8 * n, 8)
        for h in range(2):
            copy = pltpu.make_async_copy(
                stage.at[:, planes, h], stress_out.at[:, planes, :, half(h)], out_sems.at[n, h]
            )
            copy.start()
            outs.append(copy)
    for copy in outs:
        copy.wait()


def extend(parts, cur, weight, stress, halos):
    shape = lambda *s: jax.ShapeDtypeStruct(s, F32)
    z = 2 * LANES
    return pl.pallas_call(
        extend_kernel,
        out_shape=[shape(CX, CY, z), shape(COMPS, CX, CY, z)],
        in_specs=[VMEM, VMEM, VMEM, ANY, ANY, ANY, VMEM, VMEM, VMEM, VMEM],
        out_specs=[VMEM, ANY],
        scratch_shapes=[
            pltpu.VMEM((COMPS, CX + 4, 2, ROWS, LANES), F32),
            *[pltpu.VMEM((COMPS, 2, ROWS, LANES), F32)] * 4,
            *[pltpu.VMEM((7, 2, ROWS, LANES), F32)] * 2,
            pltpu.VMEM((COMPS, CX, 2, CY, LANES), F32),
            pltpu.SemaphoreType.DMA((4, 2)),
            pltpu.SemaphoreType.DMA((2, 2, COMPS)),
            pltpu.SemaphoreType.DMA((4, 2)),
        ],
        compiler_params=pltpu.CompilerParams(vmem_limit_bytes=46 * MIB),
        name="extend",
    )(parts, cur, weight, stress, *halos)


def on_device(level, velocity, stress, tiles):
    nx, ny = lax.axis_size("gx"), lax.axis_size("gy")

    def send(value, dx, dy):
        if dy == 0:
            return lax.ppermute(value, "gx", [(i, (i + dx) % nx) for i in range(nx)])
        if dx == 0:
            return lax.ppermute(value, "gy", [(i, (i + dy) % ny) for i in range(ny)])
        pairs = [
            (i * ny + j, (i + dx) % nx * ny + (j + dy) % ny) for i in range(nx) for j in range(ny)
        ]
        return lax.ppermute(value, ("gx", "gy"), pairs)

    to_xp, to_xn, to_yp, to_yn, to_syp, to_syn = cut(level, stress)
    xlo, xhi = send(to_xn, 1, 0), send(to_xp, -1, 0)
    ylo, yhi = send(to_yn, 0, 1), send(to_yp, 0, -1)
    drift = inner_drift(level, velocity)
    adv, to_xp, to_xn, to_yp, to_yn, tail_p, tail_n = advect(
        tiles, level, xlo, xhi, ylo, yhi, velocity, drift,
        to_syp.reshape(8 * COMPS, 8, -1), to_syn.reshape(8 * COMPS, 8, -1),
    )
    axlo, axhi = send(to_xn, 1, 0), send(to_xp, -1, 0)
    aylo, ayhi = send(to_yn, 0, 1), send(to_yp, 0, -1)
    row = lax.broadcasted_iota(jnp.int32, (1, 8, 1), 1)

    def corners(rows, mark, tail):
        faces = [jnp.where(row == mark, f[DEEP:, rows], f[:DEEP, rows]) for f in (axlo, axhi)]
        return jnp.concatenate(faces + [tail], axis=0)

    *inner, factor, weight = inner_first(tiles, adv)
    last, axlo, axhi = lax.optimization_barrier((inner[-1], axlo, axhi))
    more = inner_second(last, factor)
    clo = send(corners(slice(-8, None), 0, tail_n), 0, 1)
    chi = send(corners(slice(0, 8), 7, tail_p), 0, -1)
    aylo, ayhi, clo, chi, more = lax.optimization_barrier((aylo, ayhi, clo, chi, more))
    cur, weight, part = sweeps(
        adv, (*inner, *more), factor, weight, (axlo, axhi, aylo, ayhi, clo, chi), nx * ny
    )
    parts = lax.all_to_all(part, ("gx", "gy"), 0, 0, tiled=True)
    return extend(parts, cur, weight, stress, (xlo, xhi, aylo, ayhi, clo, chi))


def solution(mesh):
    in_specs = (
        P("gx", "gy", None),
        P(None, "gx", "gy", None),
        P(None, "gx", "gy", None),
        P("gx", "gy", None),
    )
    out_specs = (P("gx", "gy", None), P(None, "gx", "gy", None))
    return jax.shard_map(
        on_device, mesh=mesh, in_specs=in_specs, out_specs=out_specs, check_vma=False
    )
```

```python
import functools

import jax
import jax.numpy as jnp
from jax import lax
from jax.experimental import pallas as pl
from jax.experimental.pallas import tpu as pltpu
from jax.sharding import PartitionSpec as P

TILE = 16
SWEEPS = 5
EPSILON = 1e-06
TIME_STEP = 0.4
PSEUDO_STEP = 0.3

CX = 32
CY = 32
LANES = 128
DEEP = 7
ROWS = 64
OWN = 16
UNIT = 16
COMPS = 6
F32 = jnp.float32
DOUBLED = 2.0 * 1.4426950408889634
MIB = 1024 * 1024
ANY = pl.BlockSpec(memory_space=pl.ANY)
VMEM = pl.BlockSpec(memory_space=pltpu.VMEM)
SMEM = pl.BlockSpec(memory_space=pltpu.SMEM)


def half(h):
    return pl.ds(h * LANES, LANES)


def recip(x):
    return pl.reciprocal(x, approx=True)


def lane_shift(pair, k):
    lane = lax.broadcasted_iota(jnp.int32, pair[0].shape, pair[0].ndim - 1)
    turned = [pltpu.roll(p, (-k) % LANES, p.ndim - 1) for p in pair]
    edge = lane >= LANES - k if k > 0 else lane < -k
    return [jnp.where(edge, turned[1 - h], turned[h]) for h in range(2)]


def weno(d, positive):
    v = [jnp.where(positive, d[k], d[5 - k]) for k in range(5)]
    d1, d2, d3, d4 = (v[k + 1] - v[k] for k in range(4))
    u1, u2, u3 = d2 - d1, d3 - d2, d4 - d3
    g1 = d2 + d2 + u1
    g2 = d2 + d3
    g3 = u3 - (d3 + d3)
    scale = 13.0 / 3.0
    a1 = recip(4.0 * EPSILON + (scale * u1 * u1 + g1 * g1))
    a2 = recip(4.0 * EPSILON + (scale * u2 * u2 + g2 * g2))
    a3 = recip(4.0 * EPSILON + (scale * u3 * u3 + g3 * g3))
    a1 = a1 * a1
    a2 = 6.0 * (a2 * a2)
    a3 = 3.0 * (a3 * a3)
    top = a1 * (u1 - u2) + 0.5 * (a3 * (u2 - u3))
    mid = v[2] + (d3 + d3 + d2) * (1.0 / 6.0)
    return mid + top * (recip(a1 + a2 + a3) * (1.0 / 3.0))


def band_table(tiles_ref):
    shape = (8, LANES)
    row = lax.broadcasted_iota(jnp.int32, shape, 0)
    lane = lax.broadcasted_iota(jnp.int32, shape, 1)
    numbers = (row // 2) * 16 + (row % 2) * 8 + lane // TILE
    flags = jnp.zeros(shape, F32)
    for slot in range(tiles_ref.shape[-1]):
        flags = jnp.where(numbers == tiles_ref[0, 0, slot], 1.0, flags)
    return flags


def derivative(line, speed):
    return speed * weno([line[k + 1] - line[k] for k in range(6)], speed > 0)


def along_x(pad, x, h, at, size):
    return [pad[x + k, h, pl.ds(at, size), :] for k in range(-3, 4)]


def along_y(pad, x, h, at, size):
    return [pad[x, h, pl.ds(at + k, size), :] for k in range(-3, 4)]


def cut_kernel(
    level, stress, to_xp, to_xn, to_yp, to_yn, to_syp, to_syn, faces, x_sems, y_sems
):
    copies = []
    for n, (out, at) in enumerate(((to_xp, 0), (to_xn, CX))):
        deep = lambda size: pl.ds(at and at - size, size)
        copies.append(pltpu.make_async_copy(level.at[deep(3)], out.at[pl.ds(0, 3)], x_sems.at[n, 0]))
        for c in range(COMPS):
            copies.append(
                pltpu.make_async_copy(
                    stress.at[c, deep(2)], out.at[pl.ds(3 + 2 * c, 2)], x_sems.at[n, 1 + c]
                )
            )
    for copy in copies:
        copy.start()
    sides = []
    for n, y in enumerate((0, CY - 8)):
        side = []
        for h in range(2):
            for m in range(1 + COMPS):
                src = stress.at[m - 1] if m else level
                side.append(
                    pltpu.make_async_copy(
                        src.at[:, pl.ds(y, 8), half(h)], faces.at[m, n, h], y_sems.at[m, n, h]
                    )
                )
        for copy in side:
            copy.start()
        sides.append(side)
    flat = faces.reshape(1 + COMPS, 2, 2, CX * 8, LANES)
    for n, outs in enumerate(((to_yp, to_syp), (to_yn, to_syn))):
        for copy in sides[n]:
            copy.wait()
        for h in range(2):
            for m in range(1 + COMPS):
                depth = 2 if m else 3
                out = outs[m // 4]
                first = (0, 3, 5, 7, 0, 2, 4)[m]
                for k in range(depth):
                    row = k if n == 0 else 8 - depth + k
                    for x in range(0, CX, 8):
                        out[first + k, x : x + 8, half(h)] = flat[
                            m, n, h, pl.ds(8 * x + row, 8, stride=8), :
                        ]
    for copy in copies:
        copy.wait()


def cut(level, stress):
    message = lambda planes: jax.ShapeDtypeStruct((planes, CX, 2 * LANES), F32)
    return pl.pallas_call(
        cut_kernel,
        out_shape=[message(3 + 2 * COMPS)] * 2 + [message(3 + COMPS)] * 2 + [message(COMPS)] * 2,
        in_specs=[ANY] * 2,
        out_specs=[VMEM] * 6,
        scratch_shapes=[
            pltpu.VMEM((1 + COMPS, 2, 2, CX, 8, LANES), F32),
            pltpu.SemaphoreType.DMA((2, 1 + COMPS)),
            pltpu.SemaphoreType.DMA((1 + COMPS, 2, 2)),
        ],
        compiler_params=pltpu.CompilerParams(vmem_limit_bytes=57 * MIB),
        name="cut",
    )(level, stress)


def inner_kernel(level, speed, drift, pad, sems):
    copies = [
        pltpu.make_async_copy(level.at[:, :, half(h)], pad.at[:, h], sems.at[h]) for h in range(2)
    ]
    for copy in copies:
        copy.start()
    for copy in copies:
        copy.wait()

    def plane(x, with_x):
        for unit in range(CY // UNIT):
            rows = pl.ds(unit * UNIT, UNIT)
            v = [[speed[d, x, rows, half(h)].astype(F32) for h in range(2)] for d in range(3)]
            for part in range(UNIT // 8):
                at = unit * UNIT + 8 * part
                cut = slice(8 * part, 8 * part + 8)
                center = [pad[x, h, pl.ds(at, 8), :] for h in range(2)]
                ups = [lane_shift(center, k) for k in (1, 2, 3)]
                downs = [lane_shift(center, -k) for k in (3, 2, 1)]
                for h in range(2):
                    line = [s[h] for s in downs] + [center[h]] + [s[h] for s in ups]
                    total = derivative(line, v[2][h][cut])
                    if with_x:
                        total = total + derivative(along_x(pad, x, h, at, 8), v[0][h][cut])
                    if 8 <= at < CY - 8:
                        total = total + derivative(along_y(pad, x, h, at, 8), v[1][h][cut])
                    drift[x, pl.ds(at, 8), half(h)] = total

    def inner(x, carry):
        plane(x, True)
        return carry

    def outer(x, carry):
        plane(x, False)
        plane(x + CX - 3, False)
        return carry

    lax.fori_loop(0, 3, outer, 0)
    lax.fori_loop(3, CX - 3, inner, 0, unroll=2)


def inner_drift(level, speed):
    return pl.pallas_call(
        inner_kernel,
        out_shape=jax.ShapeDtypeStruct(level.shape, F32),
        in_specs=[ANY, VMEM],
        out_specs=VMEM,
        scratch_shapes=[
            pltpu.VMEM((CX, 2, CY, LANES), F32),
            pltpu.SemaphoreType.DMA((2,)),
        ],
        compiler_params=pltpu.CompilerParams(vmem_limit_bytes=10 * MIB),
        cost_estimate=pl.CostEstimate(
            flops=180 * level.size, bytes_accessed=14 * level.size, transcendentals=9 * level.size
        ),
        name="inner_drift",
    )(level, speed)


def advect_kernel(
    tiles, level, xlo, xhi, ylo, yhi, speed, drift, stress_p, stress_n,
    adv, to_xp, to_xn, to_yp, to_yn, tail_p, tail_n,
    pad, table, faces, ends, sems, y_sems, end_sems, ride_sems,
):
    riders = [
        pltpu.make_async_copy(src, out.at[pl.ds(CX, 4 * COMPS)], ride_sems.at[n])
        for n, (src, out) in enumerate(((stress_p, to_yp), (stress_n, to_yn)))
    ]
    copies = []
    for h in range(2):
        for n, (src, at, size) in enumerate(((level, 3, CX), (xlo, 0, 3), (xhi, CX + 3, 3))):
            copies.append(
                pltpu.make_async_copy(
                    src.at[pl.ds(0, size), :, half(h)],
                    pad.at[pl.ds(at, size), h, pl.ds(8, CY), :],
                    sems.at[h, n],
                )
            )
    for n, src in enumerate((ylo, yhi)):
        copies.append(pltpu.make_async_copy(src.at[pl.ds(0, 3)], faces.at[n], y_sems.at[n]))
    for n, src in enumerate((xlo, xhi)):
        for m, y in enumerate((0, CY - 8)):
            copies.append(
                pltpu.make_async_copy(
                    src.at[pl.ds(3, 2 * COMPS), pl.ds(y, 8)], ends.at[n, m], end_sems.at[n, m]
                )
            )
    for copy in copies + riders:
        copy.start()
    table[...] = band_table(tiles)
    for copy in copies:
        copy.wait()
    for m, (tail, row) in enumerate(((tail_p, 0), (tail_n, 7))):
        tail[...] = jnp.zeros(tail.shape, F32)
        for n in range(2):
            for c in range(COMPS):
                to = n * COMPS + c
                tail[to // 8, to % 8 : to % 8 + 1, :] = ends[n, m, 2 * c + 1 - n, row : row + 1, :]
    flat = pad.reshape((CX + 6) * 2 * 48, LANES)
    for n, row in enumerate((5, 8 + CY)):
        for h in range(2):
            for k in range(3):
                for x in range(0, CX, 8):
                    rows = pl.ds(((x + 3) * 2 + h) * 48 + row + k, 8, stride=96)
                    flat[rows, :] = faces[n, k, x : x + 8, half(h)]

    def plane(x, with_x):
        for unit in range(CY // UNIT):
            rows = pl.ds(unit * UNIT, UNIT)
            for h in range(2):
                vx = speed[0, x, rows, half(h)].astype(F32) if with_x else None
                vy = speed[1, x, rows, half(h)].astype(F32)
                for part in range(UNIT // 8):
                    at = unit * UNIT + 8 * part
                    cut = slice(8 * part, 8 * part + 8)
                    total = drift[x, pl.ds(at, 8), half(h)]
                    if with_x:
                        total = total + derivative(along_x(pad, x + 3, h, at + 8, 8), vx[cut])
                    if at in (0, CY - 8):
                        total = total + derivative(along_y(pad, x + 3, h, at + 8, 8), vy[cut])
                    adv[x, pl.ds(at, 8), half(h)] = (
                        pad[x + 3, h, pl.ds(at + 8, 8), :] - TIME_STEP * total
                    )

    def inner(x, carry):
        plane(x, False)
        return carry

    def outer(x, carry):
        plane(x, True)
        plane(x + CX - 3, True)
        return carry

    lax.fori_loop(0, 3, outer, 0)
    lax.fori_loop(3, CX - 3, inner, 0, unroll=2)
    low, high = CX - DEEP, CX
    to_xp[0:DEEP] = adv[0:DEEP]
    to_xn[0:DEEP] = adv[low:high]
    row8 = lax.broadcasted_iota(jnp.int32, (8, LANES), 0)
    for h in range(2):
        for j in range(2):
            rows = pl.ds(j * TILE, TILE)
            for i, face in ((0, to_xp), (1, to_xn)):
                r = i * 4 + j * 2 + h
                face[DEEP, rows, half(h)] = jnp.broadcast_to(table[r : r + 1, :], (TILE, LANES))
        for i in range(2):
            first = table[i * 4 + h : i * 4 + h + 1, :]
            last = table[i * 4 + 2 + h : i * 4 + 3 + h, :]
            for x in range(i * TILE, i * TILE + TILE):
                to_yp[x, :, half(h)] = jnp.where(row8 == 7, first, adv[x, 0:8, half(h)])
                to_yn[x, :, half(h)] = jnp.where(row8 == 0, last, adv[x, CY - 8 : CY, half(h)])
    for copy in riders:
        copy.wait()


def advect(tiles, level, xlo, xhi, ylo, yhi, speed, drift, stress_p, stress_n):
    shape = lambda *s: jax.ShapeDtypeStruct(s, F32)
    z = 2 * LANES
    return pl.pallas_call(
        advect_kernel,
        out_shape=[shape(CX, CY, z)]
        + [shape(8, CY, z)] * 2
        + [shape(CX + 4 * COMPS, 8, z)] * 2
        + [shape(2, 8, z)] * 2,
        in_specs=[SMEM, ANY, ANY, ANY, ANY, ANY, VMEM, VMEM, ANY, ANY],
        out_specs=[VMEM] * 7,
        scratch_shapes=[
            pltpu.VMEM((CX + 6, 2, 48, LANES), F32),
            pltpu.VMEM((8, LANES), F32),
            pltpu.VMEM((2, 3, CX, z), F32),
            pltpu.VMEM((2, 2, 2 * COMPS, 8, z), F32),
            pltpu.SemaphoreType.DMA((2, 3)),
            pltpu.SemaphoreType.DMA((2,)),
            pltpu.SemaphoreType.DMA((2, 2)),
            pltpu.SemaphoreType.DMA((2,)),
        ],
        compiler_params=pltpu.CompilerParams(vmem_limit_bytes=12 * MIB),
        name="advect",
    )(tiles, level, xlo, xhi, ylo, yhi, speed, drift, stress_p, stress_n)


WIDE = CX + 2 * DEEP
INNER = 48
SPLIT = 2


def sweep_rows(src, factor, x, fx, start, stride, groups, store):
    span = pl.ds if stride == 1 else functools.partial(pl.ds, stride=stride)
    rows = [span(start + k, 8) for k in range(-1, groups + 1)]
    lines = [[src[x, h, r, :] for r in rows] for h in range(2)]
    for k in range(1, groups + 1):
        center = [lines[h][k] for h in range(2)]
        up, down = lane_shift(center, 1), lane_shift(center, -1)
        for h in range(2):
            c = center[h]
            step = factor[fx, h, rows[k], :]
            positive = step > 0
            pairs = (
                (src[x - 1, h, rows[k], :], src[x + 1, h, rows[k], :]),
                (lines[h][k - 1], lines[h][k + 1]),
                (down[h], up[h]),
            )
            total = None
            for l, r in pairs:
                low = jnp.minimum(jnp.minimum(l, r), c)
                high = jnp.maximum(jnp.maximum(l, r), c)
                diff = c - jnp.where(positive, low, high)
                total = diff * diff if total is None else total + diff * diff
            slope = total * lax.rsqrt(jnp.maximum(total, 1e-36))
            store(h, rows[k], c - step * (slope - 1.0))


def band_step(value, band):
    square = value * value
    weight = band * recip(1.0 + square * (1.0 / 36.0))
    return PSEUDO_STEP * (value * lax.rsqrt(square + 1.0)) * weight, weight


def inner_sweeps(source, factor, targets, first):
    for n, target in enumerate(targets):
        sweep = first + n

        def body(x, carry, source=source, target=target):
            def store(h, rows, value):
                target[x, h, rows, :] = value

            sweep_rows(source, factor, x, x, 8, CY // 8, CY // 8, store)
            return carry

        lax.fori_loop(sweep, CX - sweep, body, 0, unroll=2)
        source = target


def inner_first_kernel(tiles, adv, done1, done2, factor, weight, own, table, sems):
    copies = [
        pltpu.make_async_copy(adv.at[:, :, half(h)], own.at[:, h, pl.ds(8, CY), :], sems.at[h])
        for h in range(2)
    ]
    for copy in copies:
        copy.start()
    table[...] = band_table(tiles)
    for copy in copies:
        copy.wait()
    for i in range(2):

        def body(x, carry, i=i):
            for h in range(2):
                for group in range(CY // 8):
                    rows = pl.ds(8 + 8 * group, 8)
                    r = i * 4 + (group // 2) * 2 + h
                    band = jnp.broadcast_to(table[r : r + 1, :], (8, LANES))
                    step, value = band_step(own[x, h, rows, :], band)
                    factor[x, h, rows, :] = step
                    weight[x, h, rows, :] = value
            return carry

        lax.fori_loop(i * TILE, (i + 1) * TILE, body, 0, unroll=2)
    inner_sweeps(own, factor, (done1, done2), 1)


def inner_second_kernel(before, factor, *done):
    inner_sweeps(before, factor, done, SPLIT + 1)


def inner_first(tiles, adv):
    return pl.pallas_call(
        inner_first_kernel,
        out_shape=[jax.ShapeDtypeStruct((CX, 2, INNER, LANES), F32)] * (SPLIT + 2),
        in_specs=[SMEM, ANY],
        out_specs=[VMEM] * (SPLIT + 2),
        scratch_shapes=[
            pltpu.VMEM((CX, 2, INNER, LANES), F32),
            pltpu.VMEM((8, LANES), F32),
            pltpu.SemaphoreType.DMA((2,)),
        ],
        compiler_params=pltpu.CompilerParams(vmem_limit_bytes=12 * MIB),
        cost_estimate=pl.CostEstimate(
            flops=100 * adv.size, bytes_accessed=24 * adv.size, transcendentals=4 * adv.size
        ),
        name="inner_first",
    )(tiles, adv)


def inner_second(before, factor):
    return pl.pallas_call(
        inner_second_kernel,
        out_shape=[jax.ShapeDtypeStruct((CX, 2, INNER, LANES), F32)] * (SWEEPS - SPLIT),
        in_specs=[VMEM] * 2,
        out_specs=[VMEM] * (SWEEPS - SPLIT),
        compiler_params=pltpu.CompilerParams(vmem_limit_bytes=12 * MIB),
        cost_estimate=pl.CostEstimate(
            flops=60 * factor.size, bytes_accessed=24 * factor.size, transcendentals=2 * factor.size
        ),
        name="inner_second",
    )(before, factor)


def sweep_kernel(
    adv, in1, in2, in3, in4, in5, own_factor, own_weight, xlo, xhi, ylo, yhi, clo, chi,
    cur_out, weight_out, part,
    buf0, buf1, buf2, buf3, buf4, factor, masks, sums, sems, x_sems,
):
    bufs = (buf0, buf1, buf2, buf3, buf4)
    copies = []
    done = []
    for h in range(2):
        pieces = (
            (adv, DEEP, CX, OWN, CY),
            (xlo.at[pl.ds(0, DEEP)], 0, DEEP, OWN, CY),
            (xhi.at[pl.ds(0, DEEP)], DEEP + CX, DEEP, OWN, CY),
            (ylo.at[pl.ds(0, CX)], DEEP, CX, OWN - 8, 8),
            (yhi.at[pl.ds(0, CX)], DEEP, CX, OWN + CY, 8),
            (clo.at[pl.ds(0, DEEP)], 0, DEEP, OWN - 8, 8),
            (clo.at[pl.ds(DEEP, DEEP)], DEEP + CX, DEEP, OWN - 8, 8),
            (chi.at[pl.ds(0, DEEP)], 0, DEEP, OWN + CY, 8),
            (chi.at[pl.ds(DEEP, DEEP)], DEEP + CX, DEEP, OWN + CY, 8),
        )
        for n, (src, x, nx, y, ny) in enumerate(pieces):
            copies.append(
                pltpu.make_async_copy(
                    src.at[:, :, half(h)],
                    buf0.at[pl.ds(x, nx), h, pl.ds(y, ny), :],
                    sems.at[h, n],
                )
            )
        for n, src in enumerate((xlo, xhi)):
            copies.append(
                pltpu.make_async_copy(
                    src.at[pl.ds(DEEP, 1), :, half(h)], masks.at[pl.ds(n, 1), h], sems.at[h, 9 + n]
                )
            )
    own = lambda ref, x: ref.at[pl.ds(x, CX), :, pl.ds(OWN, CY), :]
    for n, (src, dst) in enumerate(
        [(own_factor, own(factor, DEEP)), (own_weight, own(weight_out, 1))]
        + [(src, own(buf, DEEP)) for src, buf in zip((in1, in2, in3, in4), bufs[1:])]
        + [(in5, own(cur_out, 2))]
    ):
        done.append(pltpu.make_async_copy(src.at[:, :, pl.ds(8, CY), :], dst, x_sems.at[n]))
    for copy in copies + done[:1]:
        copy.start()
    sums[...] = jnp.zeros(sums.shape, F32)
    for copy in copies + done[:1]:
        copy.wait()
    for copy in done[2:] + done[1:2]:
        copy.start()

    def prepare(x, groups, bands, keep):
        for h in range(2):
            for group in groups:
                rows = pl.ds(OWN + 8 * group, 8)
                value = buf0[x, h, rows, :]
                if group == -1:
                    band = jnp.broadcast_to(value[0:1], value.shape)
                elif group == 4:
                    band = jnp.broadcast_to(value[7:8], value.shape)
                else:
                    band = masks[bands, h, pl.ds(8 * group, 8), :]
                step, weight = band_step(value, band)
                factor[x, h, rows, :] = step
                if keep:
                    weight_out[x - DEEP + 1, h, rows, :] = weight

    def run(start, stop, groups, bands, keep):
        def body(x, carry):
            prepare(x, groups, bands, keep)
            return carry

        lax.fori_loop(start, stop, body, 0, unroll=2)

    everything = tuple(range(-1, 5))
    run(1, DEEP - 1, everything, 0, False)
    prepare(DEEP - 1, everything, 0, True)
    run(DEEP, DEEP + CX, (-1, 4), 0, True)
    prepare(DEEP + CX, everything, 1, True)
    run(DEEP + CX + 1, WIDE - 1, everything, 1, False)

    for sweep in range(1, SWEEPS + 1):
        done[sweep + 1].wait()
        offset, target = (0, bufs[sweep]) if sweep < SWEEPS else (SWEEPS, cur_out)
        groups = 6 if DEEP - sweep > 4 else 5
        source = bufs[sweep - 1]

        def whole(x, source=source, target=target, offset=offset, groups=groups):
            def store(h, rows, value):
                target[x - offset, h, rows, :] = value

            start = OWN + CY // 2 - 4 * groups
            sweep_rows(source, factor, x, x, start, groups, groups, store)

        def ends(x, source=source, target=target, offset=offset, sweep=sweep):
            def store(h, rows, value):
                target[x - offset, h, rows, :] = value

            for start in (OWN + sweep - 8, OWN + CY - sweep):
                sweep_rows(source, factor, x, x, start, 1, 1, store)

        def outer(n, carry, whole=whole, sweep=sweep):
            whole(sweep + n)
            whole(WIDE - 1 - sweep - n)
            return carry

        def middle(x, carry, ends=ends):
            ends(x)
            return carry

        lax.fori_loop(0, DEEP, outer, 0)
        count_x = CX - 2 * sweep
        at_once = max(k for k in range(2, 14) if count_x % k == 0)
        lax.fori_loop(DEEP + sweep, DEEP + CX - sweep, middle, 0, unroll=at_once)

    def count(x, carry):
        for h in range(2):
            for unit in range(CY // UNIT):
                rows = pl.ds(OWN + unit * UNIT, UNIT)
                after = jnp.tanh(cur_out[x + 2, h, rows, :])
                before = jnp.tanh(buf0[x + DEEP, h, rows, :])
                sums[0] += after - before
                sums[1] += 1.0 - after * after
        return carry

    lax.fori_loop(0, CX, count, 0, unroll=2)
    done[1].wait()
    lane = lax.broadcasted_iota(jnp.int32, (1, LANES), 1)
    sums_row = jnp.where(lane < 64, jnp.sum(sums[0]), jnp.sum(sums[1]))
    part[...] = jnp.broadcast_to(sums_row, part.shape)


def sweeps(adv, inner, factor, weight, halos, count):
    shape = lambda *s: jax.ShapeDtypeStruct(s, F32)
    return pl.pallas_call(
        sweep_kernel,
        out_shape=[
            shape(CX + 4, 2, ROWS, LANES), shape(CX + 2, 2, ROWS, LANES), shape(count, 1, LANES)
        ],
        in_specs=[ANY] * (SWEEPS + 9),
        out_specs=[VMEM] * 3,
        scratch_shapes=[pltpu.VMEM((WIDE, 2, ROWS, LANES), F32)] * SWEEPS
        + [
            pltpu.VMEM((WIDE, 2, ROWS, LANES), F32),
            pltpu.VMEM((2, 2, CY, LANES), F32),
            pltpu.VMEM((2, UNIT, LANES), F32),
            pltpu.SemaphoreType.DMA((2, 11)),
            pltpu.SemaphoreType.DMA((2 + SWEEPS,)),
        ],
        compiler_params=pltpu.CompilerParams(vmem_limit_bytes=30 * MIB),
        name="sweeps",
    )(adv, *inner, factor, weight, *halos)


CHUNKS = ((0, 10), (10, 18), (18, 26), (26, 32))


def extend_kernel(
    parts, cur, weight, stress, xlo, xhi, ylo, yhi, sylo, syhi, clo, chi,
    level_out, stress_out,
    pad, ring0, ring1, ring2, ring3, mix0, mix1, stage, sems, x_sems, out_sems,
):
    ring, mix = (ring0, ring1, ring2, ring3), (mix0, mix1)

    def chunk(n):
        start, stop = CHUNKS[n]
        own = stress.at[:, pl.ds(start, stop - start)]
        copies = [
            pltpu.make_async_copy(
                own.at[:, :, :, half(h)],
                pad.at[:, pl.ds(start + 2, stop - start), h, pl.ds(OWN, CY), :],
                sems.at[n, h],
            )
            for h in range(2)
        ]
        for side, src in ((0, xlo), (3, xhi)):
            if n == side:
                at = 0 if n == 0 else CX + 2
                for h in range(2):
                    for c in range(COMPS):
                        copies.append(
                            pltpu.make_async_copy(
                                src.at[pl.ds(3 + 2 * c, 2), :, half(h)],
                                pad.at[c, pl.ds(at, 2), h, pl.ds(OWN, CY), :],
                                x_sems.at[side % 2, h, c],
                            )
                        )
        return copies

    chunks = [chunk(n) for n in range(len(CHUNKS))]
    for copies in chunks:
        for copy in copies:
            copy.start()
    sums = jnp.sum(parts[...], axis=0)
    shift = sums[:, 0:1] / sums[:, 64:65]
    flat = pad.reshape(COMPS, (CX + 4) * 2 * ROWS, LANES)
    for h in range(2):
        for c in range(COMPS):
            for face, rest, row in ((ylo, sylo, OWN - 2), (yhi, syhi, OWN + CY)):
                for k in range(2):
                    for x in range(0, CX, 8):
                        at = ((x + 2) * 2 + h) * ROWS + row + k
                        if c < 3:
                            value = face[3 + 2 * c + k, x : x + 8, half(h)]
                        else:
                            value = rest[CX + 4 * (2 * c - 6 + k) + x // 8, :, half(h)]
                        flat[c, pl.ds(at, 8, stride=2 * ROWS), :] = value
            for corner, row in ((clo, OWN - 1), (chi, OWN + CY)):
                for x, n in ((1, c), (CX + 2, COMPS + c)):
                    at = 2 * DEEP + n // 8
                    pad[c, x, h, row : row + 1, :] = corner[at, n % 8 : n % 8 + 1, half(h)]

    def blend(mixes, center, around):
        value = mixes[6] * center
        for n in range(6):
            value = value + mixes[n] * around[n]
        return value

    def neighbours(load, groups):
        start = OWN + CY // 2 - 4 * groups
        for k in range(groups):
            rows, below, above = (pl.ds(start + k + d, 8, stride=groups) for d in (0, -1, 1))
            center = [load(0, h, rows) for h in range(2)]
            up, down = lane_shift(center, 1), lane_shift(center, -1)
            yield rows, center, [
                [
                    load(-1, h, rows), load(1, h, rows), load(0, h, below), load(0, h, above),
                    down[h], up[h],
                ]
                for h in range(2)
            ]

    def first_step(i, slot, groups=5):
        levels = neighbours(lambda dx, h, r: cur[i + 1 + dx, h, r, :] * DOUBLED, groups)
        comps = [
            neighbours(lambda dx, h, r, c=c: pad[c, i + 1 + dx, h, r, :], groups)
            for c in range(COMPS)
        ]
        for rows, center, around in levels:
            mixes = []
            for h in range(2):
                c = center[h]
                w = [recip(1.0 + jnp.exp2(jnp.minimum(n - c, 125.5))) for n in around[h]]
                total = w[0] + w[1] + w[2] + w[3] + w[4] + w[5]
                gate = weight[i, h, rows, :] * 0.5 * (
                    1.0 + jnp.tanh(c * (2.0 / DOUBLED) - 2.0 * shift)
                )
                scaled = gate * recip(total)
                w = [scaled * n for n in w] + [1.0 - gate]
                mixes.append(w)
                for n in range(7):
                    mix[slot % 2][n, h, rows, :] = w[n]
            for comp in range(COMPS):
                _, center, around = next(comps[comp])
                for h in range(2):
                    ring[slot][comp, h, rows, :] = blend(mixes[h], center[h], around[h])

    def second_step(x, slot):
        slots = {dx: (slot + dx) % 4 for dx in (-1, 0, 1)}
        groups = CY // 8
        comps = [
            neighbours(lambda dx, h, r, c=c: ring[slots[dx]][c, h, r, :], groups)
            for c in range(COMPS)
        ]
        for k in range(groups):
            rows = pl.ds(OWN + k, 8, stride=groups)
            mixes = [[mix[slot % 2][n, h, rows, :] for n in range(7)] for h in range(2)]
            for comp in range(COMPS):
                _, center, around = next(comps[comp])
                for h in range(2):
                    stage[comp, x, h, pl.ds(k, 8, stride=groups), :] = blend(
                        mixes[h], center[h], around[h]
                    )
        for h in range(2):
            level_out[x, :, half(h)] = cur[x + 2, h, OWN : OWN + CY, :] - shift

    outs = []
    for n in range(len(CHUNKS)):
        for copy in chunks[n]:
            copy.wait()
        if n == 0:
            first_step(0, 0, groups=4)
            first_step(1, 1)

        def body(group, carry):
            for k in range(4):
                i = group * 4 + k + 2
                first_step(i, (k + 2) % 4)
                second_step(i - 2, (k + 1) % 4)
            return carry

        lax.fori_loop(2 * n, 2 * n + 2, body, 0)
        planes = pl.ds(8 * n, 8)
        for h in range(2):
            copy = pltpu.make_async_copy(
                stage.at[:, planes, h], stress_out.at[:, planes, :, half(h)], out_sems.at[n, h]
            )
            copy.start()
            outs.append(copy)
    for copy in outs:
        copy.wait()


def extend(parts, cur, weight, stress, halos):
    shape = lambda *s: jax.ShapeDtypeStruct(s, F32)
    z = 2 * LANES
    return pl.pallas_call(
        extend_kernel,
        out_shape=[shape(CX, CY, z), shape(COMPS, CX, CY, z)],
        in_specs=[VMEM, VMEM, VMEM, ANY, ANY, ANY] + [VMEM] * 6,
        out_specs=[VMEM, ANY],
        scratch_shapes=[
            pltpu.VMEM((COMPS, CX + 4, 2, ROWS, LANES), F32),
            *[pltpu.VMEM((COMPS, 2, ROWS, LANES), F32)] * 4,
            *[pltpu.VMEM((7, 2, ROWS, LANES), F32)] * 2,
            pltpu.VMEM((COMPS, CX, 2, CY, LANES), F32),
            pltpu.SemaphoreType.DMA((4, 2)),
            pltpu.SemaphoreType.DMA((2, 2, COMPS)),
            pltpu.SemaphoreType.DMA((4, 2)),
        ],
        compiler_params=pltpu.CompilerParams(vmem_limit_bytes=46 * MIB),
        name="extend",
    )(parts, cur, weight, stress, *halos)


def on_device(level, velocity, stress, tiles):
    nx, ny = lax.axis_size("gx"), lax.axis_size("gy")

    def send(value, dx, dy):
        if dy == 0:
            return lax.ppermute(value, "gx", [(i, (i + dx) % nx) for i in range(nx)])
        if dx == 0:
            return lax.ppermute(value, "gy", [(i, (i + dy) % ny) for i in range(ny)])
        pairs = [
            (i * ny + j, (i + dx) % nx * ny + (j + dy) % ny) for i in range(nx) for j in range(ny)
        ]
        return lax.ppermute(value, ("gx", "gy"), pairs)

    to_xp, to_xn, to_yp, to_yn, to_syp, to_syn = cut(level, stress)
    xlo, xhi = send(to_xn, 1, 0), send(to_xp, -1, 0)
    ylo, yhi = send(to_yn, 0, 1), send(to_yp, 0, -1)
    drift = inner_drift(level, velocity)
    adv, to_xp, to_xn, to_yp, to_yn, tail_p, tail_n = advect(
        tiles, level, xlo, xhi, ylo, yhi, velocity, drift,
        to_syp.reshape(4 * COMPS, 8, -1), to_syn.reshape(4 * COMPS, 8, -1),
    )
    axlo, axhi = send(to_xn, 1, 0), send(to_xp, -1, 0)
    aylo, ayhi = send(to_yn, 0, 1), send(to_yp, 0, -1)
    row = lax.broadcasted_iota(jnp.int32, (1, 8, 1), 1)

    def corners(rows, mark, tail):
        faces = [jnp.where(row == mark, f[DEEP:, rows], f[:DEEP, rows]) for f in (axlo, axhi)]
        return jnp.concatenate(faces + [tail], axis=0)

    *inner, factor, weight = inner_first(tiles, adv)
    last, axlo, axhi = lax.optimization_barrier((inner[-1], axlo, axhi))
    more = inner_second(last, factor)
    clo = send(corners(slice(-8, None), 0, tail_n), 0, 1)
    chi = send(corners(slice(0, 8), 7, tail_p), 0, -1)
    aylo, ayhi, clo, chi, more = lax.optimization_barrier((aylo, ayhi, clo, chi, more))
    cur, weight, part = sweeps(
        adv, (*inner, *more), factor, weight, (axlo, axhi, aylo, ayhi, clo, chi), nx * ny
    )
    parts = lax.all_to_all(part, ("gx", "gy"), 0, 0, tiled=True)
    return extend(parts, cur, weight, stress, (xlo, xhi, ylo, yhi, aylo, ayhi, clo, chi))


def solution(mesh):
    in_specs = (
        P("gx", "gy", None),
        P(None, "gx", "gy", None),
        P(None, "gx", "gy", None),
        P("gx", "gy", None),
    )
    out_specs = (P("gx", "gy", None), P(None, "gx", "gy", None))
    return jax.shard_map(
        on_device, mesh=mesh, in_specs=in_specs, out_specs=out_specs, check_vma=False
    )
```
